32 devices in a mesh: grp: 2 (over x), ch: 16 (over z, y, core).
Axes of the slice: x: 2, y: 2, z: 4, core: 2. Of those that a mesh axis runs over, the one named last changes fastest.
Arguments:
- features: bfloat16 [2048, 2048], P('ch', 'grp'), parts along dimension 1, may hold values from -50 to 50
- dw_weight: float32 [2048, 49], P('ch'), may hold values from -0.875 to 0.875
- norm_gain: float32 [2048], replicated, may hold values from 0.25 to 1.75
- layer_scale: float32 [2048], replicated, may hold values from 0.2 to 1
- w_in: bfloat16 [8192, 2048], P('ch'), may hold values from -0.125 to 0.125
- w_out: bfloat16 [8192, 2048], P('ch'), may hold values from -0.0625 to 0.0625
- w_head: bfloat16 [2048, 150], replicated, may hold values from -3 to 3
- labels: int32 [2048], P('grp'), parts along dimension 0, may hold values from 0 to 149
Outputs:
- d_features: float32 [2048, 2048], P('ch', 'grp'), parts along dimension 1
- d_dw: float32 [2048, 98], P('ch', 'grp'), parts along dimension 1
- d_scale: float32 [4096], P(('grp', 'ch')), parts along dimension 0
- d_w_in: float32 [16384, 2048], P(('grp', 'ch')), parts along dimension 0
- d_w_out: float32 [16384, 2048], P(('grp', 'ch')), parts along dimension 0
- d_head: float32 [2048, 300], P('ch', 'grp'), parts along dimension 1
- mean_loss: float32 [2], P('grp'), parts along dimension 0
The draws below stay inside these ranges and needn't reach their ends.
There are 2 independent parts, one for each index of `grp`. The reference program is written for one: setup_inputs(seed, part) draws one part's arguments, and reference() takes and returns one part's arrays. A program takes and returns all parts, laid end to end along the dimension named above; an argument that names none is the same for every part. Nothing has to cross between parts.
All inputs are finite; a program needn't handle non-finite values.
Results may differ from the reference program's by a relative error of at most 0.012.
Values may be sent and summed in bfloat16 or wider, within the bound.
No kernel may reach another device: no remote copies, remote signals or barrier semaphores. Data moves between devices by JAX's collectives and lax.ppermute only.
A program may use at most 128 MiB of HBM per device.

```python
import math
import jax
import jax.numpy as jnp
from jax import lax

C = 2048
FF = 8192
K = 150
KS = 7
WIN_H = 32
WIN_W = 32
TOKENS = 1024


def draw_features(key, part):
    key_base, key_tok = jax.random.split(jax.random.fold_in(key, 11), 2)
    base = jnp.clip(jax.random.normal(key_base, (C, TOKENS), jnp.float32), -4.0, 4.0)
    ramp = 0.3 * jnp.power(10.0, jnp.arange(C, dtype=jnp.float32) / C)
    tok_scale = jnp.exp(jax.random.uniform(key_tok, (TOKENS,), jnp.float32, math.log(0.3), math.log(3.0)))
    values = base * ramp[:, None] * tok_scale[None, :]
    return jnp.clip(values, -50.0, 50.0).astype(jnp.bfloat16)


def draw_w_head(key, part):
    key_base = jax.random.fold_in(jax.random.fold_in(key, 23), 0)
    spread = 2.0 / math.sqrt(C)
    values = jnp.clip(jax.random.normal(key_base, (C, K), jnp.float32), -4.0, 4.0) * spread
    return jnp.clip(values, -3.0, 3.0).astype(jnp.bfloat16)


def plant(values, rng, least, largest):
    longest = values.shape.index(max(values.shape))
    spots = []
    for shift in (0, 1):
        where = [jax.random.randint(jax.random.fold_in(rng, axis), (), 0, length) for axis, length in enumerate(values.shape)]
        where[longest] = (where[longest] + shift) % values.shape[longest]
        spots.append(tuple(where))
    return values.at[spots[0]].set(least).at[spots[1]].set(largest)


def block_levels(stream_key, shape, cuts, least, top_value):
    loudness, own = 1.0, jax.random.fold_in(stream_key, 6)
    for position, parts in cuts:
        heights = jnp.exp(jax.random.uniform(jax.random.fold_in(own, position), (parts,), jnp.float32, least / len(cuts), top_value / len(cuts)))
        loudness = loudness * jnp.repeat(heights, shape[position] // parts).reshape([-1 if axis == position else 1 for axis in range(len(shape))])
    return loudness


def gaussian(key, extent, scale, most, cuts=(), kind=jnp.bfloat16):
    result = jax.random.normal(key, extent, jnp.float32) * scale
    if len(cuts) > 0:
        result = block_levels(key, extent, cuts, -0.22, 0.18) * result
    return jnp.clip(result, min=-most, max=most).astype(kind)


def setup_inputs(seed: int = 0, part: int = 0) -> dict:
    key_of = jax.random.split(jax.random.key(seed), 9)
    part_splits = jax.random.split(jax.random.fold_in(key_of[8], part), 9)
    features = draw_features(jax.random.fold_in(jax.random.fold_in(key_of[8], part), 71), part)
    dw_weight = gaussian(key_of[1], (C, KS * KS), (KS * KS) ** -0.5, 0.875, ((0, 16),), jnp.float32)
    norm_gain = jnp.clip(1.0 + 0.15 * jax.random.normal(key_of[2], (C,), jnp.float32), 0.25, 1.75)
    layer_scale = jnp.clip(jnp.exp(jax.random.uniform(key_of[3], (C,), jnp.float32, math.log(0.2), math.log(1.0))), 0.2, 1.0)
    w_in = gaussian(key_of[4], (FF, C), C ** -0.5, 0.125, ((0, 16),))
    w_out = gaussian(key_of[5], (FF, C), FF ** -0.5, 0.0625, ((0, 16),))
    w_head = draw_w_head(jax.random.fold_in(key_of[8], 71), part)
    labels = plant(jax.random.randint(part_splits[7], (TOKENS,), 0, K), jax.random.fold_in(part_splits[7], 1), 0, K - 1).astype(jnp.int32)
    return {"features": features, "dw_weight": dw_weight, "norm_gain": norm_gain, "layer_scale": layer_scale, "w_in": w_in, "w_out": w_out, "w_head": w_head, "labels": labels}


norm_eps = 1e-06

def conv_apply(in_grid, kernel):
    half = KS // 2
    padded = jnp.pad(in_grid, ((0, 0), (half, half), (half, half)))
    running = jnp.zeros(in_grid.shape, in_grid.dtype)
    for row_shift in range(KS):
        for col_shift in range(KS):
            tap = kernel[:, row_shift * KS + col_shift]
            running = running + tap[:, None, None] * padded[:, row_shift:row_shift + WIN_H, col_shift:col_shift + WIN_W]
    return running

def gelu_parts(values):
    cum_prob = 0.5 * (1.0 + lax.erf(values * 0.7071067811865476))
    density = jnp.exp(-0.5 * values * values) * 0.3989422804014327
    return (values * cum_prob, cum_prob + values * density)

def reference(features, dw_weight, norm_gain, layer_scale, w_in, w_out, w_head, labels):
    highest = lax.Precision.HIGHEST
    inputs_wide = features.astype(jnp.float32)
    in_grid = inputs_wide.reshape(C, WIN_H, WIN_W)
    conv_out = conv_apply(in_grid, dw_weight).reshape(C, TOKENS).astype(jnp.bfloat16)
    conv_wide = conv_out.astype(jnp.float32)
    tok_mean = lax.optimization_barrier(jnp.mean(conv_wide, axis=0))
    centered = conv_wide - tok_mean[None, :]
    tok_var = lax.optimization_barrier(jnp.mean(centered * centered, axis=0))
    inv_std = 1.0 / jnp.sqrt(tok_var + norm_eps)
    normed = centered * inv_std[None, :]
    norm_out = (norm_gain[:, None] * normed).astype(jnp.bfloat16)
    pre_act = jnp.dot(w_in, norm_out, preferred_element_type=jnp.float32)
    gelu_out, gelu_slope = gelu_parts(pre_act)
    hidden = gelu_out.astype(jnp.bfloat16)
    branch_sum = lax.dot_general(w_out, hidden, (((0,), (0,)), ((), ())), preferred_element_type=jnp.float32)
    block_out = inputs_wide + layer_scale[:, None] * branch_sum
    head_wide = w_head.astype(jnp.float32)
    logits = lax.dot_general(block_out, head_wide, (((0,), (0,)), ((), ())), precision=highest)
    row_max = lax.optimization_barrier(jnp.max(logits, axis=1, keepdims=True))
    exp_terms = jnp.exp(logits - row_max)
    exp_total = lax.optimization_barrier(jnp.sum(exp_terms, axis=1, keepdims=True))
    log_total = jnp.log(exp_total) + row_max
    onehot = (labels[:, None] == jnp.arange(K, dtype=jnp.int32)[None, :]).astype(jnp.float32)
    picked = lax.optimization_barrier(jnp.sum(logits * onehot, axis=1))
    mean_loss = jnp.mean(log_total[:, 0] - picked).reshape(1)
    logit_grad = exp_terms / exp_total - onehot
    out_grad = lax.dot_general(head_wide, logit_grad, (((1,), (1,)), ((), ())), precision=highest)
    d_head = jnp.dot(block_out, logit_grad, precision=highest)
    d_scale = lax.optimization_barrier(jnp.sum(out_grad * branch_sum, axis=1))
    branch_grad = (layer_scale[:, None] * out_grad).astype(jnp.bfloat16)
    hidden_grad = jnp.dot(w_out, branch_grad, preferred_element_type=jnp.float32)
    d_w_out = lax.dot_general(hidden, branch_grad, (((1,), (1,)), ((), ())), preferred_element_type=jnp.float32)
    pre_grad = (hidden_grad * gelu_slope).astype(jnp.bfloat16)
    d_w_in = lax.dot_general(pre_grad, norm_out, (((1,), (1,)), ((), ())), preferred_element_type=jnp.float32)
    norm_grad = lax.dot_general(w_in, pre_grad, (((0,), (0,)), ((), ())), preferred_element_type=jnp.float32)
    gained = norm_gain[:, None] * norm_grad
    conv_grad = (gained - lax.optimization_barrier(jnp.mean(gained, axis=0))[None, :] - normed * lax.optimization_barrier(jnp.mean(gained * normed, axis=0))[None, :]) * inv_std[None, :]
    unused, pullback = jax.vjp(conv_apply, in_grid, dw_weight)
    grid_grad, d_dw = pullback(conv_grad.reshape(C, WIN_H, WIN_W))
    d_features = out_grad + grid_grad.reshape(C, TOKENS)
    return (d_features, d_dw, d_scale, d_w_in, d_w_out, d_head, mean_loss)
```

```python
import jax
import jax.numpy as jnp
import numpy as np
from jax import lax
from jax.sharding import PartitionSpec as P

KS = 7
WIN_H = 32
WIN_W = 32
norm_eps = 1e-06

WALK = (0, 2, 4, 6, 7, 5, 3, 1)
CHIPS = len(WALK)
REL = np.array([[WALK[(WALK.index(chip) + d) % CHIPS] for d in range(CHIPS)] for chip in range(CHIPS)], np.int32)


def walk_perm(step):
    return [
        (WALK[p] * 2 + c, WALK[(p + step) % CHIPS] * 2 + c) for p in range(CHIPS) for c in range(2)
    ]


def flip_perm(bit):
    return [(i, i ^ bit) for i in range(2 * CHIPS)]


def send(value, perm):
    return lax.ppermute(value, "ch", perm)


FORTH, BACK, SIBLING = walk_perm(1), walk_perm(-1), flip_perm(1)


def gather_walk(block):
    half = block.shape[0] // 2
    mine = [None] * CHIPS
    mine[0] = forth = back = block
    for step in range(1, CHIPS // 2):
        forth, back = send(forth, FORTH), send(back, BACK)
        mine[(-step) % CHIPS], mine[step] = forth, back
    upper, lower = send(forth[:half], FORTH), send(back[half:], BACK)
    mine[CHIPS // 2] = jnp.concatenate([upper, lower], axis=0)
    return [(b, send(b, SIBLING)) for b in mine]


def scatter_walk(parts):
    half = parts[0].shape[0] // 2
    far = parts[CHIPS // 2]
    forth, back = send(far[:half], FORTH), send(far[half:], BACK)
    wide = lambda v: v.astype(jnp.float32)
    for step in range(CHIPS // 2 - 1, 0, -1):
        ahead, behind = wide(parts[step]), wide(parts[(-step) % CHIPS])
        if step == CHIPS // 2 - 1:
            ahead = jnp.concatenate([ahead[:half] + wide(forth), ahead[half:]], axis=0)
            behind = jnp.concatenate([behind[:half], behind[half:] + wide(back)], axis=0)
        else:
            ahead, behind = ahead + wide(forth), behind + wide(back)
        forth, back = send(ahead.astype(jnp.bfloat16), FORTH), send(behind.astype(jnp.bfloat16), BACK)
    return wide(parts[0]) + wide(forth) + wide(back)


def conv_apply(in_grid, kernel):
    half = KS // 2
    padded = jnp.pad(in_grid, ((0, 0), (half, half), (half, half)))
    running = jnp.zeros(in_grid.shape, in_grid.dtype)
    for row_shift in range(KS):
        for col_shift in range(KS):
            tap = kernel[:, row_shift * KS + col_shift]
            running = (
                running
                + tap[:, None, None]
                * padded[:, row_shift : row_shift + WIN_H, col_shift : col_shift + WIN_W]
            )
    return running


def gelu_parts(values):
    cum_prob = 0.5 * (1.0 + lax.erf(values * 0.7071067811865476))
    density = jnp.exp(-0.5 * values * values) * 0.3989422804014327
    return (values * cum_prob, cum_prob + values * density)


def dot(a, b, dims):
    return lax.dot_general(a, b, (dims, ((), ())), preferred_element_type=jnp.float32)


def halves(value, bit, me):
    width = value.shape[1] // 2
    up = (me & bit) != 0
    low, high = value[:, :width], value[:, width:]
    return jnp.where(up, high, low), jnp.where(up, low, high)


def join(kept, other, bit, me):
    up = (me & bit) != 0
    return jnp.where(up, jnp.concatenate([other, kept], 1), jnp.concatenate([kept, other], 1))


def per_device(features, dw_weight, norm_gain, layer_scale, w_in, w_out, w_head, labels):
    bf, f32 = jnp.bfloat16, jnp.float32
    rows, tok_count = features.shape
    channels = w_in.shape[1]
    classes = w_head.shape[1]
    me = lax.axis_index("ch")
    core = me % 2
    rel_chip = jnp.asarray(REL)[me // 2]
    order = jnp.stack([rel_chip * 2 + core, rel_chip * 2 + 1 - core], 1).reshape(-1)
    my_scale = lax.dynamic_slice_in_dim(layer_scale, me * rows, rows, 0)
    my_head = lax.dynamic_slice_in_dim(w_head, me * rows, rows, 0)

    inputs_wide = features.astype(f32)
    in_grid = inputs_wide.reshape(rows, WIN_H, WIN_W)
    conv_out = conv_apply(in_grid, dw_weight).reshape(rows, tok_count).astype(bf)
    pairs = gather_walk(conv_out)
    conv_all = jnp.concatenate([b for pair in pairs for b in pair], axis=0)

    gain_rel = norm_gain.reshape(-1, rows)[order].reshape(-1)
    w_rel = w_in.reshape(-1, 2 * CHIPS, rows)[:, order].reshape(w_in.shape)
    w_gain = (w_rel.astype(f32) * gain_rel[None, :]).astype(bf)
    gain_sum = jnp.sum(w_gain.astype(f32), axis=1)
    head_scaled = (layer_scale[:, None] * w_head.astype(f32)).astype(bf)
    mix = dot(w_out, head_scaled, ((1,), (0,))).astype(bf)

    conv_wide = conv_all.astype(f32)
    tok_mean = jnp.mean(conv_wide, axis=0)
    centered = conv_wide - tok_mean[None, :]
    inv_std = lax.rsqrt(jnp.mean(centered * centered, axis=0) + norm_eps)
    pre_act = (dot(w_gain, conv_all, ((1,), (0,))) - gain_sum[:, None] * tok_mean[None, :]) * inv_std[None, :]
    gelu_out, gelu_slope = gelu_parts(pre_act)
    hidden = gelu_out.astype(bf)
    logits = dot(mix, hidden, ((0,), (0,))) + dot(my_head, features, ((0,), (0,)))
    kept = jnp.pad(logits, ((0, 2), (0, 0)))
    for bit in (1, 2, 4):
        keep, give = halves(kept, bit, me)
        kept = keep + send(give, flip_perm(bit))
    kept = kept + send(kept, flip_perm(8))
    labels_kept = labels[None, :]
    for bit in (1, 2, 4):
        labels_kept, _ = halves(labels_kept, bit, me)
    class_id = lax.broadcasted_iota(jnp.int32, kept.shape, 0)
    real = class_id < classes
    kept = jnp.where(real, kept, -jnp.inf)
    col_max = jnp.max(kept, axis=0, keepdims=True)
    exp_terms = jnp.exp(kept - col_max)
    exp_total = jnp.sum(exp_terms, axis=0, keepdims=True)
    onehot = class_id == labels_kept
    picked = jnp.sum(jnp.where(onehot, kept, 0.0), axis=0, keepdims=True)
    loss = jnp.log(exp_total) + col_max - picked
    loss_high = loss.astype(bf).astype(f32)
    grad = exp_terms / exp_total - onehot.astype(f32)
    grad = jnp.where(class_id == classes, loss_high, jnp.where(class_id == classes + 1, loss - loss_high, grad))
    grad = grad.astype(bf)
    for bit in (4, 2, 1):
        grad = join(grad, send(grad, flip_perm(bit)), bit, me)
    loss_rows = grad[classes:].astype(f32)
    mean_loss = (jnp.sum(loss_rows) / tok_count).reshape(1)
    grad = grad[:classes]

    out_grad = dot(my_head, grad, ((1,), (0,)))
    hidden_grad = dot(mix, grad, ((1,), (0,)))
    pre_scaled = (hidden_grad * gelu_slope * inv_std[None, :]).astype(bf)
    pre_wide = pre_scaled.astype(f32)
    mean_part = jnp.sum(pre_wide * gain_sum[:, None], axis=0) / channels
    proj_part = jnp.sum(pre_wide * pre_act, axis=0) / channels
    mixed = dot(hidden, grad, ((1,), (1,))).astype(bf)
    d_w_out = dot(mixed, w_head, ((1,), (1,))) * layer_scale[None, :]

    to_channels = dot(w_gain, pre_scaled, ((0,), (0,)))
    w_out_rel = w_out.reshape(-1, 2 * CHIPS, rows)[:, order].reshape(w_out.shape)
    branch = dot(mixed, w_out_rel, ((0,), (0,)))
    branch = jnp.pad(branch, ((0, 160 - classes), (0, 0))).reshape(20, 8, 2 * CHIPS, rows)
    branch = branch.transpose(2, 0, 1, 3).reshape(2 * CHIPS, 20, 8 * rows)
    extra = jnp.concatenate(
        [branch, jnp.broadcast_to(jnp.stack([mean_part, proj_part])[None], (2 * CHIPS, 2, tok_count)), jnp.zeros((2 * CHIPS, 10, tok_count), f32)], axis=1
    )
    blocks = jnp.concatenate([to_channels.reshape(2 * CHIPS, rows, tok_count), extra], axis=1)
    parts = []
    for d in range(CHIPS):
        theirs = send(blocks[2 * d + 1].astype(bf), SIBLING)
        parts.append((blocks[2 * d] + theirs.astype(f32)).astype(bf))
    got = scatter_walk(parts)
    branch_mine = got[rows : rows + 20].reshape(160, rows)[:classes].T
    mean_all, proj_all = got[rows + 20], got[rows + 21]

    shift = jnp.sum(pre_wide * tok_mean[None, :], axis=1)
    d_w_in_rel = (dot(pre_scaled, conv_all, ((1,), (1,))) - shift[:, None]) * gain_rel[None, :]
    back_order = jnp.argsort(order)
    d_w_in = d_w_in_rel.reshape(-1, 2 * CHIPS, rows)[:, back_order].reshape(w_in.shape)
    d_head = dot(features, grad, ((1,), (1,))) + my_scale[:, None] * branch_mine
    d_scale = jnp.sum(my_head.astype(f32) * branch_mine, axis=1)

    normed = (conv_out.astype(f32) - tok_mean[None, :]) * inv_std[None, :]
    conv_grad = got[:rows] - mean_all[None, :] - normed * proj_all[None, :]
    unused, pullback = jax.vjp(conv_apply, in_grid, dw_weight)
    grid_grad, d_dw = pullback(conv_grad.reshape(rows, WIN_H, WIN_W))
    d_features = out_grad + grid_grad.reshape(rows, tok_count)
    return (d_features, d_dw, d_scale, d_w_in, d_w_out, d_head, mean_loss)


def plain_device(features, dw_weight, norm_gain, layer_scale, w_in, w_out, w_head, labels):
    highest = lax.Precision.HIGHEST
    my_rows = features.shape[0]
    tok_count = features.shape[1]
    class_count = w_head.shape[1]
    row_offset = lax.axis_index("ch") * my_rows
    inputs_wide = features.astype(jnp.float32)
    in_grid = inputs_wide.reshape(my_rows, WIN_H, WIN_W)
    conv_out = conv_apply(in_grid, dw_weight).reshape(my_rows, tok_count).astype(jnp.bfloat16)
    conv_all = lax.all_gather(conv_out, "ch", axis=0, tiled=True)
    conv_wide = conv_all.astype(jnp.float32)
    tok_mean = jnp.mean(conv_wide, axis=0)
    centered = conv_wide - tok_mean[None, :]
    tok_var = jnp.mean(centered * centered, axis=0)
    inv_std = 1.0 / jnp.sqrt(tok_var + norm_eps)
    normed = centered * inv_std[None, :]
    norm_out = (norm_gain[:, None] * normed).astype(jnp.bfloat16)
    pre_act = jnp.dot(w_in, norm_out, preferred_element_type=jnp.float32)
    gelu_out, gelu_slope = gelu_parts(pre_act)
    hidden = gelu_out.astype(jnp.bfloat16)
    my_scale = lax.dynamic_slice_in_dim(layer_scale, row_offset, my_rows, 0)
    head_wide = w_head.astype(jnp.float32)
    my_head = lax.dynamic_slice_in_dim(head_wide, row_offset, my_rows, 0)
    w_cols = w_out
    branch_sum = lax.psum_scatter(
        lax.dot_general(
            w_cols, hidden, (((0,), (0,)), ((), ())), preferred_element_type=jnp.float32
        ),
        "ch",
        scatter_dimension=0,
        tiled=True,
    )
    block_out = inputs_wide + my_scale[:, None] * branch_sum
    part_logits = lax.dot_general(block_out, my_head, (((0,), (0,)), ((), ())), precision=highest)
    logits = lax.psum(part_logits, "ch")
    row_max = jnp.max(logits, axis=1, keepdims=True)
    exp_terms = jnp.exp(logits - row_max)
    exp_total = jnp.sum(exp_terms, axis=1, keepdims=True)
    log_total = jnp.log(exp_total) + row_max
    onehot = (labels[:, None] == jnp.arange(class_count, dtype=jnp.int32)[None, :]).astype(
        jnp.float32
    )
    picked = jnp.sum(logits * onehot, axis=1)
    mean_loss = jnp.mean(log_total[:, 0] - picked).reshape(1)
    logit_grad = exp_terms / exp_total - onehot
    out_grad = lax.dot_general(my_head, logit_grad, (((1,), (1,)), ((), ())), precision=highest)
    d_head = jnp.dot(block_out, logit_grad, precision=highest)
    d_scale = jnp.sum(out_grad * branch_sum, axis=1)
    branch_grad = (my_scale[:, None] * out_grad).astype(jnp.bfloat16)
    incoming = lax.all_gather(branch_grad, "ch", axis=0, tiled=True)
    hidden_acc = jnp.dot(w_cols, incoming, preferred_element_type=jnp.float32)
    tile_grad = lax.dot_general(
        hidden, incoming, (((1,), (1,)), ((), ())), preferred_element_type=jnp.float32
    )
    pre_grad = (hidden_acc * gelu_slope).astype(jnp.bfloat16)
    d_w_in = lax.dot_general(
        pre_grad, norm_out, (((1,), (1,)), ((), ())), preferred_element_type=jnp.float32
    )
    norm_grad = lax.dot_general(
        w_in, pre_grad, (((0,), (0,)), ((), ())), preferred_element_type=jnp.float32
    )
    gained = norm_gain[:, None] * norm_grad
    conv_term = (
        gained
        - jnp.mean(gained, axis=0)[None, :]
        - normed * jnp.mean(gained * normed, axis=0)[None, :]
    ) * inv_std[None, :]
    conv_grad = lax.psum_scatter(conv_term, "ch", scatter_dimension=0, tiled=True)
    unused, pullback = jax.vjp(conv_apply, in_grid, dw_weight)
    grid_grad, d_dw = pullback(conv_grad.reshape(my_rows, WIN_H, WIN_W))
    d_features = out_grad + grid_grad.reshape(my_rows, tok_count)
    return (d_features, d_dw, d_scale, d_w_in, tile_grad, d_head, mean_loss)


def solution(mesh):
    placed = (P("ch", "grp"), P("ch", None), P(), P(), P("ch", None), P("ch", None), P(), P("grp"))
    return jax.shard_map(
        per_device if mesh.shape["ch"] == 2 * CHIPS else plain_device,
        mesh=mesh,
        in_specs=placed,
        out_specs=(
            P("ch", "grp"),
            P("ch", "grp"),
            P(("grp", "ch")),
            P(("grp", "ch"), None),
            P(("grp", "ch"), None),
            P("ch", "grp"),
            P("grp"),
        ),
        check_vma=False,
    )
```

```python
import functools

import jax
import jax.numpy as jnp
import numpy as np
from jax import lax
from jax.experimental import pallas as pl
from jax.experimental.pallas import tpu as pltpu
from jax.sharding import PartitionSpec as P

KS = 7
HALF = KS // 2
WIN_H = 32
WIN_W = 32
norm_eps = 1e-06
BF = jnp.bfloat16
F32 = jnp.float32

WALK = (0, 2, 4, 6, 7, 5, 3, 1)
CHIPS = len(WALK)
REL = np.array([[WALK[(WALK.index(chip) + d) % CHIPS] for d in range(CHIPS)] for chip in range(CHIPS)], np.int32)
CLASS_ROWS = 160
EXTRA = 24
LANE = 128


def walk_perm(step):
    return [
        (WALK[p] * 2 + c, WALK[(p + step) % CHIPS] * 2 + c) for p in range(CHIPS) for c in range(2)
    ]


def flip_perm(bit):
    return [(i, i ^ bit) for i in range(2 * CHIPS)]


def send(value, perm):
    return lax.ppermute(value, "ch", perm)


FORTH, BACK, SIBLING = walk_perm(1), walk_perm(-1), flip_perm(1)
VMEM = pl.BlockSpec(memory_space=pltpu.VMEM)
SMEM = pl.BlockSpec(memory_space=pltpu.SMEM)


def call(kernel, outs, ins, scratch=(), flops=0, moved=0, limit=40, name=None):
    result = pl.pallas_call(
        kernel,
        out_shape=[jax.ShapeDtypeStruct(s, d) for s, d in outs],
        in_specs=[s for _, s in ins],
        out_specs=[VMEM] * len(outs),
        scratch_shapes=list(scratch),
        compiler_params=pltpu.CompilerParams(vmem_limit_bytes=limit << 20),
        cost_estimate=pl.CostEstimate(flops=int(flops), bytes_accessed=int(moved), transcendentals=0),
        name=name,
    )(*[a for a, _ in ins])
    return result


def dot(a, b, dims):
    return lax.dot_general(a, b, (dims, ((), ())), preferred_element_type=F32)


def shifted_copies(grid_pad, copies):
    for j in range(KS):
        copies[j] = grid_pad[:, pl.ds(8 + j - HALF, WIN_W), :]


def clear_border(grid_pad):
    grid_pad[...] = jnp.zeros_like(grid_pad)


def put_rows(grid_pad, row, tile):
    grid_pad[pl.ds(row + HALF, 4), pl.ds(8, WIN_W), :] = tile.T.reshape(4, WIN_W, tile.shape[0])


def put_taps(weight, taps):
    square = jnp.concatenate([weight, jnp.zeros((weight.shape[0], LANE - KS * KS), F32)], axis=1)
    taps[...] = square.T


def conv_rows(copies, taps, row, flip):
    acc = None
    for j in range(KS):
        for i in range(KS):
            index = (KS - 1 - i) * KS + KS - 1 - j if flip else i * KS + j
            term = taps[index : index + 1, :][None] * copies[j, pl.ds(row + i, 4)]
            acc = term if acc is None else acc + term
    return acc


def conv_kernel(x_ref, w_ref, out_ref, grid_pad, copies, taps):
    clear_border(grid_pad)
    put_taps(w_ref[...], taps)
    for g in range(8):
        put_rows(grid_pad, 4 * g, x_ref[:, g * LANE : (g + 1) * LANE].astype(F32))
    shifted_copies(grid_pad, copies)

    for g in range(8):
        acc = conv_rows(copies, taps, 4 * g, False)
        out_ref[:, g * LANE : (g + 1) * LANE] = acc.reshape(LANE, LANE).T.astype(BF)


def weights_kernel(w_in_ref, gain_ref, w_out_ref, scale_ref, head_ref, w_gain_ref, w_gain_t_ref, gain_sum_ref, mix_ref):
    w_gain = (w_in_ref[...].astype(F32) * gain_ref[...]).astype(BF)
    w_gain_ref[...] = w_gain
    w_gain_t_ref[...] = w_gain.T
    gain_sum_ref[...] = jnp.sum(w_gain.astype(F32), axis=1, keepdims=True)
    scaled = (head_ref[...].astype(F32) * scale_ref[...]).astype(BF)
    mix_ref[...] = dot(w_out_ref[...], scaled, ((1,), (0,))).astype(BF)


def add_blocks(offs_ref, w_gain_ref, blocks, ids, shift, acc, sums):
    for n, (own, sib) in enumerate(blocks):
        left = w_gain_ref[:, pl.ds(pl.multiple_of(offs_ref[2 * ids[n]], LANE), LANE)]
        right = w_gain_ref[:, pl.ds(pl.multiple_of(offs_ref[2 * ids[n] + 1], LANE), LANE)]
        pair = jnp.concatenate([own[...], sib[...]], axis=0)
        term = dot(jnp.concatenate([left, right], axis=1), pair, ((1,), (0,)))
        acc = term if acc is None else acc + term
        away = pair.astype(F32) - shift
        first = jnp.sum(away, axis=0, keepdims=True)
        second = jnp.sum(away * away, axis=0, keepdims=True)
        sums = (first, second) if sums is None else (sums[0] + first, sums[1] + second)
    return acc, sums


def early_kernel(ids, offs_ref, w_gain_ref, *refs):
    blocks, (acc_ref, sums_ref) = refs[:-2], refs[-2:]
    blocks = [(blocks[2 * n], blocks[2 * n + 1]) for n in range(len(ids))]
    shift = jnp.mean(blocks[0][0][...].astype(F32), axis=0, keepdims=True)
    acc, (first, second) = add_blocks(offs_ref, w_gain_ref, blocks, ids, shift, None, None)
    acc_ref[...] = acc
    sums_ref[...] = jnp.concatenate([shift, first, second, jnp.zeros((5, shift.shape[1]), F32)], axis=0)


def forward_kernel(ids, classes, offs_ref, w_gain_ref, acc_ref, sums_ref, gain_sum_ref, mix_ref, head_ref, x_ref, *refs):
    blocks, (pre_ref, hidden_ref, stats_ref, logits_ref) = refs[:-4], refs[-4:]
    blocks = [(blocks[2 * n], blocks[2 * n + 1]) for n in range(len(ids))]
    shift, first, second = sums_ref[0:1, :], sums_ref[1:2, :], sums_ref[2:3, :]
    acc, (first, second) = add_blocks(offs_ref, w_gain_ref, blocks, ids, shift, acc_ref[...], (first, second))
    channels = w_gain_ref.shape[1]
    away = first / channels
    tok_mean = shift + away
    inv_std = lax.rsqrt(second / channels - away * away + norm_eps)
    stats_ref[...] = jnp.concatenate([tok_mean, inv_std, jnp.zeros((6, shift.shape[1]), F32)], axis=0)
    pre_act = (acc - gain_sum_ref[...] * tok_mean) * inv_std
    pre_ref[...] = pre_act
    hidden = (pre_act * (0.5 * (1.0 + lax.erf(pre_act * 0.7071067811865476)))).astype(BF)
    hidden_ref[...] = hidden
    logits = dot(mix_ref[...], hidden, ((0,), (0,))) + dot(head_ref[...], x_ref[...], ((0,), (0,)))
    core = offs_ref[2 * CHIPS]
    chunks = logits_ref.shape[1]
    for g in range(2 * chunks):
        logits_ref[(g // chunks) ^ core, g % chunks] = logits[:, g * LANE : (g + 1) * LANE]


def slope_kernel(pre_ref, stats_ref, slope_ref):
    pre_act = pre_ref[...]
    cum_prob = 0.5 * (1.0 + lax.erf(pre_act * 0.7071067811865476))
    density = jnp.exp(-0.5 * pre_act * pre_act) * 0.3989422804014327
    slope_ref[...] = (cum_prob + pre_act * density) * stats_ref[1:2, :]


def grad_kernel(offs_ref, own_ref, sib_ref, mix_ref, slope_ref, pre_ref, gain_sum_ref, hidden_ref, grad_ref, scaled_ref, means_ref, mixed_ref):
    core = offs_ref[2 * CHIPS]
    chunks = own_ref.shape[0]
    for g in range(chunks):
        grad_ref[:, pl.ds(pl.multiple_of((core * chunks + g) * LANE, LANE), LANE)] = own_ref[g]
        grad_ref[:, pl.ds(pl.multiple_of(((1 - core) * chunks + g) * LANE, LANE), LANE)] = sib_ref[g]
    grad = grad_ref[...]
    scaled = (dot(mix_ref[...], grad, ((1,), (0,))) * slope_ref[...]).astype(BF)
    scaled_ref[...] = scaled
    wide = scaled.astype(F32)
    mean_part = jnp.sum(wide * gain_sum_ref[...], axis=0, keepdims=True)
    proj_part = jnp.sum(wide * pre_ref[...], axis=0, keepdims=True)
    rows = [part[:, g * LANE : (g + 1) * LANE] for part in (mean_part, proj_part) for g in range(8)]
    means_ref[...] = jnp.concatenate(rows + [jnp.zeros((EXTRA - 16, LANE), F32)], axis=0)
    mixed_ref[...] = dot(hidden_ref[...], grad, ((1,), (1,))).astype(BF)


def message_kernel(ids, offs_ref, w_gain_t_ref, scaled_ref, w_out_ref, mixed_ref, means_ref, *outs):
    scaled = scaled_ref[...]
    for n, d in enumerate(ids):
        for side in range(2):
            off = pl.multiple_of(offs_ref[2 * d + side], LANE)
            rows = dot(w_gain_t_ref[pl.ds(off, LANE), :], scaled, ((1,), (0,)))
            branch = dot(mixed_ref[...], w_out_ref[:, pl.ds(off, LANE)], ((0,), (0,)))
            branch = jnp.concatenate([branch, jnp.zeros((7 * EXTRA - CLASS_ROWS, LANE), F32)], axis=0)
            extra = jnp.concatenate([branch[g * EXTRA : (g + 1) * EXTRA] for g in range(7)] + [means_ref[...]], axis=1)
            message = jnp.concatenate([rows, extra], axis=0)
            out = outs[2 * n + side]
            out[...] = message.astype(out.dtype)


def d_w_out_kernel(mixed_ref, head_ref, scale_ref, out_ref):
    out_ref[...] = dot(mixed_ref[...], head_ref[...], ((1,), (1,))) * scale_ref[...]


def d_w_in_kernel(offs_ref, scaled_ref, stats_ref, gain_ref, *refs):
    blocks, out_ref = refs[:-1], refs[-1]
    scaled = scaled_ref[...]
    shift = jnp.sum(scaled.astype(F32) * stats_ref[0:1, :], axis=1, keepdims=True)
    for d in range(CHIPS):
        pair = jnp.concatenate([blocks[2 * d][...], blocks[2 * d + 1][...]], axis=0)
        both = dot(scaled, pair, ((1,), (1,))) - shift
        for side in range(2):
            at = pl.ds(pl.multiple_of(offs_ref[2 * d + side], LANE), LANE)
            out_ref[:, at] = both[:, side * LANE : (side + 1) * LANE] * gain_ref[:, at]


def last_kernel(classes, mine_ref, forth_ref, back_ref, x_ref, conv_ref, stats_ref, w_ref, head_ref, scale_ref, grad_ref,
                d_x_ref, d_dw_ref, d_scale_ref, d_head_ref, grid_pad, copies, taps, copies_x, sums):
    rows, tokens = x_ref.shape
    channels = rows * 2 * CHIPS
    got = mine_ref[...].astype(F32) + forth_ref[...].astype(F32) + back_ref[...].astype(F32)
    extra = got[rows:]
    branch = jnp.concatenate([extra[:, g * LANE : (g + 1) * LANE] for g in range(7)], axis=0)[:CLASS_ROWS]
    means = extra[:, 7 * LANE :]
    tok_mean, inv_std = stats_ref[0:1, :], stats_ref[1:2, :]
    put_taps(w_ref[...], taps)
    clear_border(grid_pad)
    for g in range(8):
        put_rows(grid_pad, 4 * g, x_ref[:, g * LANE : (g + 1) * LANE].astype(F32))
    shifted_copies(grid_pad, copies_x)
    for g in range(8):
        at = slice(g * LANE, (g + 1) * LANE)
        normed = (conv_ref[:, at].astype(F32) - tok_mean[:, at]) * inv_std[:, at]
        conv_grad = got[:rows, at] - (means[g : g + 1, :] + normed * means[8 + g : 9 + g, :]) * (1.0 / channels)
        put_rows(grid_pad, 4 * g, conv_grad)
    shifted_copies(grid_pad, copies)
    out_grad = dot(head_ref[...], grad_ref[...], ((1,), (0,)))
    for g in range(8):
        at = slice(g * LANE, (g + 1) * LANE)
        d_x_ref[:, at] = out_grad[:, at] + conv_rows(copies, taps, 4 * g, True).reshape(LANE, LANE).T
        conv_grad = copies[HALF, pl.ds(4 * g + HALF, 4)]
        for j in range(KS):
            for i in range(KS):
                prod = (conv_grad * copies_x[j, pl.ds(4 * g + i, 4)]).reshape(16, 8, LANE)
                total = jnp.sum(prod, axis=0)
                index = i * KS + j
                if g == 0:
                    sums[index] = total
                else:
                    sums[index] += total
    d_taps = jnp.sum(sums[...], axis=1)
    d_taps = jnp.concatenate([d_taps, jnp.zeros((LANE - KS * KS, rows), F32)], axis=0).T
    d_dw_ref[...] = d_taps[:, : KS * KS]
    branch = jnp.concatenate([branch, jnp.zeros((2 * LANE - CLASS_ROWS, rows), F32)], axis=0).T
    branch = branch[:, :CLASS_ROWS]
    d_scale_ref[...] = jnp.sum(head_ref[...].astype(F32) * branch, axis=1, keepdims=True)
    d_head = dot(x_ref[...], grad_ref[...], ((1,), (1,))) + scale_ref[...] * branch
    d_head_ref[...] = d_head[:, :classes]


def gather_walk(block):
    half = block.shape[0] // 2
    mine = [None] * CHIPS
    mine[0] = forth = back = block
    for step in range(1, CHIPS // 2):
        forth, back = send(forth, FORTH), send(back, BACK)
        mine[(-step) % CHIPS], mine[step] = forth, back
    upper, lower = send(forth[:half], FORTH), send(back[half:], BACK)
    mine[CHIPS // 2] = jnp.concatenate([upper, lower], axis=0)
    return [(b, send(b, SIBLING)) for b in mine]


def sum_kernel(widths, *refs):
    for n, at in enumerate(widths):
        own, sib, arrived, out = refs[n], refs[len(widths) + n], refs[2 * len(widths) + n], refs[3 * len(widths) + n]
        total = own[...] + sib[...].astype(F32)
        more = arrived[...].astype(F32)
        if at > 0:
            total = jnp.concatenate([total[:at] + more, total[at:]], axis=0) if more.shape[0] < total.shape[0] else total + more
        elif at < 0:
            total = jnp.concatenate([total[:at], total[at:] + more], axis=0)
        else:
            total = total + more
        out[...] = total.astype(BF)


def far_kernel(own, sib, upper, lower):
    total = own[...] + sib[...].astype(F32)
    cut = upper.shape[0]
    upper[...] = total[:cut].astype(BF)
    lower[...] = total[cut:].astype(BF)


def scatter_walk(own, sib):
    height, width = own[0].shape
    cut = 80
    forth, back = call(far_kernel, [((cut, width), BF), ((height - cut, width), BF)], [(own[CHIPS // 2], VMEM), (sib[CHIPS // 2], VMEM)], name="far_sum")
    forth, back = send(forth, FORTH), send(back, BACK)
    for step in range(CHIPS // 2 - 1, 0, -1):
        ends = (cut, cut - height) if step == CHIPS // 2 - 1 else (0, 0)
        other = (-step) % CHIPS
        forth, back = call(
            functools.partial(sum_kernel, ends),
            [((height, width), BF)] * 2,
            [(a, VMEM) for a in (own[step], own[other], sib[step], sib[other], forth, back)],
            name="walk_sum",
        )
        forth, back = send(forth, FORTH), send(back, BACK)
    return forth, back


def per_device(features, dw_weight, norm_gain, layer_scale, w_in, w_out, w_head, labels):
    rows, tokens = features.shape
    hidden_units, channels = w_in.shape
    classes = w_head.shape[1]
    chunks = tokens // LANE // 2
    me = lax.axis_index("ch")
    core = me % 2
    rel_chip = jnp.asarray(REL)[me // 2]
    offs = jnp.stack([rel_chip * 2 + core, rel_chip * 2 + 1 - core], 1).reshape(-1) * rows
    offs = jnp.concatenate([offs, core[None]]).astype(jnp.int32)
    my_scale = lax.dynamic_slice_in_dim(layer_scale, me * rows, rows, 0)[:, None]
    head_pad = jnp.pad(w_head, ((0, 0), (0, CLASS_ROWS - classes)))
    my_head = lax.dynamic_slice_in_dim(head_pad, me * rows, rows, 0)
    grid_shape = pltpu.VMEM((WIN_H + 2 * HALF, WIN_W + 16, LANE), F32)
    copies_shape = pltpu.VMEM((KS, WIN_H + 2 * HALF, WIN_W, LANE), F32)
    taps_shape = pltpu.VMEM((LANE, LANE), F32)

    (conv_out,) = call(
        conv_kernel, [((rows, tokens), BF)], [(features, VMEM), (dw_weight, VMEM)],
        [grid_shape, copies_shape, taps_shape], name="conv_forward",
    )
    pairs = gather_walk(conv_out)
    w_gain, w_gain_t, gain_sum, mix = call(
        weights_kernel,
        [((hidden_units, channels), BF), ((channels, hidden_units), BF), ((hidden_units, 1), F32), ((hidden_units, CLASS_ROWS), BF)],
        [(w_in, VMEM), (norm_gain[None, :], VMEM), (w_out, VMEM), (layer_scale[:, None], VMEM), (head_pad, VMEM)],
        flops=4e9, moved=16e6, name="weights_ready",
    )
    early, late = (0, 1, 7, 2, 6), (3, 5, 4)
    acc, sums = call(
        functools.partial(early_kernel, early),
        [((hidden_units, tokens), F32), ((8, tokens), F32)],
        [(offs, SMEM), (w_gain, VMEM)] + [(b, VMEM) for d in early for b in pairs[d]],
        flops=2e9, moved=8e6, name="forward_early",
    )
    pre_act, hidden, stats, logits = call(
        functools.partial(forward_kernel, late, classes),
        [((hidden_units, tokens), F32), ((hidden_units, tokens), BF), ((8, tokens), F32), ((2, chunks, CLASS_ROWS, LANE), F32)],
        [(offs, SMEM), (w_gain, VMEM), (acc, VMEM), (sums, VMEM), (gain_sum, VMEM), (mix, VMEM), (my_head, VMEM), (features, VMEM)]
        + [(b, VMEM) for d in late for b in pairs[d]],
        flops=2e9, moved=8e6, name="forward_late",
    )
    (slope,) = call(slope_kernel, [((hidden_units, tokens), F32)], [(pre_act, VMEM), (stats, VMEM)], flops=1e9, moved=4e6, name="gelu_slope")

    kept = logits[0] + send(logits[1], SIBLING)
    first = core * chunks
    for bit in (2, 4):
        width = kept.shape[0] // 2
        up = (me // bit) % 2
        keep = lax.dynamic_slice_in_dim(kept, up * width, width, 0)
        give = lax.dynamic_slice_in_dim(kept, (1 - up) * width, width, 0)
        kept = keep + send(give, flip_perm(bit))
        first = first + up * width
    kept = kept[0]
    kept = kept + send(kept, flip_perm(8))
    labels_kept = lax.dynamic_slice_in_dim(labels, first * LANE, LANE, 0)[None, :]
    class_id = lax.broadcasted_iota(jnp.int32, kept.shape, 0)
    kept = jnp.where(class_id < classes, kept, -jnp.inf)
    col_max = jnp.max(kept, axis=0, keepdims=True)
    exp_terms = jnp.exp(kept - col_max)
    exp_total = jnp.sum(exp_terms, axis=0, keepdims=True)
    onehot = class_id == labels_kept
    picked = jnp.sum(jnp.where(onehot, kept, 0.0), axis=0, keepdims=True)
    loss = jnp.log(exp_total) + col_max - picked
    loss_high = loss.astype(BF).astype(F32)
    grad = exp_terms / exp_total - onehot.astype(F32)
    grad = jnp.where(class_id == classes, loss_high, jnp.where(class_id == classes + 1, loss - loss_high, grad))
    grad = grad.astype(BF)[None]
    for bit in (4, 2):
        other = send(grad, flip_perm(bit))
        up = (me // bit) % 2 == 1
        grad = jnp.concatenate([jnp.where(up, other, grad), jnp.where(up, grad, other)], 0)
    sib_grad = send(grad, SIBLING)

    grad, scaled, means, mixed = call(
        grad_kernel,
        [((CLASS_ROWS, tokens), BF), ((hidden_units, tokens), BF), ((EXTRA, LANE), F32), ((hidden_units, CLASS_ROWS), BF)],
        [(offs, SMEM), (grad, VMEM), (sib_grad, VMEM), (mix, VMEM), (slope, VMEM), (pre_act, VMEM), (gain_sum, VMEM), (hidden, VMEM)],
        flops=1e9, moved=8e6, name="hidden_grad",
    )
    mean_loss = (jnp.sum(grad[classes : classes + 2].astype(F32)) / tokens).reshape(1)

    own, sib = [None] * CHIPS, [None] * CHIPS
    height = rows + EXTRA
    for ids in ((4,), (3, 5), (2, 6), (1, 7, 0)):
        made = call(
            functools.partial(message_kernel, ids),
            [((height, tokens), F32), ((height, tokens), BF)] * len(ids),
            [(offs, SMEM), (w_gain_t, VMEM), (scaled, VMEM), (w_out, VMEM), (mixed, VMEM), (means, VMEM)],
            flops=4e8 * len(ids), moved=2e6, name="messages",
        )
        for n, d in enumerate(ids):
            own[d], sib[d] = made[2 * n], send(made[2 * n + 1], SIBLING)
    forth, back = scatter_walk(own, sib)

    (d_w_out,) = call(
        d_w_out_kernel, [((hidden_units, channels), F32)], [(mixed, VMEM), (head_pad, VMEM), (layer_scale[None, :], VMEM)],
        flops=2e9, moved=8e6, name="d_w_out",
    )
    (d_w_in,) = call(
        d_w_in_kernel,
        [((hidden_units, channels), F32)],
        [(offs, SMEM), (scaled, VMEM), (stats, VMEM), (norm_gain[None, :], VMEM)] + [(b, VMEM) for pair in pairs for b in pair],
        flops=2e9, moved=8e6, name="d_w_in",
    )
    mine = own[0] + sib[0].astype(F32)
    d_features, d_dw, d_scale, d_head = call(
        functools.partial(last_kernel, classes),
        [((rows, tokens), F32), ((rows, KS * KS), F32), ((rows, 1), F32), ((rows, classes), F32)],
        [(a, VMEM) for a in (mine, forth, back, features, conv_out, stats, dw_weight, my_head, my_scale, grad)],
        [grid_shape, copies_shape, taps_shape, copies_shape, pltpu.VMEM((KS * KS, 8, LANE), F32)], name="conv_backward",
    )
    return (d_features, d_dw, d_scale[:, 0], d_w_in, d_w_out, d_head, mean_loss)


def conv_apply(in_grid, kernel):
    half = KS // 2
    padded = jnp.pad(in_grid, ((0, 0), (half, half), (half, half)))
    running = jnp.zeros(in_grid.shape, in_grid.dtype)
    for row_shift in range(KS):
        for col_shift in range(KS):
            tap = kernel[:, row_shift * KS + col_shift]
            running = (
                running
                + tap[:, None, None]
                * padded[:, row_shift : row_shift + WIN_H, col_shift : col_shift + WIN_W]
            )
    return running


def gelu_parts(values):
    cum_prob = 0.5 * (1.0 + lax.erf(values * 0.7071067811865476))
    density = jnp.exp(-0.5 * values * values) * 0.3989422804014327
    return (values * cum_prob, cum_prob + values * density)


def plain_device(features, dw_weight, norm_gain, layer_scale, w_in, w_out, w_head, labels):
    highest = lax.Precision.HIGHEST
    my_rows = features.shape[0]
    tok_count = features.shape[1]
    class_count = w_head.shape[1]
    row_offset = lax.axis_index("ch") * my_rows
    inputs_wide = features.astype(jnp.float32)
    in_grid = inputs_wide.reshape(my_rows, WIN_H, WIN_W)
    conv_out = conv_apply(in_grid, dw_weight).reshape(my_rows, tok_count).astype(jnp.bfloat16)
    conv_all = lax.all_gather(conv_out, "ch", axis=0, tiled=True)
    conv_wide = conv_all.astype(jnp.float32)
    tok_mean = jnp.mean(conv_wide, axis=0)
    centered = conv_wide - tok_mean[None, :]
    tok_var = jnp.mean(centered * centered, axis=0)
    inv_std = 1.0 / jnp.sqrt(tok_var + norm_eps)
    normed = centered * inv_std[None, :]
    norm_out = (norm_gain[:, None] * normed).astype(jnp.bfloat16)
    pre_act = jnp.dot(w_in, norm_out, preferred_element_type=jnp.float32)
    gelu_out, gelu_slope = gelu_parts(pre_act)
    hidden = gelu_out.astype(jnp.bfloat16)
    my_scale = lax.dynamic_slice_in_dim(layer_scale, row_offset, my_rows, 0)
    head_wide = w_head.astype(jnp.float32)
    my_head = lax.dynamic_slice_in_dim(head_wide, row_offset, my_rows, 0)
    w_cols = w_out
    branch_sum = lax.psum_scatter(
        lax.dot_general(
            w_cols, hidden, (((0,), (0,)), ((), ())), preferred_element_type=jnp.float32
        ),
        "ch",
        scatter_dimension=0,
        tiled=True,
    )
    block_out = inputs_wide + my_scale[:, None] * branch_sum
    part_logits = lax.dot_general(block_out, my_head, (((0,), (0,)), ((), ())), precision=highest)
    logits = lax.psum(part_logits, "ch")
    row_max = jnp.max(logits, axis=1, keepdims=True)
    exp_terms = jnp.exp(logits - row_max)
    exp_total = jnp.sum(exp_terms, axis=1, keepdims=True)
    log_total = jnp.log(exp_total) + row_max
    onehot = (labels[:, None] == jnp.arange(class_count, dtype=jnp.int32)[None, :]).astype(
        jnp.float32
    )
    picked = jnp.sum(logits * onehot, axis=1)
    mean_loss = jnp.mean(log_total[:, 0] - picked).reshape(1)
    logit_grad = exp_terms / exp_total - onehot
    out_grad = lax.dot_general(my_head, logit_grad, (((1,), (1,)), ((), ())), precision=highest)
    d_head = jnp.dot(block_out, logit_grad, precision=highest)
    d_scale = jnp.sum(out_grad * branch_sum, axis=1)
    branch_grad = (my_scale[:, None] * out_grad).astype(jnp.bfloat16)
    incoming = lax.all_gather(branch_grad, "ch", axis=0, tiled=True)
    hidden_acc = jnp.dot(w_cols, incoming, preferred_element_type=jnp.float32)
    tile_grad = lax.dot_general(
        hidden, incoming, (((1,), (1,)), ((), ())), preferred_element_type=jnp.float32
    )
    pre_grad = (hidden_acc * gelu_slope).astype(jnp.bfloat16)
    d_w_in = lax.dot_general(
        pre_grad, norm_out, (((1,), (1,)), ((), ())), preferred_element_type=jnp.float32
    )
    norm_grad = lax.dot_general(
        w_in, pre_grad, (((0,), (0,)), ((), ())), preferred_element_type=jnp.float32
    )
    gained = norm_gain[:, None] * norm_grad
    conv_term = (
        gained
        - jnp.mean(gained, axis=0)[None, :]
        - normed * jnp.mean(gained * normed, axis=0)[None, :]
    ) * inv_std[None, :]
    conv_grad = lax.psum_scatter(conv_term, "ch", scatter_dimension=0, tiled=True)
    unused, pullback = jax.vjp(conv_apply, in_grid, dw_weight)
    grid_grad, d_dw = pullback(conv_grad.reshape(my_rows, WIN_H, WIN_W))
    d_features = out_grad + grid_grad.reshape(my_rows, tok_count)
    return (d_features, d_dw, d_scale, d_w_in, tile_grad, d_head, mean_loss)


def solution(mesh):
    placed = (P("ch", "grp"), P("ch", None), P(), P(), P("ch", None), P("ch", None), P(), P("grp"))
    return jax.shard_map(
        per_device if mesh.shape["ch"] == 2 * CHIPS else plain_device,
        mesh=mesh,
        in_specs=placed,
        out_specs=(
            P("ch", "grp"),
            P("ch", "grp"),
            P(("grp", "ch")),
            P(("grp", "ch"), None),
            P(("grp", "ch"), None),
            P("ch", "grp"),
            P("grp"),
        ),
        check_vma=False,
    )
```

```python
import functools

import jax
import jax.numpy as jnp
import numpy as np
from jax import lax
from jax.experimental import pallas as pl
from jax.experimental.pallas import tpu as pltpu
from jax.sharding import PartitionSpec as P

KS = 7
HALF = KS // 2
WIN_H = 32
WIN_W = 32
norm_eps = 1e-06
BF = jnp.bfloat16
F32 = jnp.float32

WALK = (0, 2, 4, 6, 7, 5, 3, 1)
CHIPS = len(WALK)
CORES = 2
REL = np.array([[WALK[(WALK.index(chip) + d) % CHIPS] for d in range(CHIPS)] for chip in range(CHIPS)], np.int32)
PLACES = np.array(
    [
        [REL[dev // 2][d] * 2 + (dev % 2 ^ side) for d in range(CHIPS) for side in range(2)] + [dev % 2, dev]
        for dev in range(2 * CHIPS)
    ],
    np.int32,
)
CORE, MINE = 2 * CHIPS, 2 * CHIPS + 1
MARKS = np.broadcast_to(
    np.array([[dev >> bit & 1 for bit in range(8)] for dev in range(2 * CHIPS)], np.int32)[:, :, None], (2 * CHIPS, 8, 128)
)
CLASS_ROWS = 160
EXTRA = 24
SUB_ROWS = 16
LANE = 128


def walk_perm(step):
    return [
        (WALK[p] * 2 + c, WALK[(p + step) % CHIPS] * 2 + c) for p in range(CHIPS) for c in range(2)
    ]


def flip_perm(bit):
    return [(i, i ^ bit) for i in range(2 * CHIPS)]


def send(value, perm):
    return lax.ppermute(value, "ch", perm)


FORTH, BACK, SIBLING = walk_perm(1), walk_perm(-1), flip_perm(1)
VMEM = pl.BlockSpec(memory_space=pltpu.VMEM)
SMEM = pl.BlockSpec(memory_space=pltpu.SMEM)


def call(kernel, outs, ins, scratch=(), flops=0, moved=0, limit=40, name=None, after=(), out_spaces=None):
    count = len(ins)

    def body(*refs):
        kernel(*refs[:count], *refs[count + len(after) :])

    result = pl.pallas_call(
        body,
        out_shape=[jax.ShapeDtypeStruct(s, d) for s, d in outs],
        in_specs=[s for _, s in ins] + [pl.BlockSpec(memory_space=pl.ANY)] * len(after),
        out_specs=[pl.BlockSpec(memory_space=space) for space in out_spaces or [pltpu.VMEM] * len(outs)],
        scratch_shapes=list(scratch),
        compiler_params=pltpu.CompilerParams(vmem_limit_bytes=limit << 20),
        cost_estimate=pl.CostEstimate(flops=int(flops), bytes_accessed=int(moved), transcendentals=0),
        name=name,
    )(*[a for a, _ in ins], *after)
    return result


def dot(a, b, dims):
    return lax.dot_general(a, b, (dims, ((), ())), preferred_element_type=F32)


def shifted_copies(grid_pad, copies):
    for j in range(KS):
        copies[j] = grid_pad[:, pl.ds(8 + j - HALF, WIN_W), :]


def clear_border(grid_pad):
    grid_pad[...] = jnp.zeros_like(grid_pad)


def put_rows(grid_pad, row, tile):
    grid_pad[pl.ds(row + HALF, 4), pl.ds(8, WIN_W), :] = tile.T.reshape(4, WIN_W, tile.shape[0])


def conv_rows(copies, taps, row, flip):
    acc = None
    for j in range(KS):
        for i in range(KS):
            index = (KS - 1 - i) * KS + KS - 1 - j if flip else i * KS + j
            term = taps[index : index + 1, :][None] * copies[j, pl.ds(row + i, 4)]
            acc = term if acc is None else acc + term
    return acc


def conv_kernel(x_ref, taps, out_ref, grid_pad, copies):
    clear_border(grid_pad)
    for g in range(8):
        put_rows(grid_pad, 4 * g, x_ref[:, g * LANE : (g + 1) * LANE].astype(F32))
    shifted_copies(grid_pad, copies)
    for g in range(8):
        acc = conv_rows(copies, taps, 4 * g, False)
        out_ref[:, g * LANE : (g + 1) * LANE] = acc.reshape(LANE, LANE).T.astype(BF)


def copies_kernel(x_ref, copies, grid_pad):
    clear_border(grid_pad)
    for g in range(8):
        put_rows(grid_pad, 4 * g, x_ref[:, g * LANE : (g + 1) * LANE].astype(F32))
    shifted_copies(grid_pad, copies)


def columns(places_ref, entry):
    return pl.ds(pl.multiple_of(places_ref[entry] * LANE, LANE), LANE)


def weights_kernel(places_ref, w_in_ref, gain_ref, own_ref, sib_ref, gain_sum_ref):
    total = None
    for d in range(CHIPS):
        for side, out in enumerate((own_ref, sib_ref)):
            at = columns(places_ref, 2 * d + side)
            part = (w_in_ref[:, at].astype(F32) * gain_ref[:, at]).astype(BF)
            out[:, d * LANE : (d + 1) * LANE] = part
            wide = part.astype(F32)
            total = wide if total is None else total + wide
    gain_sum_ref[...] = jnp.sum(total, axis=1, keepdims=True)


def mix_kernel(w_out_ref, scale_ref, head_ref, head_pad_ref, mix_ref):
    head_pad_ref[...] = jnp.zeros_like(head_pad_ref)
    head_pad_ref[0 : head_ref.shape[0], :] = head_ref[...]
    head = head_pad_ref[...]
    scaled = (head.astype(F32) * scale_ref[...]).astype(BF)
    mix_ref[...] = dot(w_out_ref[...], scaled, ((1,), (1,))).astype(BF)


def turn_kernel(own_ref, sib_ref, out_ref):
    units = own_ref.shape[0]
    out_ref[:, :units] = own_ref[...].T
    out_ref[:, units:] = sib_ref[...].T


def add_blocks(own_ref, sib_ref, held, ids, shift, sums):
    away = held.astype(F32) - shift
    first = jnp.sum(away, axis=0, keepdims=True)
    second = jnp.sum(away * away, axis=0, keepdims=True)
    if sums is not None:
        first, second = sums[0] + first, sums[1] + second
    pick = lambda ref: jnp.concatenate([ref[:, d * LANE : (d + 1) * LANE] for d in ids], axis=1)
    return dot(pick(own_ref), held, ((1,), (0,))), dot(pick(sib_ref), held, ((1,), (0,))), first, second


def first_kernel(ids, own_ref, sib_ref, *refs):
    blocks, (acc_ref, give_ref, sums_ref) = refs[:-3], refs[-3:]
    shift = jnp.mean(blocks[0][...].astype(F32), axis=0, keepdims=True)
    held = jnp.concatenate([b[...] for b in blocks], axis=0)
    acc, give, first, second = add_blocks(own_ref, sib_ref, held, ids, shift, None)
    acc_ref[...] = acc
    give_ref[...] = give
    sums_ref[...] = jnp.concatenate([shift, first, second, jnp.zeros((5, shift.shape[1]), F32)], axis=0)


def next_kernel(ids, own_ref, sib_ref, acc_in_ref, give_in_ref, sums_in_ref, *refs):
    blocks, (acc_ref, give_ref, sums_ref) = refs[:-3], refs[-3:]
    shift, first, second = sums_in_ref[0:1, :], sums_in_ref[1:2, :], sums_in_ref[2:3, :]
    held = jnp.concatenate([b[...] for b in blocks], axis=0)
    acc, give, first, second = add_blocks(own_ref, sib_ref, held, ids, shift, (first, second))
    acc_ref[...] = acc_in_ref[...] + acc
    give_ref[...] = (give_in_ref[...] + give).astype(give_ref.dtype)
    sums_ref[...] = jnp.concatenate([shift, first, second, jnp.zeros((5, shift.shape[1]), F32)], axis=0)


def pack_kernel(*refs):
    refs[-1][...] = jnp.concatenate([ref[...] for ref in refs[:-1]], axis=0)


def forward_kernel(places_ref, acc_ref, got_ref, sums_ref, sib_sums_ref, gain_sum_ref, mix_ref, head_ref, x_ref, own_ref, sib_ref, *refs):
    blocks, (pre_ref, hidden_ref, stats_ref, keep_ref, give_ref, scratch) = refs[:-6], refs[-6:]
    held = jnp.concatenate([b[...] for b in blocks], axis=0)
    at = slice(CHIPS // 2 * LANE, (CHIPS // 2 + 1) * LANE)
    acc = dot(jnp.concatenate([own_ref[:, at], sib_ref[:, at]], axis=1), held, ((1,), (0,)))
    shift = sums_ref[0:1, :]
    away = held.astype(F32) - shift
    sets = [(held.shape[0], shift, jnp.sum(away, axis=0, keepdims=True), jnp.sum(away * away, axis=0, keepdims=True))]
    sets += [((CHIPS - 1) * LANE, ref[0:1, :], ref[1:2, :], ref[2:3, :]) for ref in (sums_ref, sib_sums_ref)]
    means = [base + first / count for count, base, first, _ in sets]
    channels = 2 * CHIPS * LANE
    tok_mean = sum(s[0] * mean for s, mean in zip(sets, means)) / channels
    spread = sum(second - first * first / count + count * (mean - tok_mean) ** 2 for (count, _, first, second), mean in zip(sets, means))
    inv_std = lax.rsqrt(spread / channels + norm_eps)
    stats_ref[...] = jnp.concatenate([tok_mean, inv_std, jnp.zeros((6, tok_mean.shape[1]), F32)], axis=0)
    pre_act = (acc + acc_ref[...] + got_ref[...].astype(F32) - gain_sum_ref[...] * tok_mean) * inv_std
    pre_ref[...] = pre_act
    hidden = (pre_act * (0.5 * (1.0 + lax.erf(pre_act * 0.7071067811865476)))).astype(BF)
    hidden_ref[...] = hidden
    my_head = head_ref[:, columns(places_ref, MINE)]
    logits = dot(mix_ref[...], hidden, ((0,), (0,))) + dot(my_head, x_ref[...], ((1,), (0,)))
    core = places_ref[CORE]
    chunks = keep_ref.shape[0]
    for g in range(2 * chunks):
        scratch[g] = logits[:, g * LANE : (g + 1) * LANE]
    keep_ref[...] = scratch[pl.ds(chunks * core, chunks)]
    give_ref[...] = scratch[pl.ds(chunks - chunks * core, chunks)]


def slope_kernel(pre_ref, stats_ref, slope_ref):
    pre_act = pre_ref[...]
    cum_prob = 0.5 * (1.0 + lax.erf(pre_act * 0.7071067811865476))
    density = jnp.exp(-0.5 * pre_act * pre_act) * 0.3989422804014327
    slope_ref[...] = (cum_prob + pre_act * density) * stats_ref[1:2, :]


def fold_kernel(row, marks_ref, keep_ref, got_ref, kept_ref, give_ref):
    bit = jnp.broadcast_to(marks_ref[row : row + 1, :], kept_ref.shape[-2:]) == 1
    half = keep_ref.shape[0] // 2
    for g in range(half):
        low, high = keep_ref[g] + got_ref[g], keep_ref[half + g] + got_ref[half + g]
        kept_ref[g] = jnp.where(bit, high, low)
        give_ref[g] = jnp.where(bit, low, high)


def add_kernel(a_ref, b_ref, out_ref):
    out_ref[...] = a_ref[...] + b_ref[...]


def softmax_kernel(classes, marks_ref, kept_ref, got_ref, labels_ref, grad_ref):
    kept = kept_ref[0] + got_ref[0]
    chunk = 4 * marks_ref[0:1, :] + 2 * marks_ref[1:2, :] + marks_ref[2:3, :]
    labels = labels_ref[:, :LANE]
    for g in range(1, labels_ref.shape[1] // LANE):
        labels = jnp.where(chunk == g, labels_ref[:, g * LANE : (g + 1) * LANE], labels)
    class_id = lax.broadcasted_iota(jnp.int32, kept.shape, 0)
    kept = jnp.where(class_id < classes, kept, -jnp.inf)
    col_max = jnp.max(kept, axis=0, keepdims=True)
    exp_terms = jnp.exp(kept - col_max)
    exp_total = jnp.sum(exp_terms, axis=0, keepdims=True)
    onehot = class_id == labels
    picked = jnp.sum(jnp.where(onehot, kept, 0.0), axis=0, keepdims=True)
    loss = jnp.log(exp_total) + col_max - picked
    loss_high = loss.astype(BF).astype(F32)
    grad = exp_terms / exp_total - onehot.astype(F32)
    grad = jnp.where(class_id == classes, loss_high, jnp.where(class_id == classes + 1, loss - loss_high, grad))
    grad_ref[0] = grad.astype(BF)


def join_kernel(row, marks_ref, own_ref, other_ref, out_ref):
    bit = jnp.broadcast_to(marks_ref[row : row + 1, :], own_ref.shape[1:]) == 1
    half = own_ref.shape[0]
    for g in range(half):
        own, other = own_ref[g].astype(F32), other_ref[g].astype(F32)
        out_ref[g] = jnp.where(bit, other, own).astype(BF)
        out_ref[half + g] = jnp.where(bit, own, other).astype(BF)


def grad_kernel(places_ref, own_ref, sib_ref, mix_ref, slope_ref, pre_ref, gain_sum_ref, grad_ref, scaled_ref, means_ref):
    core = places_ref[CORE]
    chunks = own_ref.shape[0]
    for g in range(chunks):
        grad_ref[:, pl.ds(pl.multiple_of((core * chunks + g) * LANE, LANE), LANE)] = own_ref[g]
        grad_ref[:, pl.ds(pl.multiple_of(((1 - core) * chunks + g) * LANE, LANE), LANE)] = sib_ref[g]
    scaled = (dot(mix_ref[...], grad_ref[...], ((1,), (0,))) * slope_ref[...]).astype(BF)
    scaled_ref[...] = scaled
    wide = scaled.astype(F32)
    mean_part = jnp.sum(wide * gain_sum_ref[...], axis=0, keepdims=True)
    proj_part = jnp.sum(wide * pre_ref[...], axis=0, keepdims=True)
    means_ref[...] = jnp.concatenate([mean_part, proj_part, jnp.zeros((SUB_ROWS - 2, wide.shape[1]), F32)], axis=0)


def branch_kernel(places_ref, hidden_ref, grad_ref, w_out_ref, means_ref, mixed_ref, keep_ref, give_ref):
    mixed = dot(hidden_ref[...], grad_ref[...], ((1,), (1,))).astype(BF)
    mixed_ref[...] = mixed
    for side, out in enumerate((keep_ref, give_ref)):
        cols = jnp.concatenate([w_out_ref[:, columns(places_ref, 2 * d + side)] for d in range(CHIPS)], axis=1)
        both = jnp.concatenate([dot(mixed, cols, ((0,), (0,))), means_ref[...]], axis=0)
        out[...] = both.astype(out.dtype)


def message_of(d, turned_ref, own_ref, got_ref, keep_ref, sib_ref):
    units = own_ref.shape[0]
    at = slice(d * LANE, (d + 1) * LANE)
    rows = dot(turned_ref[at, :units], own_ref[...], ((1,), (0,))) + dot(turned_ref[at, units:], got_ref[...], ((1,), (0,)))
    means = keep_ref[CLASS_ROWS:, :] + sib_ref[CLASS_ROWS:, :].astype(F32)
    means = [means[n : n + 1, g * LANE : (g + 1) * LANE] for n in range(2) for g in range(8)]
    means = jnp.concatenate(means + [jnp.zeros((EXTRA - 16, LANE), F32)], axis=0)
    branch = keep_ref[:CLASS_ROWS, at] + sib_ref[:CLASS_ROWS, at].astype(F32)
    branch = jnp.concatenate([branch, jnp.zeros((7 * EXTRA - CLASS_ROWS, LANE), F32)], axis=0)
    extra = jnp.concatenate([branch[g * EXTRA : (g + 1) * EXTRA] for g in range(7)] + [means], axis=1)
    return jnp.concatenate([rows, extra], axis=0)


def message_kernel(ids, *refs):
    for d, out in zip(ids, refs[-len(ids) :]):
        out[...] = message_of(d, *refs[: -len(ids)])


def far_kernel(*refs):
    upper, lower = refs[-2:]
    cut = upper.shape[0]
    total = message_of(CHIPS // 2, *refs[:-2])
    upper[...] = total[:cut].astype(BF)
    lower[...] = total[cut:].astype(BF)


def sum_kernel(ahead, behind, forth, back, ahead_out, behind_out):
    ahead, behind = ahead[...], behind[...]
    height, cut = ahead.shape[0], forth.shape[0]
    if cut < height:
        ahead_out[...] = jnp.concatenate([ahead[:cut] + forth[...].astype(F32), ahead[cut:]], axis=0).astype(BF)
        behind_out[...] = jnp.concatenate([behind[:cut], behind[cut:] + back[...].astype(F32)], axis=0).astype(BF)
    else:
        ahead_out[...] = (ahead + forth[...].astype(F32)).astype(BF)
        behind_out[...] = (behind + back[...].astype(F32)).astype(BF)


def d_w_out_kernel(mixed_ref, head_ref, scale_ref, out_ref, done_ref, held, sems):
    done_ref[...] = jnp.zeros_like(done_ref)
    mixed = mixed_ref[...]
    copies = []
    for n in range(sems.shape[0]):
        at = slice(n * held.shape[1] // sems.shape[0], (n + 1) * held.shape[1] // sems.shape[0])
        held[:, at] = dot(mixed, head_ref[:, at], ((1,), (0,))) * scale_ref[:, at]
        copies.append(pltpu.make_async_copy(held.at[:, at], out_ref.at[:, at], sems.at[n]))
        copies[-1].start()
    for copy in copies:
        copy.wait()


def d_w_in_kernel(places_ref, gain_ref, scaled_ref, stats_ref, own_ref, sib_ref, out_ref, done_ref, held, sems):
    done_ref[...] = jnp.zeros_like(done_ref)
    scaled = scaled_ref[...]
    shift = jnp.sum(scaled.astype(F32) * stats_ref[0:1, :], axis=1, keepdims=True)
    copies = []
    for side, blocks in enumerate((own_ref, sib_ref)):
        for n in range(0, CHIPS, 2):
            both = dot(scaled, blocks[n * LANE : (n + 2) * LANE, :], ((1,), (1,))) - shift
            for k in range(2):
                at = columns(places_ref, 2 * (n + k) + side)
                slot = len(copies)
                held[slot] = both[:, k * LANE : (k + 1) * LANE] * gain_ref[:, at]
                copies.append(pltpu.make_async_copy(held.at[slot], out_ref.at[:, at], sems.at[slot]))
                copies[-1].start()
    for copy in copies:
        copy.wait()


def head_kernel(classes, places_ref, x_ref, head_ref, grad_ref, out_grad_ref, d_head_ref, loss_ref):
    my_head = head_ref[:, columns(places_ref, MINE)]
    grad = grad_ref[...]
    out_grad_ref[...] = dot(my_head, grad, ((0,), (0,)))
    d_head_ref[...] = dot(grad, x_ref[...], ((1,), (1,)))
    loss_ref[...] = (jnp.sum(grad[classes : classes + 2].astype(F32)) / grad.shape[1]).reshape(1, 1)


def last_kernel(classes, places_ref, mine_ref, forth_ref, back_ref, conv_ref, stats_ref, taps, copies_x, out_grad_ref, head_grad_ref, head_ref, scale_ref,
                d_x_ref, d_dw_ref, d_scale_ref, d_head_ref, grid_pad, copies, sums):
    rows = conv_ref.shape[0]
    channels = rows * 2 * CHIPS
    got = mine_ref[...] + forth_ref[...].astype(F32) + back_ref[...].astype(F32)
    extra = got[rows:]
    branch = jnp.concatenate([extra[:, g * LANE : (g + 1) * LANE] for g in range(7)], axis=0)[:CLASS_ROWS]
    means = extra[:, 7 * LANE :]
    clear_border(grid_pad)
    for g in range(8):
        at = slice(g * LANE, (g + 1) * LANE)
        normed = (conv_ref[:, at].astype(F32) - stats_ref[0:1, at]) * stats_ref[1:2, at]
        conv_grad = got[:rows, at] - (means[g : g + 1, :] + normed * means[8 + g : 9 + g, :]) * (1.0 / channels)
        put_rows(grid_pad, 4 * g, conv_grad)
    shifted_copies(grid_pad, copies)
    for g in range(8):
        at = slice(g * LANE, (g + 1) * LANE)
        d_x_ref[:, at] = out_grad_ref[:, at] + conv_rows(copies, taps, 4 * g, True).reshape(LANE, LANE).T
    for g in range(8):
        conv_grad = copies[HALF, pl.ds(4 * g + HALF, 4)]
        for j in range(KS):
            for i in range(KS):
                prod = (conv_grad * copies_x[j, pl.ds(4 * g + i, 4)]).reshape(16, 8, LANE)
                total = jnp.sum(prod, axis=0)
                index = i * KS + j
                if g == 0:
                    sums[index] = total
                else:
                    sums[index] += total
    d_dw_ref[...] = jnp.sum(sums[...], axis=1)
    at = columns(places_ref, MINE)
    d_scale_ref[...] = jnp.sum(head_ref[:, at].astype(F32) * branch, axis=0, keepdims=True)
    d_head_ref[...] = (head_grad_ref[...] + scale_ref[:, at] * branch)[:classes]


def walk_step(walk, step):
    forth, back = walk[(1 - step) % CHIPS][0], walk[step - 1][0]
    half = forth.shape[0] // 2
    if step < CHIPS // 2:
        walk[(-step) % CHIPS], walk[step] = (send(forth, FORTH),), (send(back, BACK),)
    else:
        walk[step] = (send(forth[:half], FORTH), send(back[half:], BACK))


def hold(walk, step, *others):
    spots = [((-step) % CHIPS), step]
    held = lax.optimization_barrier((walk[spots[0]][0], walk[spots[1]][0], *others))
    walk[spots[0]], walk[spots[1]] = (held[0],), (held[1],)
    return held[2:]


def per_device(features, dw_weight, norm_gain, layer_scale, w_in, w_out, w_head, labels):
    rows, tokens = features.shape
    units, channels = w_in.shape
    classes = w_head.shape[1]
    me = lax.axis_index("ch")
    places = lax.dynamic_index_in_dim(jnp.asarray(PLACES), me, 0, keepdims=False)
    marks = lax.dynamic_index_in_dim(jnp.asarray(MARKS), me, 0, keepdims=False)
    taps = dw_weight.T
    scale_row, gain_row, labels_row = layer_scale[None, :], norm_gain[None, :], labels[None, :]
    grid_shape = pltpu.VMEM((WIN_H + 2 * HALF, WIN_W + 16, LANE), F32)
    copies_size = (KS, WIN_H + 2 * HALF, WIN_W, LANE)
    half_channels = CHIPS * rows
    vm = lambda *arrays: [(a, VMEM) for a in arrays]
    spot, mark = [(places, SMEM)], vm(marks)
    f32s, bf16s, sums_size = ((units, tokens), F32), ((units, tokens), BF), ((8, tokens), F32)

    (conv_out,) = call(
        conv_kernel, [((rows, tokens), BF)], vm(features, taps), [grid_shape, pltpu.VMEM(copies_size, F32)], limit=12, name="conv_forward",
        after=[places, marks],
    )
    walk = {0: (conv_out,)}
    walk_step(walk, 1)
    w_own, w_give, gain_sum = call(
        weights_kernel,
        [((units, half_channels), BF), ((units, half_channels), BF), ((units, 1), F32)],
        spot + vm(w_in, gain_row), flops=4e8, moved=4e6, limit=12, name="weights_ready", after=[conv_out],
    )
    w_own, w_give, gain_sum = hold(walk, 1, w_own, w_give, gain_sum)
    w_sib = send(w_give, SIBLING)
    walk_step(walk, 2)
    so_far = call(
        functools.partial(first_kernel, (0, 1, 7)), [f32s, f32s, sums_size],
        vm(w_own, w_sib, *walk[0], *walk[1], *walk[7]), flops=1e9, moved=4e6, limit=16, name="forward_first",
    )
    so_far = hold(walk, 2, *so_far)
    walk_step(walk, 3)
    head_pad, mix = call(
        mix_kernel,
        [((CLASS_ROWS, channels), BF), ((units, CLASS_ROWS), BF)],
        vm(w_out, scale_row, w_head.T), flops=1e9, moved=4e6, limit=12, name="mix_ready", after=[so_far[2]],
    )
    so_far = call(
        functools.partial(next_kernel, (2, 6)), [f32s, f32s, sums_size],
        vm(w_own, w_sib, *so_far, *walk[2], *walk[6]), flops=6e8, moved=4e6, limit=16, name="forward_next",
    )
    *so_far, head_pad, mix = hold(walk, 3, *so_far, head_pad, mix)
    walk_step(walk, 4)
    acc, give, sums = call(
        functools.partial(next_kernel, (3, 5)), [f32s, bf16s, sums_size],
        vm(w_own, w_sib, *so_far, *walk[3], *walk[5]), flops=6e8, moved=4e6, limit=16, name="forward_next",
    )
    got, sib_sums = send(give, SIBLING), send(sums, SIBLING)
    far = [*walk[4], *[send(b, SIBLING) for b in walk[4]]]
    chunks = tokens // LANE // 2
    chunk = lambda count, kind=F32: ((count, CLASS_ROWS, LANE), kind)
    pre_act, hidden, stats, keep, give = call(
        forward_kernel, [f32s, bf16s, sums_size, chunk(chunks), chunk(chunks)],
        spot + vm(acc, got, sums, sib_sums, gain_sum, mix, head_pad, features, w_own, w_give, *far),
        [pltpu.VMEM((2 * chunks, CLASS_ROWS, LANE), F32)], flops=1e9, moved=4e6, limit=16, name="forward_hidden",
    )

    kept, give = call(functools.partial(fold_kernel, 1), [chunk(2), chunk(2)], mark + vm(keep, send(give, SIBLING)), limit=4, name="fold_core")
    (packed,) = call(
        pack_kernel, [((half_channels, tokens), BF)], vm(*[b for d in range(CHIPS) for b in walk[d]]), flops=4e8, moved=4e6, limit=10, name="pack_blocks", after=[kept],
    )
    sib_packed = send(packed, SIBLING)
    kept, give = call(functools.partial(fold_kernel, 2), [chunk(1), chunk(1)], mark + vm(kept, send(give, flip_perm(2))), limit=4, name="fold_y", after=[packed])
    (slope,) = call(slope_kernel, [f32s], vm(pre_act, stats), flops=5e8, moved=4e6, limit=8, name="gelu_slope", after=[kept])
    (kept,) = call(add_kernel, [chunk(1)], vm(kept, send(give, flip_perm(4))), limit=4, name="fold_z", after=[slope])
    (turned,) = call(turn_kernel, [((half_channels, 2 * units), BF)], vm(w_own, w_sib), flops=4e8, moved=4e6, limit=10, name="weights_turned", after=[kept])
    (grad,) = call(
        functools.partial(softmax_kernel, classes), [chunk(1, BF)], mark + vm(kept, send(kept, flip_perm(8)), labels_row), limit=4, name="class_grad", after=[turned, sib_packed],
    )
    (copies_x,) = call(copies_kernel, [(copies_size, F32)], vm(features), [grid_shape], flops=4e8, moved=4e6, limit=12, name="window_copies", after=[grad])
    (grad,) = call(functools.partial(join_kernel, 2), [chunk(2, BF)], mark + vm(grad, send(grad, flip_perm(4))), limit=4, name="join_z", after=[copies_x])
    (grad,) = call(functools.partial(join_kernel, 1), [chunk(4, BF)], mark + vm(grad, send(grad, flip_perm(2))), limit=4, name="join_y")

    grad, scaled, means = call(
        grad_kernel, [((CLASS_ROWS, tokens), BF), bf16s, ((SUB_ROWS, tokens), F32)],
        spot + vm(grad, send(grad, SIBLING), mix, slope, pre_act, gain_sum), flops=6e8, moved=4e6, limit=12, name="hidden_grad",
    )
    got = send(scaled, SIBLING)
    extra_rows = CLASS_ROWS + SUB_ROWS
    mixed, keep, give = call(
        branch_kernel, [((units, CLASS_ROWS), BF), ((extra_rows, half_channels), F32), ((extra_rows, half_channels), BF)],
        spot + vm(hidden, grad, w_out, means), flops=8e8, moved=4e6, limit=12, name="class_products",
    )
    sources = vm(turned, scaled, got, keep, send(give, SIBLING))
    height = rows + EXTRA
    cut = 80
    forth, back = call(far_kernel, [((cut, tokens), BF), ((height - cut, tokens), BF)], sources, flops=3e8, moved=2e6, limit=8, name="message_far")
    forth, back = send(forth, FORTH), send(back, BACK)
    d_w_out, d_w_out_done = call(
        d_w_out_kernel, [((units, channels), F32), ((8, LANE), F32)], vm(mixed, head_pad, scale_row),
        [pltpu.VMEM((units, channels), F32), pltpu.SemaphoreType.DMA((4,))], flops=1e9, moved=8e6, limit=12, name="d_w_out", out_spaces=(pl.ANY, pltpu.VMEM),
        after=[forth],
    )
    out_grad, head_grad, mean_loss = call(
        functools.partial(head_kernel, classes), [((rows, tokens), F32), ((CLASS_ROWS, rows), F32), ((1, 1), F32)],
        spot + vm(features, head_pad, grad), flops=4e8, moved=2e6, limit=8, name="class_head", after=[forth],
    )
    beside = {3: [], 2: [d_w_out_done, out_grad], 1: []}
    for step in range(CHIPS // 2 - 1, 0, -1):
        ahead, behind = call(
            functools.partial(message_kernel, (step, CHIPS - step)), [((height, tokens), F32)] * 2, sources,
            flops=6e8, moved=2e6, limit=8, name="messages",
        )
        forth, back = call(sum_kernel, [((height, tokens), BF)] * 2, vm(ahead, behind, forth, back), limit=6, name="walk_sum", after=beside[step])
        if step == 2:
            d_w_in, d_w_in_done = call(
                d_w_in_kernel, [((units, channels), F32), ((8, LANE), F32)], spot + vm(gain_row, scaled, stats, packed, sib_packed),
                [pltpu.VMEM((2 * CHIPS, units, LANE), F32), pltpu.SemaphoreType.DMA((2 * CHIPS,))],
                flops=2e9, moved=8e6, limit=12, name="d_w_in", out_spaces=(pl.ANY, pltpu.VMEM), after=[forth],
            )
            beside[1] = [d_w_in_done]
        forth, back = send(forth, FORTH), send(back, BACK)
    (mine,) = call(functools.partial(message_kernel, (0,)), [((height, tokens), F32)], sources, flops=3e8, moved=2e6, limit=8, name="messages", after=[ahead])
    d_features, d_dw, d_scale, d_head = call(
        functools.partial(last_kernel, classes),
        [((rows, tokens), F32), ((KS * KS, rows), F32), ((1, rows), F32), ((classes, rows), F32)],
        spot + vm(mine, forth, back, conv_out, stats, taps, copies_x, out_grad, head_grad, head_pad, scale_row),
        [grid_shape, pltpu.VMEM(copies_size, F32), pltpu.VMEM((KS * KS, 8, LANE), F32)], limit=16, name="conv_backward",
    )
    return (d_features, d_dw.T, d_scale[0], d_w_in, d_w_out, d_head.T, mean_loss[0])


def conv_apply(in_grid, kernel):
    half = KS // 2
    padded = jnp.pad(in_grid, ((0, 0), (half, half), (half, half)))
    running = jnp.zeros(in_grid.shape, in_grid.dtype)
    for row_shift in range(KS):
        for col_shift in range(KS):
            tap = kernel[:, row_shift * KS + col_shift]
            running = (
                running
                + tap[:, None, None]
                * padded[:, row_shift : row_shift + WIN_H, col_shift : col_shift + WIN_W]
            )
    return running


def gelu_parts(values):
    cum_prob = 0.5 * (1.0 + lax.erf(values * 0.7071067811865476))
    density = jnp.exp(-0.5 * values * values) * 0.3989422804014327
    return (values * cum_prob, cum_prob + values * density)


def plain_device(features, dw_weight, norm_gain, layer_scale, w_in, w_out, w_head, labels):
    highest = lax.Precision.HIGHEST
    my_rows = features.shape[0]
    tok_count = features.shape[1]
    class_count = w_head.shape[1]
    row_offset = lax.axis_index("ch") * my_rows
    inputs_wide = features.astype(jnp.float32)
    in_grid = inputs_wide.reshape(my_rows, WIN_H, WIN_W)
    conv_out = conv_apply(in_grid, dw_weight).reshape(my_rows, tok_count).astype(jnp.bfloat16)
    conv_all = lax.all_gather(conv_out, "ch", axis=0, tiled=True)
    conv_wide = conv_all.astype(jnp.float32)
    tok_mean = jnp.mean(conv_wide, axis=0)
    centered = conv_wide - tok_mean[None, :]
    tok_var = jnp.mean(centered * centered, axis=0)
    inv_std = 1.0 / jnp.sqrt(tok_var + norm_eps)
    normed = centered * inv_std[None, :]
    norm_out = (norm_gain[:, None] * normed).astype(jnp.bfloat16)
    pre_act = jnp.dot(w_in, norm_out, preferred_element_type=jnp.float32)
    gelu_out, gelu_slope = gelu_parts(pre_act)
    hidden = gelu_out.astype(jnp.bfloat16)
    my_scale = lax.dynamic_slice_in_dim(layer_scale, row_offset, my_rows, 0)
    head_wide = w_head.astype(jnp.float32)
    my_head = lax.dynamic_slice_in_dim(head_wide, row_offset, my_rows, 0)
    w_cols = w_out
    branch_sum = lax.psum_scatter(
        lax.dot_general(
            w_cols, hidden, (((0,), (0,)), ((), ())), preferred_element_type=jnp.float32
        ),
        "ch",
        scatter_dimension=0,
        tiled=True,
    )
    block_out = inputs_wide + my_scale[:, None] * branch_sum
    part_logits = lax.dot_general(block_out, my_head, (((0,), (0,)), ((), ())), precision=highest)
    logits = lax.psum(part_logits, "ch")
    row_max = jnp.max(logits, axis=1, keepdims=True)
    exp_terms = jnp.exp(logits - row_max)
    exp_total = jnp.sum(exp_terms, axis=1, keepdims=True)
    log_total = jnp.log(exp_total) + row_max
    onehot = (labels[:, None] == jnp.arange(class_count, dtype=jnp.int32)[None, :]).astype(
        jnp.float32
    )
    picked = jnp.sum(logits * onehot, axis=1)
    mean_loss = jnp.mean(log_total[:, 0] - picked).reshape(1)
    logit_grad = exp_terms / exp_total - onehot
    out_grad = lax.dot_general(my_head, logit_grad, (((1,), (1,)), ((), ())), precision=highest)
    d_head = jnp.dot(block_out, logit_grad, precision=highest)
    d_scale = jnp.sum(out_grad * branch_sum, axis=1)
    branch_grad = (my_scale[:, None] * out_grad).astype(jnp.bfloat16)
    incoming = lax.all_gather(branch_grad, "ch", axis=0, tiled=True)
    hidden_acc = jnp.dot(w_cols, incoming, preferred_element_type=jnp.float32)
    tile_grad = lax.dot_general(
        hidden, incoming, (((1,), (1,)), ((), ())), preferred_element_type=jnp.float32
    )
    pre_grad = (hidden_acc * gelu_slope).astype(jnp.bfloat16)
    d_w_in = lax.dot_general(
        pre_grad, norm_out, (((1,), (1,)), ((), ())), preferred_element_type=jnp.float32
    )
    norm_grad = lax.dot_general(
        w_in, pre_grad, (((0,), (0,)), ((), ())), preferred_element_type=jnp.float32
    )
    gained = norm_gain[:, None] * norm_grad
    conv_term = (
        gained
        - jnp.mean(gained, axis=0)[None, :]
        - normed * jnp.mean(gained * normed, axis=0)[None, :]
    ) * inv_std[None, :]
    conv_grad = lax.psum_scatter(conv_term, "ch", scatter_dimension=0, tiled=True)
    unused, pullback = jax.vjp(conv_apply, in_grid, dw_weight)
    grid_grad, d_dw = pullback(conv_grad.reshape(my_rows, WIN_H, WIN_W))
    d_features = out_grad + grid_grad.reshape(my_rows, tok_count)
    return (d_features, d_dw, d_scale, d_w_in, tile_grad, d_head, mean_loss)


def solution(mesh):
    placed = (P("ch", "grp"), P("ch", None), P(), P(), P("ch", None), P("ch", None), P(), P("grp"))
    return jax.shard_map(
        per_device if mesh.shape["ch"] == 2 * CHIPS else plain_device,
        mesh=mesh,
        in_specs=placed,
        out_specs=(
            P("ch", "grp"),
            P("ch", "grp"),
            P(("grp", "ch")),
            P(("grp", "ch"), None),
            P(("grp", "ch"), None),
            P("ch", "grp"),
            P("grp"),
        ),
        check_vma=False,
    )
```

```python
import functools

import jax
import jax.numpy as jnp
import numpy as np
from jax import lax
from jax.experimental import pallas as pl
from jax.experimental.pallas import tpu as pltpu
from jax.sharding import PartitionSpec as P

KS = 7
HALF = KS // 2
WIN_H = 32
WIN_W = 32
norm_eps = 1e-06
BF = jnp.bfloat16
F32 = jnp.float32

WALK = (0, 2, 4, 6, 7, 5, 3, 1)
CHIPS = len(WALK)
CORES = 2
REL = np.array([[WALK[(WALK.index(chip) + d) % CHIPS] for d in range(CHIPS)] for chip in range(CHIPS)], np.int32)
PLACES = np.array(
    [
        [REL[dev // 2][d] * 2 + (dev % 2 ^ side) for d in range(CHIPS) for side in range(2)] + [dev % 2, dev]
        for dev in range(2 * CHIPS)
    ],
    np.int32,
)
CORE, MINE = 2 * CHIPS, 2 * CHIPS + 1
MARKS = np.broadcast_to(
    np.array([[dev >> bit & 1 for bit in range(8)] for dev in range(2 * CHIPS)], np.int32)[:, :, None], (2 * CHIPS, 8, 128)
)
CLASS_ROWS = 160
EXTRA = 24
SUB_ROWS = 16
LANE = 128


def walk_perm(step):
    return [
        (WALK[p] * 2 + c, WALK[(p + step) % CHIPS] * 2 + c) for p in range(CHIPS) for c in range(2)
    ]


def flip_perm(bit):
    return [(i, i ^ bit) for i in range(2 * CHIPS)]


def send(value, perm):
    return lax.ppermute(value, "ch", perm)


FORTH, BACK, SIBLING = walk_perm(1), walk_perm(-1), flip_perm(1)
VMEM = pl.BlockSpec(memory_space=pltpu.VMEM)
SMEM = pl.BlockSpec(memory_space=pltpu.SMEM)
HBM = pl.BlockSpec(memory_space=pltpu.HBM)


def call(kernel, outs, ins, scratch=(), flops=0, moved=0, limit=40, name=None, after=(), out_spaces=None):
    count = len(ins)

    def body(*refs):
        kernel(*refs[:count], *refs[count + len(after) :])

    result = pl.pallas_call(
        body,
        out_shape=[jax.ShapeDtypeStruct(s, d) for s, d in outs],
        in_specs=[s for _, s in ins] + [pl.BlockSpec(memory_space=pl.ANY)] * len(after),
        out_specs=[pl.BlockSpec(memory_space=space) for space in out_spaces or [pltpu.VMEM] * len(outs)],
        scratch_shapes=list(scratch),
        compiler_params=pltpu.CompilerParams(vmem_limit_bytes=limit << 20),
        cost_estimate=pl.CostEstimate(flops=int(flops), bytes_accessed=int(moved), transcendentals=0),
        name=name,
    )(*[a for a, _ in ins], *after)
    return result


def dot(a, b, dims):
    return lax.dot_general(a, b, (dims, ((), ())), preferred_element_type=F32)


def shifted_copies(grid_pad, copies):
    for j in range(KS):
        copies[j] = grid_pad[:, pl.ds(8 + j - HALF, WIN_W), :]


def clear_border(grid_pad):
    grid_pad[...] = jnp.zeros_like(grid_pad)


def put_rows(grid_pad, row, tile):
    grid_pad[pl.ds(row + HALF, 4), pl.ds(8, WIN_W), :] = tile.T.reshape(4, WIN_W, tile.shape[0])


def conv_rows(copies, taps, row, flip):
    acc = None
    for j in range(KS):
        for i in range(KS):
            index = (KS - 1 - i) * KS + KS - 1 - j if flip else i * KS + j
            term = taps[index : index + 1, :][None] * copies[j, pl.ds(row + i, 4)]
            acc = term if acc is None else acc + term
    return acc


def conv_kernel(x_hbm, taps_hbm, out_ref, x_ref, taps, grid_pad, copies, sems):
    fetches = [pltpu.make_async_copy(x_hbm, x_ref, sems.at[0]), pltpu.make_async_copy(taps_hbm, taps, sems.at[1])]
    for fetch in fetches:
        fetch.start()
    clear_border(grid_pad)
    for fetch in fetches:
        fetch.wait()
    for g in range(8):
        put_rows(grid_pad, 4 * g, x_ref[:, g * LANE : (g + 1) * LANE].astype(F32))
    shifted_copies(grid_pad, copies)
    for g in range(8):
        acc = conv_rows(copies, taps, 4 * g, False)
        out_ref[:, g * LANE : (g + 1) * LANE] = acc.reshape(LANE, LANE).T.astype(BF)


def copies_kernel(x_ref, copies, grid_pad):
    clear_border(grid_pad)
    for g in range(8):
        put_rows(grid_pad, 4 * g, x_ref[:, g * LANE : (g + 1) * LANE].astype(F32))
    shifted_copies(grid_pad, copies)


def columns(places_ref, entry):
    return pl.ds(pl.multiple_of(places_ref[entry] * LANE, LANE), LANE)


def weights_kernel(places_ref, w_in_ref, gain_ref, own_ref, sib_ref, gain_sum_ref):
    total = None
    for d in range(CHIPS):
        for side, out in enumerate((own_ref, sib_ref)):
            at = columns(places_ref, 2 * d + side)
            part = (w_in_ref[:, at].astype(F32) * gain_ref[:, at]).astype(BF)
            out[:, d * LANE : (d + 1) * LANE] = part
            wide = part.astype(F32)
            total = wide if total is None else total + wide
    gain_sum_ref[...] = jnp.sum(total, axis=1, keepdims=True)


def mix_kernel(places_ref, w_out_ref, scale_ref, head_ref, head_pad_ref, mix_ref, walk_ref):
    for d in range(CHIPS):
        for side in range(2):
            walk_ref[:, (side * CHIPS + d) * LANE : (side * CHIPS + d + 1) * LANE] = w_out_ref[:, columns(places_ref, 2 * d + side)]
    head_pad_ref[...] = jnp.zeros_like(head_pad_ref)
    head_pad_ref[0 : head_ref.shape[0], :] = head_ref[...]
    head = head_pad_ref[...]
    scaled = (head.astype(F32) * scale_ref[...]).astype(BF)
    mix_ref[...] = dot(w_out_ref[...], scaled, ((1,), (1,))).astype(BF)


def turn_kernel(own_ref, sib_ref, out_ref):
    units = own_ref.shape[0]
    out_ref[:, :units] = own_ref[...].T
    out_ref[:, units:] = sib_ref[...].T


def add_blocks(own_ref, sib_ref, held, ids, shift, sums):
    away = held.astype(F32) - shift
    first = jnp.sum(away, axis=0, keepdims=True)
    second = jnp.sum(away * away, axis=0, keepdims=True)
    if sums is not None:
        first, second = sums[0] + first, sums[1] + second
    pick = lambda ref: jnp.concatenate([ref[:, d * LANE : (d + 1) * LANE] for d in ids], axis=1)
    return dot(pick(own_ref), held, ((1,), (0,))), dot(pick(sib_ref), held, ((1,), (0,))), first, second


def first_kernel(ids, own_ref, sib_ref, *refs):
    blocks, (acc_ref, give_ref, sums_ref) = refs[:-3], refs[-3:]
    shift = jnp.mean(blocks[0][...].astype(F32), axis=0, keepdims=True)
    held = jnp.concatenate([b[...] for b in blocks], axis=0)
    acc, give, first, second = add_blocks(own_ref, sib_ref, held, ids, shift, None)
    acc_ref[...] = acc
    give_ref[...] = give
    sums_ref[...] = jnp.concatenate([shift, first, second, jnp.zeros((5, shift.shape[1]), F32)], axis=0)


def next_kernel(ids, own_ref, sib_ref, acc_in_ref, give_in_ref, sums_in_ref, *refs):
    blocks, (acc_ref, give_ref, sums_ref) = refs[:-3], refs[-3:]
    shift, first, second = sums_in_ref[0:1, :], sums_in_ref[1:2, :], sums_in_ref[2:3, :]
    held = jnp.concatenate([b[...] for b in blocks], axis=0)
    acc, give, first, second = add_blocks(own_ref, sib_ref, held, ids, shift, (first, second))
    acc_ref[...] = acc_in_ref[...] + acc
    give_ref[...] = (give_in_ref[...] + give).astype(give_ref.dtype)
    sums_ref[...] = jnp.concatenate([shift, first, second, jnp.zeros((5, shift.shape[1]), F32)], axis=0)


def pairs_kernel(ids, own_ref, sib_ref, acc_in_ref, shift_ref, *refs):
    blocks, (acc_ref, sums_ref) = refs[:-2], refs[-2:]
    held = jnp.concatenate([b[...] for b in blocks], axis=0)
    pick = [ref[:, d * LANE : (d + 1) * LANE] for ref in (own_ref, sib_ref) for d in ids]
    acc_ref[...] = acc_in_ref[...] + dot(jnp.concatenate(pick, axis=1), held, ((1,), (0,)))
    shift = shift_ref[0:1, :]
    away = held.astype(F32) - shift
    first = jnp.sum(away, axis=0, keepdims=True)
    second = jnp.sum(away * away, axis=0, keepdims=True)
    sums_ref[...] = jnp.concatenate([shift, first, second, jnp.zeros((5, shift.shape[1]), F32)], axis=0)


def pack_kernel(*refs):
    refs[-1][...] = jnp.concatenate([ref[...] for ref in refs[:-1]], axis=0)


def forward_kernel(places_ref, acc_ref, got_ref, sums_ref, sib_sums_ref, pair_sums_ref, gain_sum_ref, mix_ref, head_ref, x_ref, own_ref, sib_ref, *refs):
    blocks, (pre_ref, hidden_ref, stats_ref, keep_ref, give_ref, scratch) = refs[:-6], refs[-6:]
    held = jnp.concatenate([b[...] for b in blocks], axis=0)
    at = slice(CHIPS // 2 * LANE, (CHIPS // 2 + 1) * LANE)
    acc = dot(jnp.concatenate([own_ref[:, at], sib_ref[:, at]], axis=1), held, ((1,), (0,)))
    shift = sums_ref[0:1, :]
    away = held.astype(F32) - shift
    sets = [(held.shape[0], shift, jnp.sum(away, axis=0, keepdims=True), jnp.sum(away * away, axis=0, keepdims=True))]
    sets += [(count * LANE, ref[0:1, :], ref[1:2, :], ref[2:3, :]) for count, ref in ((5, sums_ref), (5, sib_sums_ref), (4, pair_sums_ref))]
    means = [base + first / count for count, base, first, _ in sets]
    channels = 2 * CHIPS * LANE
    tok_mean = sum(s[0] * mean for s, mean in zip(sets, means)) / channels
    spread = sum(second - first * first / count + count * (mean - tok_mean) ** 2 for (count, _, first, second), mean in zip(sets, means))
    inv_std = lax.rsqrt(spread / channels + norm_eps)
    stats_ref[...] = jnp.concatenate([tok_mean, inv_std, jnp.zeros((6, tok_mean.shape[1]), F32)], axis=0)
    pre_act = (acc + acc_ref[...] + got_ref[...].astype(F32) - gain_sum_ref[...] * tok_mean) * inv_std
    pre_ref[...] = pre_act
    hidden = (pre_act * (0.5 * (1.0 + lax.erf(pre_act * 0.7071067811865476)))).astype(BF)
    hidden_ref[...] = hidden
    my_head = head_ref[:, columns(places_ref, MINE)]
    logits = dot(mix_ref[...], hidden, ((0,), (0,))) + dot(my_head, x_ref[...], ((1,), (0,)))
    core = places_ref[CORE]
    chunks = keep_ref.shape[0]
    for g in range(2 * chunks):
        scratch[g] = logits[:, g * LANE : (g + 1) * LANE]
    keep_ref[...] = scratch[pl.ds(chunks * core, chunks)]
    give_ref[...] = scratch[pl.ds(chunks - chunks * core, chunks)]


def slope_kernel(pre_ref, stats_ref, slope_ref):
    pre_act = pre_ref[...]
    cum_prob = 0.5 * (1.0 + lax.erf(pre_act * 0.7071067811865476))
    density = jnp.exp(-0.5 * pre_act * pre_act) * 0.3989422804014327
    slope_ref[...] = (cum_prob + pre_act * density) * stats_ref[1:2, :]


def pick(marks_ref, y, z, chunks):
    size = chunks[0].shape
    bit_y = jnp.broadcast_to(marks_ref[1:2, :], size) != y
    bit_z = jnp.broadcast_to(marks_ref[2:3, :], size) != z
    return jnp.where(bit_y, jnp.where(bit_z, chunks[3], chunks[2]), jnp.where(bit_z, chunks[1], chunks[0]))


def fold_kernel(marks_ref, keep_ref, got_ref, *outs):
    chunks = [keep_ref[g] + got_ref[g] for g in range(4)]
    for out, (y, z) in zip(outs, ((0, 0), (1, 0), (0, 1), (1, 1))):
        out[...] = pick(marks_ref, y, z, chunks)


def add_kernel(*refs):
    refs[-1][...] = sum(ref[...] for ref in refs[:-1])


def softmax_kernel(classes, marks_ref, kept_ref, got_ref, labels_ref, grad_ref):
    kept = kept_ref[...] + got_ref[...]
    chunk = 4 * marks_ref[0:1, :] + 2 * marks_ref[1:2, :] + marks_ref[2:3, :]
    labels = labels_ref[:, :LANE]
    for g in range(1, labels_ref.shape[1] // LANE):
        labels = jnp.where(chunk == g, labels_ref[:, g * LANE : (g + 1) * LANE], labels)
    class_id = lax.broadcasted_iota(jnp.int32, kept.shape, 0)
    kept = jnp.where(class_id < classes, kept, -jnp.inf)
    col_max = jnp.max(kept, axis=0, keepdims=True)
    exp_terms = jnp.exp(kept - col_max)
    exp_total = jnp.sum(exp_terms, axis=0, keepdims=True)
    onehot = class_id == labels
    picked = jnp.sum(jnp.where(onehot, kept, 0.0), axis=0, keepdims=True)
    loss = jnp.log(exp_total) + col_max - picked
    loss_high = loss.astype(BF).astype(F32)
    grad = exp_terms / exp_total - onehot.astype(F32)
    grad = jnp.where(class_id == classes, loss_high, jnp.where(class_id == classes + 1, loss - loss_high, grad))
    grad_ref[...] = grad.astype(BF)


def join_kernel(marks_ref, own_ref, y_ref, z_ref, both_ref, out_ref):
    chunks = [ref[...].astype(F32) for ref in (own_ref, z_ref, y_ref, both_ref)]
    for g in range(4):
        out_ref[g] = pick(marks_ref, g // 2, g % 2, chunks).astype(BF)


def grad_kernel(places_ref, own_ref, sib_ref, mix_ref, slope_ref, grad_ref, scaled_ref):
    core = places_ref[CORE]
    chunks = own_ref.shape[0]
    for g in range(chunks):
        grad_ref[:, pl.ds(pl.multiple_of((core * chunks + g) * LANE, LANE), LANE)] = own_ref[g]
        grad_ref[:, pl.ds(pl.multiple_of(((1 - core) * chunks + g) * LANE, LANE), LANE)] = sib_ref[g]
    scaled_ref[...] = (dot(mix_ref[...], grad_ref[...], ((1,), (0,))) * slope_ref[...]).astype(BF)


def branch_kernel(hidden_ref, grad_ref, w_out_ref, scaled_ref, pre_ref, gain_sum_ref, mixed_ref, keep_ref, give_ref):
    mixed = dot(hidden_ref[...], grad_ref[...], ((1,), (1,))).astype(BF)
    mixed_ref[...] = mixed
    branch = dot(mixed, w_out_ref[...], ((0,), (0,)))
    wide = scaled_ref[...].astype(F32)
    mean_part = jnp.sum(wide * gain_sum_ref[...], axis=0, keepdims=True)
    proj_part = jnp.sum(wide * pre_ref[...], axis=0, keepdims=True)
    means = jnp.concatenate([mean_part, proj_part, jnp.zeros((SUB_ROWS - 2, wide.shape[1]), F32)], axis=0)
    width = keep_ref.shape[1]
    for side, out in enumerate((keep_ref, give_ref)):
        out[...] = jnp.concatenate([branch[:, side * width : (side + 1) * width], means], axis=0).astype(out.dtype)


def message_of(d, turned_ref, own_ref, got_ref, keep_ref, sib_ref):
    units = own_ref.shape[0]
    at = slice(d * LANE, (d + 1) * LANE)
    rows = dot(turned_ref[at, :units], own_ref[...], ((1,), (0,))) + dot(turned_ref[at, units:], got_ref[...], ((1,), (0,)))
    means = keep_ref[CLASS_ROWS:, :] + sib_ref[CLASS_ROWS:, :].astype(F32)
    means = [means[n : n + 1, g * LANE : (g + 1) * LANE] for n in range(2) for g in range(8)]
    means = jnp.concatenate(means + [jnp.zeros((EXTRA - 16, LANE), F32)], axis=0)
    branch = keep_ref[:CLASS_ROWS, at] + sib_ref[:CLASS_ROWS, at].astype(F32)
    branch = jnp.concatenate([branch, jnp.zeros((7 * EXTRA - CLASS_ROWS, LANE), F32)], axis=0)
    extra = jnp.concatenate([means] + [branch[g * EXTRA : (g + 1) * EXTRA] for g in range(7)], axis=1)
    return jnp.concatenate([rows, extra], axis=0)


def message_kernel(ids, *refs):
    for d, out in zip(ids, refs[-len(ids) :]):
        out[...] = message_of(d, *refs[: -len(ids)])


def far_kernel(*refs):
    upper, lower = refs[-2:]
    cut = upper.shape[0]
    total = message_of(CHIPS // 2, *refs[:-2])
    upper[...] = total[:cut].astype(BF)
    lower[...] = total[cut:].astype(BF)


def sum_kernel(begin, own_ref, got_ref, *outs):
    own, got = own_ref[...], got_ref[...].astype(F32)
    end = begin + got.shape[0]
    pieces = [own[:begin]] * (begin > 0) + [own[begin:end] + got] + [own[end:]] * (end < own.shape[0])
    total = jnp.concatenate(pieces, axis=0) if len(pieces) > 1 else pieces[0]
    for n, out in enumerate(outs):
        width = out.shape[1]
        out[...] = total[:, n * width : (n + 1) * width].astype(BF)


def d_w_out_kernel(mixed_ref, head_ref, scale_ref, out_ref, done_ref, held, sems):
    done_ref[...] = jnp.zeros_like(done_ref)
    mixed = mixed_ref[...]
    copies = []
    for n in range(sems.shape[0]):
        at = slice(n * held.shape[1] // sems.shape[0], (n + 1) * held.shape[1] // sems.shape[0])
        held[:, at] = dot(mixed, head_ref[:, at], ((1,), (0,))) * scale_ref[:, at]
        copies.append(pltpu.make_async_copy(held.at[:, at], out_ref.at[:, at], sems.at[n]))
        copies[-1].start()
    for copy in copies:
        copy.wait()


def d_w_in_kernel(places_ref, gain_ref, scaled_ref, stats_ref, own_ref, sib_ref, out_ref, done_ref, held, sems):
    done_ref[...] = jnp.zeros_like(done_ref)
    scaled = scaled_ref[...]
    shift = jnp.sum(scaled.astype(F32) * stats_ref[0:1, :], axis=1, keepdims=True)
    copies = []
    for side, blocks in enumerate((own_ref, sib_ref)):
        for n in range(0, CHIPS, 2):
            both = dot(scaled, blocks[n * LANE : (n + 2) * LANE, :], ((1,), (1,))) - shift
            for k in range(2):
                at = columns(places_ref, 2 * (n + k) + side)
                slot = len(copies)
                held[slot] = both[:, k * LANE : (k + 1) * LANE] * gain_ref[:, at]
                copies.append(pltpu.make_async_copy(held.at[slot], out_ref.at[:, at], sems.at[slot]))
                copies[-1].start()
    for copy in copies:
        copy.wait()


def head_kernel(classes, places_ref, x_ref, head_ref, grad_ref, out_grad_ref, d_head_ref, loss_ref):
    my_head = head_ref[:, columns(places_ref, MINE)]
    grad = grad_ref[...]
    out_grad_ref[...] = dot(my_head, grad, ((0,), (0,)))
    d_head_ref[...] = dot(grad, x_ref[...], ((1,), (1,)))
    loss_ref[...] = (jnp.sum(grad[classes : classes + 2].astype(F32)) / grad.shape[1]).reshape(1, 1)


def put_conv_grad(groups, got, means_rows, conv_ref, stats_ref, grid_pad):
    rows = conv_ref.shape[0]
    channels = rows * 2 * CHIPS
    for n, g in enumerate(groups):
        at = slice(g * LANE, (g + 1) * LANE)
        normed = (conv_ref[:, at].astype(F32) - stats_ref[0:1, at]) * stats_ref[1:2, at]
        conv_grad = got[:rows, n * LANE : (n + 1) * LANE] - (means_rows[g : g + 1, :] + normed * means_rows[8 + g : 9 + g, :]) * (1.0 / channels)
        put_rows(grid_pad, 4 * g, conv_grad)


def add_taps(groups, copies, copies_x, sums):
    for g in groups:
        conv_grad = copies[HALF, pl.ds(4 * g + HALF, 4)]
        for j in range(KS):
            for i in range(KS):
                prod = (conv_grad * copies_x[j, pl.ds(4 * g + i, 4)]).reshape(16, 8, LANE)
                index = i * KS + j
                total = jnp.sum(prod, axis=0)
                if g == 0:
                    sums[index] = total
                else:
                    sums[index] += total


def copy_rows(begin, end, grid_pad, copies):
    rows = pl.ds(begin, end - begin)
    for j in range(KS):
        copies[j, rows] = grid_pad[rows, pl.ds(8 + j - HALF, WIN_W), :]


def upper_kernel(mine_ref, forth_ref, back_ref, conv_ref, stats_ref, taps, copies_x, out_grad_ref,
                 d_x_ref, sums, grid_pad, extra_ref, copies):
    rows = conv_ref.shape[0]
    width = forth_ref.shape[1]
    got = mine_ref[:, :width] + forth_ref[...].astype(F32) + back_ref[...].astype(F32)
    extra_ref[...] = got[rows:]
    clear_border(grid_pad)
    put_conv_grad(range(4), got, got[rows:, :LANE], conv_ref, stats_ref, grid_pad)
    copy_rows(0, 16 + HALF, grid_pad, copies)
    for g in range(3):
        at = slice(g * LANE, (g + 1) * LANE)
        d_x_ref[:, at] = out_grad_ref[:, at] + conv_rows(copies, taps, 4 * g, True).reshape(LANE, LANE).T
    add_taps(range(4), copies, copies_x, sums)


def lower_kernel(classes, places_ref, mine_ref, forth_ref, back_ref, conv_ref, stats_ref, taps, copies_x, out_grad_ref, head_grad_ref, head_ref, scale_ref,
                 d_upper_ref, sums_ref, grid_ref, extra_ref, d_x_ref, d_dw_ref, d_scale_ref, d_head_ref, grid_pad, copies, sums):
    rows = conv_ref.shape[0]
    width = forth_ref.shape[1]
    got = mine_ref[:, width:] + forth_ref[...].astype(F32) + back_ref[...].astype(F32)
    extra = jnp.concatenate([extra_ref[...], got[rows:]], axis=1)
    branch = jnp.concatenate([extra[:, g * LANE : (g + 1) * LANE] for g in range(1, 8)], axis=0)[:CLASS_ROWS]
    sums[...] = sums_ref[...]
    grid_pad[...] = grid_ref[...]
    put_conv_grad(range(4, 8), got, extra[:, :LANE], conv_ref, stats_ref, grid_pad)
    copy_rows(12, WIN_H + 2 * HALF, grid_pad, copies)
    d_x_ref[:, : 3 * LANE] = d_upper_ref[...]
    for g in range(3, 8):
        at = slice(g * LANE, (g + 1) * LANE)
        d_x_ref[:, at] = out_grad_ref[:, at] + conv_rows(copies, taps, 4 * g, True).reshape(LANE, LANE).T
    add_taps(range(4, 8), copies, copies_x, sums)
    d_dw_ref[...] = jnp.sum(sums[...], axis=1)
    at = columns(places_ref, MINE)
    d_scale_ref[...] = jnp.sum(head_ref[:, at].astype(F32) * branch, axis=0, keepdims=True)
    d_head_ref[...] = (head_grad_ref[...] + scale_ref[:, at] * branch)[:classes]


def walk_step(walk, step):
    forth, back = walk[(1 - step) % CHIPS][0], walk[step - 1][0]
    half = forth.shape[0] // 2
    if step < CHIPS // 2:
        walk[(-step) % CHIPS], walk[step] = (send(forth, FORTH),), (send(back, BACK),)
    else:
        walk[step] = (send(forth[:half], FORTH), send(back[half:], BACK))


def hold(walk, step, *others):
    spots = [(-step) % CHIPS, step]
    held = lax.optimization_barrier((walk[spots[0]][0], walk[spots[1]][0], *others))
    walk[spots[0]], walk[spots[1]] = (held[0],), (held[1],)
    return held[2:]


def per_device(features, dw_weight, norm_gain, layer_scale, w_in, w_out, w_head, labels):
    rows, tokens = features.shape
    units, channels = w_in.shape
    classes = w_head.shape[1]
    me = lax.axis_index("ch")
    places = lax.dynamic_index_in_dim(jnp.asarray(PLACES), me, 0, keepdims=False)
    marks = lax.dynamic_index_in_dim(jnp.asarray(MARKS), me, 0, keepdims=False)
    taps = dw_weight.T
    scale_row, gain_row, labels_row = layer_scale[None, :], norm_gain[None, :], labels[None, :]
    grid_shape = pltpu.VMEM((WIN_H + 2 * HALF, WIN_W + 16, LANE), F32)
    copies_size = (KS, WIN_H + 2 * HALF, WIN_W, LANE)
    half_channels = CHIPS * rows
    vm = lambda *arrays: [(a, VMEM) for a in arrays]
    spot, mark = [(places, SMEM)], vm(marks)
    f32s, bf16s, sums_size = ((units, tokens), F32), ((units, tokens), BF), ((8, tokens), F32)

    conv_out, features, taps = call(
        conv_kernel, [((rows, tokens), BF), ((rows, tokens), BF), ((KS * KS, rows), F32)], [(features, HBM), (taps, HBM)],
        [grid_shape, pltpu.VMEM(copies_size, F32), pltpu.SemaphoreType.DMA((2,))],
        limit=12, name="conv_forward",
    )
    walk = {0: (conv_out,)}
    walk_step(walk, 1)
    w_own, w_give, gain_sum = call(
        weights_kernel,
        [((units, half_channels), BF), ((units, half_channels), BF), ((units, 1), F32)],
        spot + vm(w_in, gain_row), flops=4e8, moved=4e6, limit=12, name="weights_ready", after=[conv_out, marks],
    )
    w_own, w_give, gain_sum = hold(walk, 1, w_own, w_give, gain_sum)
    w_sib = send(w_give, SIBLING)
    walk_step(walk, 2)
    so_far = call(
        functools.partial(first_kernel, (0, 1, 7)), [f32s, f32s, sums_size],
        vm(w_own, w_sib, *walk[0], *walk[1], *walk[7]), flops=1e9, moved=4e6, limit=16, name="forward_first",
    )
    so_far = hold(walk, 2, *so_far)
    walk_step(walk, 3)
    head_pad, mix, w_out_walk = call(
        mix_kernel,
        [((CLASS_ROWS, channels), BF), ((units, CLASS_ROWS), BF), ((units, channels), BF)],
        spot + vm(w_out, scale_row, w_head.T), flops=1e9, moved=4e6, limit=12, name="mix_ready", after=[so_far[2]],
    )
    so_far = call(
        functools.partial(next_kernel, (2, 6)), [f32s, bf16s, sums_size],
        vm(w_own, w_sib, *so_far, *walk[2], *walk[6]), flops=6e8, moved=4e6, limit=16, name="forward_next",
    )
    *so_far, head_pad, mix, w_out_walk = hold(walk, 3, *so_far, head_pad, mix, w_out_walk)
    acc, give, sums = so_far
    got, sib_sums = send(give, SIBLING), send(sums, SIBLING)
    walk_step(walk, 4)
    acc, pair_sums = call(
        functools.partial(pairs_kernel, (3, 5)), [f32s, sums_size],
        vm(w_own, w_give, acc, sums, *walk[3], *walk[5], send(walk[3][0], SIBLING), send(walk[5][0], SIBLING)),
        flops=1e9, moved=4e6, limit=16, name="forward_pairs",
    )
    upper, acc, pair_sums = lax.optimization_barrier((walk[4][0], acc, pair_sums))
    walk[4] = (upper, walk[4][1])
    far = [*walk[4], *[send(b, SIBLING) for b in walk[4]]]
    chunks = tokens // LANE // 2
    chunk = lambda count, kind=F32: ((count, CLASS_ROWS, LANE), kind)
    pre_act, hidden, stats, keep, give = call(
        forward_kernel, [f32s, bf16s, sums_size, chunk(chunks), chunk(chunks)],
        spot + vm(acc, got, sums, sib_sums, pair_sums, gain_sum, mix, head_pad, features, w_own, w_give, *far),
        [pltpu.VMEM((2 * chunks, CLASS_ROWS, LANE), F32)], flops=1e9, moved=4e6, limit=16, name="forward_hidden",
    )

    own_chunk = ((CLASS_ROWS, LANE), F32)
    others = (2, 4, 6)
    kept, *gives = call(fold_kernel, [own_chunk] * 4, mark + vm(keep, send(give, SIBLING)), limit=4, name="fold_core")
    (packed,) = call(
        pack_kernel, [((half_channels, tokens), BF)], vm(*[b for d in range(CHIPS) for b in walk[d]]), flops=4e8, moved=4e6, limit=10, name="pack_blocks", after=[kept],
    )
    sib_packed = send(packed, SIBLING)
    (slope,) = call(slope_kernel, [f32s], vm(pre_act, stats), flops=5e8, moved=4e6, limit=8, name="gelu_slope", after=[packed])
    (kept,) = call(
        add_kernel, [own_chunk], vm(kept, *[send(part, flip_perm(bits)) for part, bits in zip(gives, others)]), limit=4, name="fold_chips", after=[slope],
    )
    (turned,) = call(turn_kernel, [((half_channels, 2 * units), BF)], vm(w_own, w_sib), flops=4e8, moved=4e6, limit=10, name="weights_turned", after=[kept])
    (grad,) = call(
        functools.partial(softmax_kernel, classes), [((CLASS_ROWS, LANE), BF)], mark + vm(kept, send(kept, flip_perm(8)), labels_row), limit=4, name="class_grad", after=[turned, sib_packed],
    )
    (copies_x,) = call(copies_kernel, [(copies_size, F32)], vm(features), [grid_shape], flops=4e8, moved=4e6, limit=12, name="window_copies", after=[grad])
    (grad,) = call(
        join_kernel, [((chunks, CLASS_ROWS, LANE), BF)], mark + vm(grad, *[send(grad, flip_perm(bits)) for bits in others]), limit=4, name="join_chips", after=[copies_x],
    )

    grad, scaled = call(
        grad_kernel, [((CLASS_ROWS, tokens), BF), bf16s], spot + vm(grad, send(grad, SIBLING), mix, slope), flops=6e8, moved=4e6, limit=12, name="hidden_grad",
    )
    got = send(scaled, SIBLING)
    extra_rows = CLASS_ROWS + SUB_ROWS
    mixed, keep, give = call(
        branch_kernel, [((units, CLASS_ROWS), BF), ((extra_rows, half_channels), F32), ((extra_rows, half_channels), BF)],
        vm(hidden, grad, w_out_walk, scaled, pre_act, gain_sum), flops=8e8, moved=4e6, limit=12, name="class_products",
    )
    sources = vm(turned, scaled, got, keep, send(give, SIBLING))
    height = rows + EXTRA
    cut = 80
    forth, back = call(far_kernel, [((cut, tokens), BF), ((height - cut, tokens), BF)], sources, flops=3e8, moved=2e6, limit=8, name="message_far")
    forth, back = send(forth, FORTH), send(back, BACK)
    d_w_out, d_w_out_done = call(
        d_w_out_kernel, [((units, channels), F32), ((8, LANE), F32)], vm(mixed, head_pad, scale_row),
        [pltpu.VMEM((units, channels), F32), pltpu.SemaphoreType.DMA((4,))], flops=1e9, moved=8e6, limit=12, name="d_w_out", out_spaces=(pl.ANY, pltpu.VMEM),
        after=[forth],
    )
    out_grad, head_grad, mean_loss = call(
        functools.partial(head_kernel, classes), [((rows, tokens), F32), ((CLASS_ROWS, rows), F32), ((1, 1), F32)],
        spot + vm(features, head_pad, grad), flops=4e8, moved=2e6, limit=8, name="class_head", after=[forth],
    )
    beside = {3: [], 2: [d_w_out_done, out_grad], 1: []}
    for step in range(CHIPS // 2 - 1, 0, -1):
        ahead, behind = call(
            functools.partial(message_kernel, (step, CHIPS - step)), [((height, tokens), F32)] * 2, sources,
            flops=6e8, moved=2e6, limit=8, name="messages",
        )
        first = step == CHIPS // 2 - 1
        parts = 2 if step == 1 else 1
        add = lambda begin, own, got, waits: call(
            functools.partial(sum_kernel, begin), [((height, tokens // parts), BF)] * parts, vm(own, got), limit=6, name="walk_sum", after=waits,
        )
        forth, back = add(0, ahead, forth, []), add(cut if first else 0, behind, back, beside[step])
        if step == 1:
            continue
        (forth,), (back,) = forth, back
        if step == 2:
            d_w_in, d_w_in_done = call(
                d_w_in_kernel, [((units, channels), F32), ((8, LANE), F32)], spot + vm(gain_row, scaled, stats, packed, sib_packed),
                [pltpu.VMEM((2 * CHIPS, units, LANE), F32), pltpu.SemaphoreType.DMA((2 * CHIPS,))],
                flops=2e9, moved=8e6, limit=12, name="d_w_in", out_spaces=(pl.ANY, pltpu.VMEM), after=[forth, back],
            )
            beside[1] = [d_w_in_done]
        forth, back = send(forth, FORTH), send(back, BACK)
    (mine,) = call(functools.partial(message_kernel, (0,)), [((height, tokens), F32)], sources, flops=3e8, moved=2e6, limit=8, name="messages", after=[ahead])
    ends = [(send(forth[n], FORTH), send(back[n], BACK)) for n in range(2)]
    upper = call(
        upper_kernel,
        [((rows, 3 * LANE), F32), ((KS * KS, 8, LANE), F32), (grid_shape.shape, F32), ((EXTRA, tokens // 2), F32)],
        vm(mine, *ends[0], conv_out, stats, taps, copies_x, out_grad), [pltpu.VMEM(copies_size, F32)],
        flops=4e8, moved=2e6, limit=16, name="conv_backward_upper",
    )
    d_features, d_dw, d_scale, d_head = call(
        functools.partial(lower_kernel, classes),
        [((rows, tokens), F32), ((KS * KS, rows), F32), ((1, rows), F32), ((classes, rows), F32)],
        spot + vm(mine, *ends[1], conv_out, stats, taps, copies_x, out_grad, head_grad, head_pad, scale_row, *upper),
        [grid_shape, pltpu.VMEM(copies_size, F32), pltpu.VMEM((KS * KS, 8, LANE), F32)], limit=16, name="conv_backward_lower",
    )
    return (d_features, d_dw.T, d_scale[0], d_w_in, d_w_out, d_head.T, mean_loss[0])


def conv_apply(in_grid, kernel):
    half = KS // 2
    padded = jnp.pad(in_grid, ((0, 0), (half, half), (half, half)))
    running = jnp.zeros(in_grid.shape, in_grid.dtype)
    for row_shift in range(KS):
        for col_shift in range(KS):
            tap = kernel[:, row_shift * KS + col_shift]
            running = (
                running
                + tap[:, None, None]
                * padded[:, row_shift : row_shift + WIN_H, col_shift : col_shift + WIN_W]
            )
    return running


def gelu_parts(values):
    cum_prob = 0.5 * (1.0 + lax.erf(values * 0.7071067811865476))
    density = jnp.exp(-0.5 * values * values) * 0.3989422804014327
    return (values * cum_prob, cum_prob + values * density)


def plain_device(features, dw_weight, norm_gain, layer_scale, w_in, w_out, w_head, labels):
    highest = lax.Precision.HIGHEST
    my_rows = features.shape[0]
    tok_count = features.shape[1]
    class_count = w_head.shape[1]
    row_offset = lax.axis_index("ch") * my_rows
    inputs_wide = features.astype(jnp.float32)
    in_grid = inputs_wide.reshape(my_rows, WIN_H, WIN_W)
    conv_out = conv_apply(in_grid, dw_weight).reshape(my_rows, tok_count).astype(jnp.bfloat16)
    conv_all = lax.all_gather(conv_out, "ch", axis=0, tiled=True)
    conv_wide = conv_all.astype(jnp.float32)
    tok_mean = jnp.mean(conv_wide, axis=0)
    centered = conv_wide - tok_mean[None, :]
    tok_var = jnp.mean(centered * centered, axis=0)
    inv_std = 1.0 / jnp.sqrt(tok_var + norm_eps)
    normed = centered * inv_std[None, :]
    norm_out = (norm_gain[:, None] * normed).astype(jnp.bfloat16)
    pre_act = jnp.dot(w_in, norm_out, preferred_element_type=jnp.float32)
    gelu_out, gelu_slope = gelu_parts(pre_act)
    hidden = gelu_out.astype(jnp.bfloat16)
    my_scale = lax.dynamic_slice_in_dim(layer_scale, row_offset, my_rows, 0)
    head_wide = w_head.astype(jnp.float32)
    my_head = lax.dynamic_slice_in_dim(head_wide, row_offset, my_rows, 0)
    w_cols = w_out
    branch_sum = lax.psum_scatter(
        lax.dot_general(
            w_cols, hidden, (((0,), (0,)), ((), ())), preferred_element_type=jnp.float32
        ),
        "ch",
        scatter_dimension=0,
        tiled=True,
    )
    block_out = inputs_wide + my_scale[:, None] * branch_sum
    part_logits = lax.dot_general(block_out, my_head, (((0,), (0,)), ((), ())), precision=highest)
    logits = lax.psum(part_logits, "ch")
    row_max = jnp.max(logits, axis=1, keepdims=True)
    exp_terms = jnp.exp(logits - row_max)
    exp_total = jnp.sum(exp_terms, axis=1, keepdims=True)
    log_total = jnp.log(exp_total) + row_max
    onehot = (labels[:, None] == jnp.arange(class_count, dtype=jnp.int32)[None, :]).astype(
        jnp.float32
    )
    picked = jnp.sum(logits * onehot, axis=1)
    mean_loss = jnp.mean(log_total[:, 0] - picked).reshape(1)
    logit_grad = exp_terms / exp_total - onehot
    out_grad = lax.dot_general(my_head, logit_grad, (((1,), (1,)), ((), ())), precision=highest)
    d_head = jnp.dot(block_out, logit_grad, precision=highest)
    d_scale = jnp.sum(out_grad * branch_sum, axis=1)
    branch_grad = (my_scale[:, None] * out_grad).astype(jnp.bfloat16)
    incoming = lax.all_gather(branch_grad, "ch", axis=0, tiled=True)
    hidden_acc = jnp.dot(w_cols, incoming, preferred_element_type=jnp.float32)
    tile_grad = lax.dot_general(
        hidden, incoming, (((1,), (1,)), ((), ())), preferred_element_type=jnp.float32
    )
    pre_grad = (hidden_acc * gelu_slope).astype(jnp.bfloat16)
    d_w_in = lax.dot_general(
        pre_grad, norm_out, (((1,), (1,)), ((), ())), preferred_element_type=jnp.float32
    )
    norm_grad = lax.dot_general(
        w_in, pre_grad, (((0,), (0,)), ((), ())), preferred_element_type=jnp.float32
    )
    gained = norm_gain[:, None] * norm_grad
    conv_term = (
        gained
        - jnp.mean(gained, axis=0)[None, :]
        - normed * jnp.mean(gained * normed, axis=0)[None, :]
    ) * inv_std[None, :]
    conv_grad = lax.psum_scatter(conv_term, "ch", scatter_dimension=0, tiled=True)
    unused, pullback = jax.vjp(conv_apply, in_grid, dw_weight)
    grid_grad, d_dw = pullback(conv_grad.reshape(my_rows, WIN_H, WIN_W))
    d_features = out_grad + grid_grad.reshape(my_rows, tok_count)
    return (d_features, d_dw, d_scale, d_w_in, tile_grad, d_head, mean_loss)


def solution(mesh):
    placed = (P("ch", "grp"), P("ch", None), P(), P(), P("ch", None), P("ch", None), P(), P("grp"))
    return jax.shard_map(
        per_device if mesh.shape["ch"] == 2 * CHIPS else plain_device,
        mesh=mesh,
        in_specs=placed,
        out_specs=(
            P("ch", "grp"),
            P("ch", "grp"),
            P(("grp", "ch")),
            P(("grp", "ch"), None),
            P(("grp", "ch"), None),
            P("ch", "grp"),
            P("grp"),
        ),
        check_vma=False,
    )
```

```python
import functools

import jax
import jax.numpy as jnp
import numpy as np
from jax import lax
from jax.experimental import pallas as pl
from jax.experimental.pallas import tpu as pltpu
from jax.sharding import PartitionSpec as P

KS = 7
HALF = KS // 2
WIN_H = 32
WIN_W = 32
norm_eps = 1e-06
BF = jnp.bfloat16
F32 = jnp.float32

WALK = (0, 2, 4, 6, 7, 5, 3, 1)
CHIPS = len(WALK)
CORES = 2
REL = np.array([[WALK[(WALK.index(chip) + d) % CHIPS] for d in range(CHIPS)] for chip in range(CHIPS)], np.int32)
PLACES = np.array(
    [
        [REL[dev // 2][d] * 2 + (dev % 2 ^ side) for d in range(CHIPS) for side in range(2)] + [dev % 2, dev]
        for dev in range(2 * CHIPS)
    ],
    np.int32,
)
CORE, MINE = 2 * CHIPS, 2 * CHIPS + 1
MARKS = np.broadcast_to(
    np.array([[dev >> bit & 1 for bit in range(8)] for dev in range(2 * CHIPS)], np.int32)[:, :, None], (2 * CHIPS, 8, 128)
)
CLASS_ROWS = 160
EXTRA = 24
SUB_ROWS = 16
LANE = 128


def walk_perm(step):
    return [
        (WALK[p] * 2 + c, WALK[(p + step) % CHIPS] * 2 + c) for p in range(CHIPS) for c in range(2)
    ]


def flip_perm(bit):
    return [(i, i ^ bit) for i in range(2 * CHIPS)]


def send(value, perm):
    return lax.ppermute(value, "ch", perm)


FORTH, BACK, SIBLING = walk_perm(1), walk_perm(-1), flip_perm(1)
VMEM = pl.BlockSpec(memory_space=pltpu.VMEM)
SMEM = pl.BlockSpec(memory_space=pltpu.SMEM)
HBM = pl.BlockSpec(memory_space=pltpu.HBM)


def call(kernel, outs, ins, scratch=(), flops=0, moved=0, limit=40, name=None, after=(), out_spaces=None):
    count = len(ins)

    def body(*refs):
        kernel(*refs[:count], *refs[count + len(after) :])

    result = pl.pallas_call(
        body,
        out_shape=[jax.ShapeDtypeStruct(s, d) for s, d in outs],
        in_specs=[s for _, s in ins] + [pl.BlockSpec(memory_space=pl.ANY)] * len(after),
        out_specs=[pl.BlockSpec(memory_space=space) for space in out_spaces or [pltpu.VMEM] * len(outs)],
        scratch_shapes=list(scratch),
        compiler_params=pltpu.CompilerParams(vmem_limit_bytes=limit << 20),
        cost_estimate=pl.CostEstimate(flops=int(flops), bytes_accessed=int(moved), transcendentals=0),
        name=name,
    )(*[a for a, _ in ins], *after)
    return result


def dot(a, b, dims):
    return lax.dot_general(a, b, (dims, ((), ())), preferred_element_type=F32)


def shifted_copies(grid_pad, copies):
    for j in range(KS):
        copies[j] = grid_pad[:, pl.ds(8 + j - HALF, WIN_W), :]


def clear_border(grid_pad):
    grid_pad[...] = jnp.zeros_like(grid_pad)


def put_rows(grid_pad, row, tile):
    grid_pad[pl.ds(row + HALF, 4), pl.ds(8, WIN_W), :] = tile.T.reshape(4, WIN_W, tile.shape[0])


def conv_rows(copies, taps, row, flip):
    acc = None
    for j in range(KS):
        for i in range(KS):
            index = (KS - 1 - i) * KS + KS - 1 - j if flip else i * KS + j
            term = taps[index : index + 1, :][None] * copies[j, pl.ds(row + i, 4)]
            acc = term if acc is None else acc + term
    return acc


def conv_kernel(x_hbm, taps_hbm, out_ref, x_ref, taps, grid_pad, copies, sems):
    fetches = [pltpu.make_async_copy(x_hbm, x_ref, sems.at[0]), pltpu.make_async_copy(taps_hbm, taps, sems.at[1])]
    for fetch in fetches:
        fetch.start()
    clear_border(grid_pad)
    for fetch in fetches:
        fetch.wait()
    for g in range(8):
        put_rows(grid_pad, 4 * g, x_ref[:, g * LANE : (g + 1) * LANE].astype(F32))
    shifted_copies(grid_pad, copies)
    for g in range(8):
        acc = conv_rows(copies, taps, 4 * g, False)
        out_ref[:, g * LANE : (g + 1) * LANE] = acc.reshape(LANE, LANE).T.astype(BF)


def copies_kernel(x_ref, copies, grid_pad):
    clear_border(grid_pad)
    for g in range(8):
        put_rows(grid_pad, 4 * g, x_ref[:, g * LANE : (g + 1) * LANE].astype(F32))
    shifted_copies(grid_pad, copies)


def columns(places_ref, entry):
    return pl.ds(pl.multiple_of(places_ref[entry] * LANE, LANE), LANE)


def weights_kernel(places_ref, w_in_ref, gain_ref, own_ref, sib_ref, gain_sum_ref):
    total = None
    for d in range(CHIPS):
        for side, out in enumerate((own_ref, sib_ref)):
            at = columns(places_ref, 2 * d + side)
            part = (w_in_ref[:, at].astype(F32) * gain_ref[:, at]).astype(BF)
            out[:, d * LANE : (d + 1) * LANE] = part
            wide = part.astype(F32)
            total = wide if total is None else total + wide
    gain_sum_ref[...] = jnp.sum(total, axis=1, keepdims=True)


def mix_kernel(places_ref, w_out_ref, scale_ref, head_ref, head_pad_ref, mix_ref, walk_ref, my_head_ref, my_scale_ref):
    for d in range(CHIPS):
        for side in range(2):
            walk_ref[:, (side * CHIPS + d) * LANE : (side * CHIPS + d + 1) * LANE] = w_out_ref[:, columns(places_ref, 2 * d + side)]
    head_pad_ref[...] = jnp.zeros_like(head_pad_ref)
    head_pad_ref[0 : head_ref.shape[0], :] = head_ref[...]
    head = head_pad_ref[...]
    scaled = (head.astype(F32) * scale_ref[...]).astype(BF)
    mix_ref[...] = dot(w_out_ref[...], scaled, ((1,), (1,))).astype(BF)
    my_head_ref[...] = head_pad_ref[:, columns(places_ref, MINE)]
    my_scale_ref[...] = scale_ref[:, columns(places_ref, MINE)]


def turn_kernel(own_ref, sib_ref, out_ref):
    units = own_ref.shape[0]
    out_ref[:, :units] = own_ref[...].T
    out_ref[:, units:] = sib_ref[...].T


def add_blocks(own_ref, sib_ref, held, ids, shift, sums):
    away = held.astype(F32) - shift
    first = jnp.sum(away, axis=0, keepdims=True)
    second = jnp.sum(away * away, axis=0, keepdims=True)
    if sums is not None:
        first, second = sums[0] + first, sums[1] + second
    pick = lambda ref: jnp.concatenate([ref[:, d * LANE : (d + 1) * LANE] for d in ids], axis=1)
    return dot(pick(own_ref), held, ((1,), (0,))), dot(pick(sib_ref), held, ((1,), (0,))), first, second


def first_kernel(ids, own_ref, sib_ref, *refs):
    blocks, (acc_ref, give_ref, sums_ref) = refs[:-3], refs[-3:]
    shift = jnp.mean(blocks[0][...].astype(F32), axis=0, keepdims=True)
    held = jnp.concatenate([b[...] for b in blocks], axis=0)
    acc, give, first, second = add_blocks(own_ref, sib_ref, held, ids, shift, None)
    acc_ref[...] = acc
    give_ref[...] = give
    sums_ref[...] = jnp.concatenate([shift, first, second, jnp.zeros((5, shift.shape[1]), F32)], axis=0)


def next_kernel(ids, own_ref, sib_ref, acc_in_ref, give_in_ref, sums_in_ref, *refs):
    blocks, (acc_ref, give_ref, sums_ref) = refs[:-3], refs[-3:]
    shift, first, second = sums_in_ref[0:1, :], sums_in_ref[1:2, :], sums_in_ref[2:3, :]
    held = jnp.concatenate([b[...] for b in blocks], axis=0)
    acc, give, first, second = add_blocks(own_ref, sib_ref, held, ids, shift, (first, second))
    acc_ref[...] = acc_in_ref[...] + acc
    give_ref[...] = (give_in_ref[...] + give).astype(give_ref.dtype)
    sums_ref[...] = jnp.concatenate([shift, first, second, jnp.zeros((5, shift.shape[1]), F32)], axis=0)


def pairs_kernel(ids, own_ref, sib_ref, acc_in_ref, shift_ref, *refs):
    blocks, (acc_ref, sums_ref) = refs[:-2], refs[-2:]
    held = jnp.concatenate([b[...] for b in blocks], axis=0)
    pick = [ref[:, d * LANE : (d + 1) * LANE] for ref in (own_ref, sib_ref) for d in ids]
    acc_ref[...] = acc_in_ref[...] + dot(jnp.concatenate(pick, axis=1), held, ((1,), (0,)))
    shift = shift_ref[0:1, :]
    away = held.astype(F32) - shift
    first = jnp.sum(away, axis=0, keepdims=True)
    second = jnp.sum(away * away, axis=0, keepdims=True)
    sums_ref[...] = jnp.concatenate([shift, first, second, jnp.zeros((5, shift.shape[1]), F32)], axis=0)


def pack_kernel(*refs):
    refs[-1][...] = jnp.concatenate([ref[...] for ref in refs[:-1]], axis=0)


def forward_kernel(marks_ref, acc_ref, got_ref, sums_ref, sib_sums_ref, pair_sums_ref, gain_sum_ref, mix_ref, head_ref, x_ref, own_ref, sib_ref, *refs):
    blocks, (pre_ref, hidden_ref, stats_ref, keep_ref, give_ref) = refs[:-5], refs[-5:]
    held = jnp.concatenate([b[...] for b in blocks], axis=0)
    at = slice(CHIPS // 2 * LANE, (CHIPS // 2 + 1) * LANE)
    acc = dot(jnp.concatenate([own_ref[:, at], sib_ref[:, at]], axis=1), held, ((1,), (0,)))
    shift = sums_ref[0:1, :]
    away = held.astype(F32) - shift
    sets = [(held.shape[0], shift, jnp.sum(away, axis=0, keepdims=True), jnp.sum(away * away, axis=0, keepdims=True))]
    sets += [(count * LANE, ref[0:1, :], ref[1:2, :], ref[2:3, :]) for count, ref in ((5, sums_ref), (5, sib_sums_ref), (4, pair_sums_ref))]
    means = [base + first / count for count, base, first, _ in sets]
    channels = 2 * CHIPS * LANE
    tok_mean = sum(s[0] * mean for s, mean in zip(sets, means)) / channels
    spread = sum(second - first * first / count + count * (mean - tok_mean) ** 2 for (count, _, first, second), mean in zip(sets, means))
    inv_std = lax.rsqrt(spread / channels + norm_eps)
    stats_ref[...] = jnp.concatenate([tok_mean, inv_std, jnp.zeros((6, tok_mean.shape[1]), F32)], axis=0)
    pre_act = (acc + acc_ref[...] + got_ref[...].astype(F32) - gain_sum_ref[...] * tok_mean) * inv_std
    pre_ref[...] = pre_act
    hidden = (pre_act * (0.5 * (1.0 + lax.erf(pre_act * 0.7071067811865476)))).astype(BF)
    hidden_ref[...] = hidden
    logits = dot(mix_ref[...], hidden, ((0,), (0,))) + dot(head_ref[...], x_ref[...], ((1,), (0,)))
    chunks = keep_ref.shape[0]
    core = jnp.broadcast_to(marks_ref[0:1, :], keep_ref.shape[1:]) == 1
    for g in range(chunks):
        low, high = logits[:, g * LANE : (g + 1) * LANE], logits[:, (chunks + g) * LANE : (chunks + g + 1) * LANE]
        keep_ref[g] = jnp.where(core, high, low)
        give_ref[g] = jnp.where(core, low, high)


def slope_kernel(pre_ref, stats_ref, slope_ref):
    pre_act = pre_ref[...]
    cum_prob = 0.5 * (1.0 + lax.erf(pre_act * 0.7071067811865476))
    density = jnp.exp(-0.5 * pre_act * pre_act) * 0.3989422804014327
    slope_ref[...] = (cum_prob + pre_act * density) * stats_ref[1:2, :]


def pick(marks_ref, y, z, chunks):
    size = chunks[0].shape
    bit_y = jnp.broadcast_to(marks_ref[1:2, :], size) != y
    bit_z = jnp.broadcast_to(marks_ref[2:3, :], size) != z
    return jnp.where(bit_y, jnp.where(bit_z, chunks[3], chunks[2]), jnp.where(bit_z, chunks[1], chunks[0]))


def fold_kernel(marks_ref, keep_ref, got_ref, *outs):
    chunks = [keep_ref[g] + got_ref[g] for g in range(4)]
    for out, (y, z) in zip(outs, ((0, 0), (1, 0), (0, 1), (1, 1))):
        out[...] = pick(marks_ref, y, z, chunks)


def add_kernel(*refs):
    refs[-1][...] = sum(ref[...] for ref in refs[:-1])


def softmax_kernel(classes, marks_ref, kept_ref, got_ref, labels_ref, grad_ref):
    kept = kept_ref[...] + got_ref[...]
    chunk = 4 * marks_ref[0:1, :] + 2 * marks_ref[1:2, :] + marks_ref[2:3, :]
    labels = labels_ref[:, :LANE]
    for g in range(1, labels_ref.shape[1] // LANE):
        labels = jnp.where(chunk == g, labels_ref[:, g * LANE : (g + 1) * LANE], labels)
    class_id = lax.broadcasted_iota(jnp.int32, kept.shape, 0)
    kept = jnp.where(class_id < classes, kept, -jnp.inf)
    col_max = jnp.max(kept, axis=0, keepdims=True)
    exp_terms = jnp.exp(kept - col_max)
    exp_total = jnp.sum(exp_terms, axis=0, keepdims=True)
    onehot = class_id == labels
    picked = jnp.sum(jnp.where(onehot, kept, 0.0), axis=0, keepdims=True)
    loss = jnp.log(exp_total) + col_max - picked
    loss_high = loss.astype(BF).astype(F32)
    grad = exp_terms / exp_total - onehot.astype(F32)
    grad = jnp.where(class_id == classes, loss_high, jnp.where(class_id == classes + 1, loss - loss_high, grad))
    grad_ref[...] = grad.astype(BF)


def join_kernel(marks_ref, own_ref, y_ref, z_ref, both_ref, out_ref):
    chunks = [ref[...].astype(F32) for ref in (own_ref, z_ref, y_ref, both_ref)]
    for g in range(4):
        out_ref[g] = pick(marks_ref, g // 2, g % 2, chunks).astype(BF)


def grad_kernel(marks_ref, own_ref, sib_ref, mix_ref, slope_ref, grad_ref, scaled_ref):
    chunks = own_ref.shape[0]
    core = jnp.broadcast_to(marks_ref[0:1, :], own_ref.shape[1:]) == 1
    for g in range(chunks):
        own, sib = own_ref[g].astype(F32), sib_ref[g].astype(F32)
        grad_ref[:, g * LANE : (g + 1) * LANE] = jnp.where(core, sib, own).astype(BF)
        grad_ref[:, (chunks + g) * LANE : (chunks + g + 1) * LANE] = jnp.where(core, own, sib).astype(BF)
    scaled_ref[...] = (dot(mix_ref[...], grad_ref[...], ((1,), (0,))) * slope_ref[...]).astype(BF)


def branch_kernel(hidden_ref, grad_ref, w_out_ref, scaled_ref, pre_ref, gain_sum_ref, mixed_ref, give_ref, means_ref):
    mixed = dot(hidden_ref[...], grad_ref[...], ((1,), (1,))).astype(BF)
    mixed_ref[...] = mixed
    width = give_ref.shape[1]
    wide = scaled_ref[...].astype(F32)
    mean_part = jnp.sum(wide * gain_sum_ref[...], axis=0, keepdims=True)
    proj_part = jnp.sum(wide * pre_ref[...], axis=0, keepdims=True)
    means = jnp.concatenate([mean_part, proj_part, jnp.zeros((SUB_ROWS - 2, wide.shape[1]), F32)], axis=0)
    means_ref[...] = means
    give_ref[...] = jnp.concatenate([dot(mixed, w_out_ref[:, width:], ((0,), (0,))), means], axis=0).astype(BF)


def own_branch_kernel(mixed_ref, w_out_ref, means_ref, keep_ref):
    width = keep_ref.shape[1]
    keep_ref[...] = jnp.concatenate([dot(mixed_ref[...], w_out_ref[:, :width], ((0,), (0,))), means_ref[...]], axis=0)


def message_of(d, turned_ref, own_ref, got_ref, keep_ref, sib_ref):
    units = own_ref.shape[0]
    at = slice(d * LANE, (d + 1) * LANE)
    rows = dot(turned_ref[at, :units], own_ref[...], ((1,), (0,))) + dot(turned_ref[at, units:], got_ref[...], ((1,), (0,)))
    means = keep_ref[CLASS_ROWS:, :] + sib_ref[CLASS_ROWS:, :].astype(F32)
    means = [means[n : n + 1, g * LANE : (g + 1) * LANE] for n in range(2) for g in range(8)]
    means = jnp.concatenate(means + [jnp.zeros((EXTRA - 16, LANE), F32)], axis=0)
    branch = keep_ref[:CLASS_ROWS, at] + sib_ref[:CLASS_ROWS, at].astype(F32)
    branch = jnp.concatenate([branch, jnp.zeros((7 * EXTRA - CLASS_ROWS, LANE), F32)], axis=0)
    extra = jnp.concatenate([means] + [branch[g * EXTRA : (g + 1) * EXTRA] for g in range(7)], axis=1)
    return jnp.concatenate([rows, extra], axis=0)


def message_kernel(ids, *refs):
    for d, out in zip(ids, refs[-len(ids) :]):
        out[...] = message_of(d, *refs[: -len(ids)])


def far_kernel(*refs):
    upper, lower = refs[-2:]
    cut = upper.shape[0]
    total = message_of(CHIPS // 2, *refs[:-2])
    upper[...] = total[:cut].astype(BF)
    lower[...] = total[cut:].astype(BF)


def sum_kernel(begin, own_ref, got_ref, *outs):
    own, got = own_ref[...], got_ref[...].astype(F32)
    end = begin + got.shape[0]
    pieces = [own[:begin]] * (begin > 0) + [own[begin:end] + got] + [own[end:]] * (end < own.shape[0])
    total = jnp.concatenate(pieces, axis=0) if len(pieces) > 1 else pieces[0]
    for n, out in enumerate(outs):
        width = out.shape[1]
        out[...] = total[:, n * width : (n + 1) * width].astype(BF)


def d_w_out_kernel(mixed_ref, head_ref, scale_ref, out_ref, done_ref, held, sems):
    done_ref[...] = jnp.zeros_like(done_ref)
    mixed = mixed_ref[...]
    copies = []
    for n in range(sems.shape[0]):
        at = slice(n * held.shape[1] // sems.shape[0], (n + 1) * held.shape[1] // sems.shape[0])
        held[:, at] = dot(mixed, head_ref[:, at], ((1,), (0,))) * scale_ref[:, at]
        copies.append(pltpu.make_async_copy(held.at[:, at], out_ref.at[:, at], sems.at[n]))
        copies[-1].start()
    for copy in copies:
        copy.wait()


def d_w_in_kernel(places_ref, gain_ref, scaled_ref, stats_ref, own_ref, sib_ref, out_ref, done_ref, held, sems):
    done_ref[...] = jnp.zeros_like(done_ref)
    scaled = scaled_ref[...]
    shift = jnp.sum(scaled.astype(F32) * stats_ref[0:1, :], axis=1, keepdims=True)
    copies = []
    for side, blocks in enumerate((own_ref, sib_ref)):
        for n in range(0, CHIPS, 2):
            both = dot(scaled, blocks[n * LANE : (n + 2) * LANE, :], ((1,), (1,))) - shift
            for k in range(2):
                at = columns(places_ref, 2 * (n + k) + side)
                slot = len(copies)
                held[slot] = both[:, k * LANE : (k + 1) * LANE] * gain_ref[:, at]
                copies.append(pltpu.make_async_copy(held.at[slot], out_ref.at[:, at], sems.at[slot]))
                copies[-1].start()
    for copy in copies:
        copy.wait()


def head_kernel(classes, x_ref, head_ref, grad_ref, out_grad_ref, d_head_ref, loss_ref):
    grad = grad_ref[...]
    out_grad_ref[...] = dot(head_ref[...], grad, ((0,), (0,)))
    d_head_ref[...] = dot(grad, x_ref[...], ((1,), (1,)))
    loss_ref[...] = (jnp.sum(grad[classes : classes + 2].astype(F32)) / grad.shape[1]).reshape(1, 1)


def put_conv_grad(groups, got, means_rows, conv_ref, stats_ref, grid_pad):
    rows = conv_ref.shape[0]
    channels = rows * 2 * CHIPS
    for n, g in enumerate(groups):
        at = slice(g * LANE, (g + 1) * LANE)
        normed = (conv_ref[:, at].astype(F32) - stats_ref[0:1, at]) * stats_ref[1:2, at]
        conv_grad = got[:rows, n * LANE : (n + 1) * LANE] - (means_rows[g : g + 1, :] + normed * means_rows[8 + g : 9 + g, :]) * (1.0 / channels)
        put_rows(grid_pad, 4 * g, conv_grad)


def add_taps(groups, copies, copies_x, sums):
    for g in groups:
        conv_grad = copies[HALF, pl.ds(4 * g + HALF, 4)]
        for j in range(KS):
            for i in range(KS):
                prod = (conv_grad * copies_x[j, pl.ds(4 * g + i, 4)]).reshape(16, 8, LANE)
                index = i * KS + j
                total = jnp.sum(prod, axis=0)
                if g == 0:
                    sums[index] = total
                else:
                    sums[index] += total


def copy_rows(begin, end, grid_pad, copies):
    rows = pl.ds(begin, end - begin)
    for j in range(KS):
        copies[j, rows] = grid_pad[rows, pl.ds(8 + j - HALF, WIN_W), :]


def upper_kernel(mine_ref, forth_ref, back_ref, conv_ref, stats_ref, taps, copies_x, out_grad_ref,
                 d_x_ref, sums, grid_pad, extra_ref, copies):
    rows = conv_ref.shape[0]
    width = forth_ref.shape[1]
    got = mine_ref[:, :width] + forth_ref[...].astype(F32) + back_ref[...].astype(F32)
    extra_ref[...] = got[rows:]
    clear_border(grid_pad)
    put_conv_grad(range(4), got, got[rows:, :LANE], conv_ref, stats_ref, grid_pad)
    copy_rows(0, 16 + HALF, grid_pad, copies)
    for g in range(3):
        at = slice(g * LANE, (g + 1) * LANE)
        d_x_ref[:, at] = out_grad_ref[:, at] + conv_rows(copies, taps, 4 * g, True).reshape(LANE, LANE).T
    add_taps(range(4), copies, copies_x, sums)


def lower_kernel(classes, mine_ref, forth_ref, back_ref, conv_ref, stats_ref, taps, copies_x, out_grad_ref, head_grad_ref, head_ref, scale_ref,
                 d_upper_ref, sums_ref, grid_ref, extra_ref, d_x_ref, d_dw_ref, d_scale_ref, d_head_ref, grid_pad, copies, sums):
    rows = conv_ref.shape[0]
    width = forth_ref.shape[1]
    got = mine_ref[:, width:] + forth_ref[...].astype(F32) + back_ref[...].astype(F32)
    extra = jnp.concatenate([extra_ref[...], got[rows:]], axis=1)
    branch = jnp.concatenate([extra[:, g * LANE : (g + 1) * LANE] for g in range(1, 8)], axis=0)[:CLASS_ROWS]
    sums[...] = sums_ref[...]
    grid_pad[...] = grid_ref[...]
    put_conv_grad(range(4, 8), got, extra[:, :LANE], conv_ref, stats_ref, grid_pad)
    copy_rows(12, WIN_H + 2 * HALF, grid_pad, copies)
    d_x_ref[:, : 3 * LANE] = d_upper_ref[...]
    for g in range(3, 8):
        at = slice(g * LANE, (g + 1) * LANE)
        d_x_ref[:, at] = out_grad_ref[:, at] + conv_rows(copies, taps, 4 * g, True).reshape(LANE, LANE).T
    add_taps(range(4, 8), copies, copies_x, sums)
    d_dw_ref[...] = jnp.sum(sums[...], axis=1)
    d_scale_ref[...] = jnp.sum(head_ref[...].astype(F32) * branch, axis=0, keepdims=True)
    d_head_ref[...] = (head_grad_ref[...] + scale_ref[...] * branch)[:classes]


def walk_step(walk, step):
    forth, back = walk[(1 - step) % CHIPS][0], walk[step - 1][0]
    half = forth.shape[0] // 2
    if step < CHIPS // 2:
        walk[(-step) % CHIPS], walk[step] = (send(forth, FORTH),), (send(back, BACK),)
    else:
        walk[step] = (send(forth[:half], FORTH), send(back[half:], BACK))


def hold(walk, step, *others):
    spots = [(-step) % CHIPS, step]
    held = lax.optimization_barrier((walk[spots[0]][0], walk[spots[1]][0], *others))
    walk[spots[0]], walk[spots[1]] = (held[0],), (held[1],)
    return held[2:]


def per_device(features, dw_weight, norm_gain, layer_scale, w_in, w_out, w_head, labels):
    rows, tokens = features.shape
    units, channels = w_in.shape
    classes = w_head.shape[1]
    me = lax.axis_index("ch")
    places = lax.dynamic_index_in_dim(jnp.asarray(PLACES), me, 0, keepdims=False)
    marks = lax.dynamic_index_in_dim(jnp.asarray(MARKS), me, 0, keepdims=False)
    taps = dw_weight.T
    scale_row, gain_row, labels_row = layer_scale[None, :], norm_gain[None, :], labels[None, :]
    grid_shape = pltpu.VMEM((WIN_H + 2 * HALF, WIN_W + 16, LANE), F32)
    copies_size = (KS, WIN_H + 2 * HALF, WIN_W, LANE)
    half_channels = CHIPS * rows
    vm = lambda *arrays: [(a, VMEM) for a in arrays]
    spot, mark = [(places, SMEM)], vm(marks)
    f32s, bf16s, sums_size = ((units, tokens), F32), ((units, tokens), BF), ((8, tokens), F32)

    conv_out, features, taps = call(
        conv_kernel, [((rows, tokens), BF), ((rows, tokens), BF), ((KS * KS, rows), F32)], [(features, HBM), (taps, HBM)],
        [grid_shape, pltpu.VMEM(copies_size, F32), pltpu.SemaphoreType.DMA((2,))],
        limit=12, name="conv_forward",
    )
    walk = {0: (conv_out,)}
    walk_step(walk, 1)
    w_own, w_give, gain_sum = call(
        weights_kernel,
        [((units, half_channels), BF), ((units, half_channels), BF), ((units, 1), F32)],
        spot + vm(w_in, gain_row), flops=4e8, moved=4e6, limit=12, name="weights_ready", after=[conv_out, marks],
    )
    w_own, w_give, gain_sum = hold(walk, 1, w_own, w_give, gain_sum)
    w_sib = send(w_give, SIBLING)
    walk_step(walk, 2)
    so_far = call(
        functools.partial(first_kernel, (0, 1, 7)), [f32s, f32s, sums_size],
        vm(w_own, w_sib, *walk[0], *walk[1], *walk[7]), flops=1e9, moved=4e6, limit=16, name="forward_first",
    )
    so_far = hold(walk, 2, *so_far)
    walk_step(walk, 3)
    made = call(
        mix_kernel,
        [((CLASS_ROWS, channels), BF), ((units, CLASS_ROWS), BF), ((units, channels), BF), ((CLASS_ROWS, rows), BF), ((1, rows), F32)],
        spot + vm(w_out, scale_row, w_head.T), flops=1e9, moved=4e6, limit=12, name="mix_ready", after=[so_far[2]],
    )
    so_far = call(
        functools.partial(next_kernel, (2, 6)), [f32s, bf16s, sums_size],
        vm(w_own, w_sib, *so_far, *walk[2], *walk[6]), flops=6e8, moved=4e6, limit=16, name="forward_next",
    )
    *so_far, head_pad, mix, w_out_walk, my_head, my_scale = hold(walk, 3, *so_far, *made)
    acc, give, sums = so_far
    got, sib_sums = send(give, SIBLING), send(sums, SIBLING)
    walk_step(walk, 4)
    acc, pair_sums = call(
        functools.partial(pairs_kernel, (3, 5)), [f32s, sums_size],
        vm(w_own, w_give, acc, sums, *walk[3], *walk[5], send(walk[3][0], SIBLING), send(walk[5][0], SIBLING)),
        flops=1e9, moved=4e6, limit=16, name="forward_pairs",
    )
    upper, acc, pair_sums = lax.optimization_barrier((walk[4][0], acc, pair_sums))
    walk[4] = (upper, walk[4][1])
    far = [*walk[4], *[send(b, SIBLING) for b in walk[4]]]
    chunks = tokens // LANE // 2
    chunk = lambda count, kind=F32: ((count, CLASS_ROWS, LANE), kind)
    pre_act, hidden, stats, keep, give = call(
        forward_kernel, [f32s, bf16s, sums_size, chunk(chunks), chunk(chunks)],
        mark + vm(acc, got, sums, sib_sums, pair_sums, gain_sum, mix, my_head, features, w_own, w_give, *far),
        flops=1e9, moved=4e6, limit=16, name="forward_hidden",
    )

    own_chunk = ((CLASS_ROWS, LANE), F32)
    others = (2, 4, 6)
    kept, *gives = call(fold_kernel, [own_chunk] * 4, mark + vm(keep, send(give, SIBLING)), limit=4, name="fold_core")
    (packed,) = call(
        pack_kernel, [((half_channels, tokens), BF)], vm(*[b for d in range(CHIPS) for b in walk[d]]), flops=4e8, moved=4e6, limit=10, name="pack_blocks", after=[kept],
    )
    sib_packed = send(packed, SIBLING)
    (slope,) = call(slope_kernel, [f32s], vm(pre_act, stats), flops=5e8, moved=4e6, limit=8, name="gelu_slope", after=[packed])
    (kept,) = call(
        add_kernel, [own_chunk], vm(kept, *[send(part, flip_perm(bits)) for part, bits in zip(gives, others)]), limit=4, name="fold_chips", after=[slope],
    )
    (turned,) = call(turn_kernel, [((half_channels, 2 * units), BF)], vm(w_own, w_sib), flops=4e8, moved=4e6, limit=10, name="weights_turned", after=[kept])
    (grad,) = call(
        functools.partial(softmax_kernel, classes), [((CLASS_ROWS, LANE), BF)], mark + vm(kept, send(kept, flip_perm(8)), labels_row), limit=4, name="class_grad", after=[turned, sib_packed],
    )
    (copies_x,) = call(copies_kernel, [(copies_size, F32)], vm(features), [grid_shape], flops=4e8, moved=4e6, limit=12, name="window_copies", after=[grad])
    (grad,) = call(
        join_kernel, [((chunks, CLASS_ROWS, LANE), BF)], mark + vm(grad, *[send(grad, flip_perm(bits)) for bits in others]), limit=4, name="join_chips", after=[copies_x],
    )

    grad, scaled = call(
        grad_kernel, [((CLASS_ROWS, tokens), BF), bf16s], mark + vm(grad, send(grad, SIBLING), mix, slope), flops=6e8, moved=4e6, limit=12, name="hidden_grad",
    )
    got = send(scaled, SIBLING)
    extra_rows = CLASS_ROWS + SUB_ROWS
    mixed, give, means = call(
        branch_kernel, [((units, CLASS_ROWS), BF), ((extra_rows, half_channels), BF), ((SUB_ROWS, tokens), F32)],
        vm(hidden, grad, w_out_walk, scaled, pre_act, gain_sum), flops=8e8, moved=4e6, limit=12, name="class_products",
    )
    (keep,) = call(
        own_branch_kernel, [((extra_rows, half_channels), F32)], vm(mixed, w_out_walk, means), flops=4e8, moved=4e6, limit=8, name="class_products_own",
    )
    sources = vm(turned, scaled, got, keep, send(give, SIBLING))
    height = rows + EXTRA
    cut = 80
    forth, back = call(far_kernel, [((cut, tokens), BF), ((height - cut, tokens), BF)], sources, flops=3e8, moved=2e6, limit=8, name="message_far")
    forth, back = send(forth, FORTH), send(back, BACK)
    d_w_out, d_w_out_done = call(
        d_w_out_kernel, [((units, channels), F32), ((8, LANE), F32)], vm(mixed, head_pad, scale_row),
        [pltpu.VMEM((units, channels), F32), pltpu.SemaphoreType.DMA((4,))], flops=1e9, moved=8e6, limit=12, name="d_w_out", out_spaces=(pl.ANY, pltpu.VMEM),
        after=[forth],
    )
    out_grad, head_grad, mean_loss = call(
        functools.partial(head_kernel, classes), [((rows, tokens), F32), ((CLASS_ROWS, rows), F32), ((1, 1), F32)],
        vm(features, my_head, grad), flops=4e8, moved=2e6, limit=8, name="class_head", after=[forth],
    )
    beside = {3: [], 2: [d_w_out_done, out_grad], 1: []}
    for step in range(CHIPS // 2 - 1, 0, -1):
        ahead, behind = call(
            functools.partial(message_kernel, (step, CHIPS - step)), [((height, tokens), F32)] * 2, sources,
            flops=6e8, moved=2e6, limit=8, name="messages",
        )
        first = step == CHIPS // 2 - 1
        parts = 2 if step == 1 else 1
        add = lambda begin, own, got, waits: call(
            functools.partial(sum_kernel, begin), [((height, tokens // parts), BF)] * parts, vm(own, got), limit=6, name="walk_sum", after=waits,
        )
        forth, back = add(0, ahead, forth, []), add(cut if first else 0, behind, back, beside[step])
        if step == 1:
            continue
        (forth,), (back,) = forth, back
        if step == 2:
            d_w_in, d_w_in_done = call(
                d_w_in_kernel, [((units, channels), F32), ((8, LANE), F32)], spot + vm(gain_row, scaled, stats, packed, sib_packed),
                [pltpu.VMEM((2 * CHIPS, units, LANE), F32), pltpu.SemaphoreType.DMA((2 * CHIPS,))],
                flops=2e9, moved=8e6, limit=12, name="d_w_in", out_spaces=(pl.ANY, pltpu.VMEM), after=[forth, back],
            )
            beside[1] = [d_w_in_done]
        forth, back = send(forth, FORTH), send(back, BACK)
    (mine,) = call(functools.partial(message_kernel, (0,)), [((height, tokens), F32)], sources, flops=3e8, moved=2e6, limit=8, name="messages", after=[ahead])
    ends = [(send(forth[n], FORTH), send(back[n], BACK)) for n in range(2)]
    upper = call(
        upper_kernel,
        [((rows, 3 * LANE), F32), ((KS * KS, 8, LANE), F32), (grid_shape.shape, F32), ((EXTRA, tokens // 2), F32)],
        vm(mine, *ends[0], conv_out, stats, taps, copies_x, out_grad), [pltpu.VMEM(copies_size, F32)],
        flops=4e8, moved=2e6, limit=16, name="conv_backward_upper",
    )
    d_features, d_dw, d_scale, d_head = call(
        functools.partial(lower_kernel, classes),
        [((rows, tokens), F32), ((KS * KS, rows), F32), ((1, rows), F32), ((classes, rows), F32)],
        vm(mine, *ends[1], conv_out, stats, taps, copies_x, out_grad, head_grad, my_head, my_scale, *upper),
        [grid_shape, pltpu.VMEM(copies_size, F32), pltpu.VMEM((KS * KS, 8, LANE), F32)], limit=16, name="conv_backward_lower",
    )
    return (d_features, d_dw.T, d_scale[0], d_w_in, d_w_out, d_head.T, mean_loss[0])


def conv_apply(in_grid, kernel):
    half = KS // 2
    padded = jnp.pad(in_grid, ((0, 0), (half, half), (half, half)))
    running = jnp.zeros(in_grid.shape, in_grid.dtype)
    for row_shift in range(KS):
        for col_shift in range(KS):
            tap = kernel[:, row_shift * KS + col_shift]
            running = (
                running
                + tap[:, None, None]
                * padded[:, row_shift : row_shift + WIN_H, col_shift : col_shift + WIN_W]
            )
    return running


def gelu_parts(values):
    cum_prob = 0.5 * (1.0 + lax.erf(values * 0.7071067811865476))
    density = jnp.exp(-0.5 * values * values) * 0.3989422804014327
    return (values * cum_prob, cum_prob + values * density)


def plain_device(features, dw_weight, norm_gain, layer_scale, w_in, w_out, w_head, labels):
    highest = lax.Precision.HIGHEST
    my_rows = features.shape[0]
    tok_count = features.shape[1]
    class_count = w_head.shape[1]
    row_offset = lax.axis_index("ch") * my_rows
    inputs_wide = features.astype(jnp.float32)
    in_grid = inputs_wide.reshape(my_rows, WIN_H, WIN_W)
    conv_out = conv_apply(in_grid, dw_weight).reshape(my_rows, tok_count).astype(jnp.bfloat16)
    conv_all = lax.all_gather(conv_out, "ch", axis=0, tiled=True)
    conv_wide = conv_all.astype(jnp.float32)
    tok_mean = jnp.mean(conv_wide, axis=0)
    centered = conv_wide - tok_mean[None, :]
    tok_var = jnp.mean(centered * centered, axis=0)
    inv_std = 1.0 / jnp.sqrt(tok_var + norm_eps)
    normed = centered * inv_std[None, :]
    norm_out = (norm_gain[:, None] * normed).astype(jnp.bfloat16)
    pre_act = jnp.dot(w_in, norm_out, preferred_element_type=jnp.float32)
    gelu_out, gelu_slope = gelu_parts(pre_act)
    hidden = gelu_out.astype(jnp.bfloat16)
    my_scale = lax.dynamic_slice_in_dim(layer_scale, row_offset, my_rows, 0)
    head_wide = w_head.astype(jnp.float32)
    my_head = lax.dynamic_slice_in_dim(head_wide, row_offset, my_rows, 0)
    w_cols = w_out
    branch_sum = lax.psum_scatter(
        lax.dot_general(
            w_cols, hidden, (((0,), (0,)), ((), ())), preferred_element_type=jnp.float32
        ),
        "ch",
        scatter_dimension=0,
        tiled=True,
    )
    block_out = inputs_wide + my_scale[:, None] * branch_sum
    part_logits = lax.dot_general(block_out, my_head, (((0,), (0,)), ((), ())), precision=highest)
    logits = lax.psum(part_logits, "ch")
    row_max = jnp.max(logits, axis=1, keepdims=True)
    exp_terms = jnp.exp(logits - row_max)
    exp_total = jnp.sum(exp_terms, axis=1, keepdims=True)
    log_total = jnp.log(exp_total) + row_max
    onehot = (labels[:, None] == jnp.arange(class_count, dtype=jnp.int32)[None, :]).astype(
        jnp.float32
    )
    picked = jnp.sum(logits * onehot, axis=1)
    mean_loss = jnp.mean(log_total[:, 0] - picked).reshape(1)
    logit_grad = exp_terms / exp_total - onehot
    out_grad = lax.dot_general(my_head, logit_grad, (((1,), (1,)), ((), ())), precision=highest)
    d_head = jnp.dot(block_out, logit_grad, precision=highest)
    d_scale = jnp.sum(out_grad * branch_sum, axis=1)
    branch_grad = (my_scale[:, None] * out_grad).astype(jnp.bfloat16)
    incoming = lax.all_gather(branch_grad, "ch", axis=0, tiled=True)
    hidden_acc = jnp.dot(w_cols, incoming, preferred_element_type=jnp.float32)
    tile_grad = lax.dot_general(
        hidden, incoming, (((1,), (1,)), ((), ())), preferred_element_type=jnp.float32
    )
    pre_grad = (hidden_acc * gelu_slope).astype(jnp.bfloat16)
    d_w_in = lax.dot_general(
        pre_grad, norm_out, (((1,), (1,)), ((), ())), preferred_element_type=jnp.float32
    )
    norm_grad = lax.dot_general(
        w_in, pre_grad, (((0,), (0,)), ((), ())), preferred_element_type=jnp.float32
    )
    gained = norm_gain[:, None] * norm_grad
    conv_term = (
        gained
        - jnp.mean(gained, axis=0)[None, :]
        - normed * jnp.mean(gained * normed, axis=0)[None, :]
    ) * inv_std[None, :]
    conv_grad = lax.psum_scatter(conv_term, "ch", scatter_dimension=0, tiled=True)
    unused, pullback = jax.vjp(conv_apply, in_grid, dw_weight)
    grid_grad, d_dw = pullback(conv_grad.reshape(my_rows, WIN_H, WIN_W))
    d_features = out_grad + grid_grad.reshape(my_rows, tok_count)
    return (d_features, d_dw, d_scale, d_w_in, tile_grad, d_head, mean_loss)


def solution(mesh):
    placed = (P("ch", "grp"), P("ch", None), P(), P(), P("ch", None), P("ch", None), P(), P("grp"))
    return jax.shard_map(
        per_device if mesh.shape["ch"] == 2 * CHIPS else plain_device,
        mesh=mesh,
        in_specs=placed,
        out_specs=(
            P("ch", "grp"),
            P("ch", "grp"),
            P(("grp", "ch")),
            P(("grp", "ch"), None),
            P(("grp", "ch"), None),
            P("ch", "grp"),
            P("grp"),
        ),
        check_vma=False,
    )
```

```python
import functools

import jax
import jax.numpy as jnp
import numpy as np
from jax import lax
from jax.experimental import pallas as pl
from jax.experimental.pallas import tpu as pltpu
from jax.sharding import PartitionSpec as P

KS = 7
HALF = KS // 2
WIN_H = 32
WIN_W = 32
norm_eps = 1e-06
BF = jnp.bfloat16
F32 = jnp.float32

WALK = (0, 2, 4, 6, 7, 5, 3, 1)
CHIPS = len(WALK)
CORES = 2
REL = np.array([[WALK[(WALK.index(chip) + d) % CHIPS] for d in range(CHIPS)] for chip in range(CHIPS)], np.int32)
PLACES = np.array(
    [
        [REL[dev // 2][d] * 2 + (dev % 2 ^ side) for d in range(CHIPS) for side in range(2)] + [dev % 2, dev]
        for dev in range(2 * CHIPS)
    ],
    np.int32,
)
CORE, MINE = 2 * CHIPS, 2 * CHIPS + 1
MARKS = np.broadcast_to(
    np.array([[dev >> bit & 1 for bit in range(8)] for dev in range(2 * CHIPS)], np.int32)[:, :, None], (2 * CHIPS, 8, 128)
)
CLASS_ROWS = 160
EXTRA = 24
SUB_ROWS = 16
LANE = 128


def walk_perm(step):
    return [
        (WALK[p] * 2 + c, WALK[(p + step) % CHIPS] * 2 + c) for p in range(CHIPS) for c in range(2)
    ]


def flip_perm(bit):
    return [(i, i ^ bit) for i in range(2 * CHIPS)]


def send(value, perm):
    return lax.ppermute(value, "ch", perm)


FORTH, BACK, SIBLING = walk_perm(1), walk_perm(-1), flip_perm(1)
VMEM = pl.BlockSpec(memory_space=pltpu.VMEM)
SMEM = pl.BlockSpec(memory_space=pltpu.SMEM)
HBM = pl.BlockSpec(memory_space=pltpu.HBM)


def call(kernel, outs, ins, scratch=(), flops=0, moved=0, limit=40, name=None, after=(), out_spaces=None):
    count = len(ins)

    def body(*refs):
        kernel(*refs[:count], *refs[count + len(after) :])

    result = pl.pallas_call(
        body,
        out_shape=[jax.ShapeDtypeStruct(s, d) for s, d in outs],
        in_specs=[s for _, s in ins] + [pl.BlockSpec(memory_space=pl.ANY)] * len(after),
        out_specs=[pl.BlockSpec(memory_space=space) for space in out_spaces or [pltpu.VMEM] * len(outs)],
        scratch_shapes=list(scratch),
        compiler_params=pltpu.CompilerParams(vmem_limit_bytes=limit << 20),
        cost_estimate=pl.CostEstimate(flops=int(flops), bytes_accessed=int(moved), transcendentals=0),
        name=name,
    )(*[a for a, _ in ins], *after)
    return result


def dot(a, b, dims):
    return lax.dot_general(a, b, (dims, ((), ())), preferred_element_type=F32)


def shifted_copies(grid_pad, copies):
    for j in range(KS):
        copies[j] = grid_pad[:, pl.ds(8 + j - HALF, WIN_W), :]


def clear_border(grid_pad):
    grid_pad[...] = jnp.zeros_like(grid_pad)


def put_rows(grid_pad, row, tile):
    grid_pad[pl.ds(row + HALF, 4), pl.ds(8, WIN_W), :] = tile.T.reshape(4, WIN_W, tile.shape[0])


def conv_rows(copies, taps, row, flip, count=4):
    acc = None
    for j in range(KS):
        for i in range(KS):
            index = (KS - 1 - i) * KS + KS - 1 - j if flip else i * KS + j
            term = taps[index : index + 1, :][None] * copies[j, pl.ds(row + i, count)]
            acc = term if acc is None else acc + term
    return acc


def conv_kernel(x_ref, taps, out_ref, grid_pad, copies):
    clear_border(grid_pad)
    for g in range(8):
        put_rows(grid_pad, 4 * g, x_ref[:, g * LANE : (g + 1) * LANE].astype(F32))
    shifted_copies(grid_pad, copies)
    for g in range(0, 8, 2):
        acc = conv_rows(copies, taps, 4 * g, False, 8).reshape(2 * LANE, LANE)
        for k in range(2):
            out_ref[:, (g + k) * LANE : (g + k + 1) * LANE] = acc[k * LANE : (k + 1) * LANE].T.astype(BF)


def copies_kernel(x_ref, copies, grid_pad):
    clear_border(grid_pad)
    for g in range(8):
        put_rows(grid_pad, 4 * g, x_ref[:, g * LANE : (g + 1) * LANE].astype(F32))
    shifted_copies(grid_pad, copies)


def columns(places_ref, entry):
    return pl.ds(pl.multiple_of(places_ref[entry] * LANE, LANE), LANE)


def weights_kernel(places_ref, w_in_ref, gain_ref, own_ref, sib_ref, gain_sum_ref):
    total = None
    for d in range(CHIPS):
        for side, out in enumerate((own_ref, sib_ref)):
            at = columns(places_ref, 2 * d + side)
            part = (w_in_ref[:, at].astype(F32) * gain_ref[:, at]).astype(BF)
            out[:, d * LANE : (d + 1) * LANE] = part
            wide = part.astype(F32)
            total = wide if total is None else total + wide
    gain_sum_ref[...] = jnp.sum(total, axis=1, keepdims=True)


def mix_kernel(places_ref, w_out_ref, scale_ref, head_ref, head_pad_ref, mix_ref, walk_ref, my_head_ref, my_scale_ref):
    for d in range(CHIPS):
        for side in range(2):
            walk_ref[:, (side * CHIPS + d) * LANE : (side * CHIPS + d + 1) * LANE] = w_out_ref[:, columns(places_ref, 2 * d + side)]
    head_pad_ref[...] = jnp.zeros_like(head_pad_ref)
    head_pad_ref[0 : head_ref.shape[0], :] = head_ref[...]
    head = head_pad_ref[...]
    scaled = (head.astype(F32) * scale_ref[...]).astype(BF)
    mix_ref[...] = dot(w_out_ref[...], scaled, ((1,), (1,))).astype(BF)
    my_head_ref[...] = head_pad_ref[:, columns(places_ref, MINE)]
    my_scale_ref[...] = scale_ref[:, columns(places_ref, MINE)]


def turn_kernel(own_ref, sib_ref, out_ref):
    units = own_ref.shape[0]
    out_ref[:, :units] = own_ref[...].T
    out_ref[:, units:] = sib_ref[...].T


def add_blocks(own_ref, sib_ref, held, ids, shift, sums):
    away = held.astype(F32) - shift
    first = jnp.sum(away, axis=0, keepdims=True)
    second = jnp.sum(away * away, axis=0, keepdims=True)
    if sums is not None:
        first, second = sums[0] + first, sums[1] + second
    pick = lambda ref: jnp.concatenate([ref[:, d * LANE : (d + 1) * LANE] for d in ids], axis=1)
    return dot(pick(own_ref), held, ((1,), (0,))), dot(pick(sib_ref), held, ((1,), (0,))), first, second


def first_kernel(ids, own_ref, sib_ref, *refs):
    blocks, (acc_ref, give_ref, sums_ref) = refs[:-3], refs[-3:]
    shift = jnp.mean(blocks[0][...].astype(F32), axis=0, keepdims=True)
    held = jnp.concatenate([b[...] for b in blocks], axis=0)
    acc, give, first, second = add_blocks(own_ref, sib_ref, held, ids, shift, None)
    acc_ref[...] = acc
    give_ref[...] = give
    sums_ref[...] = jnp.concatenate([shift, first, second, jnp.zeros((5, shift.shape[1]), F32)], axis=0)


def next_kernel(ids, own_ref, sib_ref, acc_in_ref, give_in_ref, sums_in_ref, *refs):
    blocks, (acc_ref, give_ref, sums_ref) = refs[:-3], refs[-3:]
    shift, first, second = sums_in_ref[0:1, :], sums_in_ref[1:2, :], sums_in_ref[2:3, :]
    held = jnp.concatenate([b[...] for b in blocks], axis=0)
    acc, give, first, second = add_blocks(own_ref, sib_ref, held, ids, shift, (first, second))
    acc_ref[...] = acc_in_ref[...] + acc
    give_ref[...] = (give_in_ref[...] + give).astype(give_ref.dtype)
    sums_ref[...] = jnp.concatenate([shift, first, second, jnp.zeros((5, shift.shape[1]), F32)], axis=0)


def pairs_kernel(ids, own_ref, sib_ref, acc_in_ref, shift_ref, *refs):
    blocks, (acc_ref, sums_ref) = refs[:-2], refs[-2:]
    held = jnp.concatenate([b[...] for b in blocks], axis=0)
    pick = [ref[:, d * LANE : (d + 1) * LANE] for ref in (own_ref, sib_ref) for d in ids]
    acc_ref[...] = acc_in_ref[...] + dot(jnp.concatenate(pick, axis=1), held, ((1,), (0,)))
    shift = shift_ref[0:1, :]
    away = held.astype(F32) - shift
    first = jnp.sum(away, axis=0, keepdims=True)
    second = jnp.sum(away * away, axis=0, keepdims=True)
    sums_ref[...] = jnp.concatenate([shift, first, second, jnp.zeros((5, shift.shape[1]), F32)], axis=0)


def pack_kernel(*refs):
    refs[-1][...] = jnp.concatenate([ref[...] for ref in refs[:-1]], axis=0)


def forward_kernel(marks_ref, acc_ref, got_ref, sums_ref, sib_sums_ref, pair_sums_ref, gain_sum_ref, mix_ref, head_ref, x_ref, own_ref, sib_ref, *refs):
    blocks, (pre_ref, hidden_ref, stats_ref, keep_ref, give_ref) = refs[:-5], refs[-5:]
    held = jnp.concatenate([b[...] for b in blocks], axis=0)
    at = slice(CHIPS // 2 * LANE, (CHIPS // 2 + 1) * LANE)
    acc = dot(jnp.concatenate([own_ref[:, at], sib_ref[:, at]], axis=1), held, ((1,), (0,)))
    shift = sums_ref[0:1, :]
    away = held.astype(F32) - shift
    sets = [(held.shape[0], shift, jnp.sum(away, axis=0, keepdims=True), jnp.sum(away * away, axis=0, keepdims=True))]
    sets += [(count * LANE, ref[0:1, :], ref[1:2, :], ref[2:3, :]) for count, ref in ((5, sums_ref), (5, sib_sums_ref), (4, pair_sums_ref))]
    means = [base + first / count for count, base, first, _ in sets]
    channels = 2 * CHIPS * LANE
    tok_mean = sum(s[0] * mean for s, mean in zip(sets, means)) / channels
    spread = sum(second - first * first / count + count * (mean - tok_mean) ** 2 for (count, _, first, second), mean in zip(sets, means))
    inv_std = lax.rsqrt(spread / channels + norm_eps)
    stats_ref[...] = jnp.concatenate([tok_mean, inv_std, jnp.zeros((6, tok_mean.shape[1]), F32)], axis=0)
    pre_act = (acc + acc_ref[...] + got_ref[...].astype(F32) - gain_sum_ref[...] * tok_mean) * inv_std
    pre_ref[...] = pre_act
    hidden = (pre_act * (0.5 * (1.0 + lax.erf(pre_act * 0.7071067811865476)))).astype(BF)
    hidden_ref[...] = hidden
    logits = dot(mix_ref[...], hidden, ((0,), (0,))) + dot(head_ref[...], x_ref[...], ((1,), (0,)))
    chunks = keep_ref.shape[0]
    core = jnp.broadcast_to(marks_ref[0:1, :], keep_ref.shape[1:]) == 1
    for g in range(chunks):
        low, high = logits[:, g * LANE : (g + 1) * LANE], logits[:, (chunks + g) * LANE : (chunks + g + 1) * LANE]
        keep_ref[g] = jnp.where(core, high, low)
        give_ref[g] = jnp.where(core, low, high)


def slope_kernel(pre_ref, stats_ref, slope_ref):
    pre_act = pre_ref[...]
    cum_prob = 0.5 * (1.0 + lax.erf(pre_act * 0.7071067811865476))
    density = jnp.exp(-0.5 * pre_act * pre_act) * 0.3989422804014327
    slope_ref[...] = (cum_prob + pre_act * density) * stats_ref[1:2, :]


def pick(marks_ref, y, z, chunks):
    size = chunks[0].shape
    bit_y = jnp.broadcast_to(marks_ref[1:2, :], size) != y
    bit_z = jnp.broadcast_to(marks_ref[2:3, :], size) != z
    return jnp.where(bit_y, jnp.where(bit_z, chunks[3], chunks[2]), jnp.where(bit_z, chunks[1], chunks[0]))


def fold_kernel(marks_ref, keep_ref, got_ref, *outs):
    chunks = [keep_ref[g] + got_ref[g] for g in range(4)]
    for out, (y, z) in zip(outs, ((0, 0), (1, 0), (0, 1), (1, 1))):
        out[...] = pick(marks_ref, y, z, chunks)


def add_kernel(*refs):
    refs[-1][...] = sum(ref[...] for ref in refs[:-1])


def softmax_kernel(classes, marks_ref, kept_ref, got_ref, labels_ref, grad_ref):
    kept = kept_ref[...] + got_ref[...]
    chunk = 4 * marks_ref[0:1, :] + 2 * marks_ref[1:2, :] + marks_ref[2:3, :]
    labels = labels_ref[:, :LANE]
    for g in range(1, labels_ref.shape[1] // LANE):
        labels = jnp.where(chunk == g, labels_ref[:, g * LANE : (g + 1) * LANE], labels)
    class_id = lax.broadcasted_iota(jnp.int32, kept.shape, 0)
    kept = jnp.where(class_id < classes, kept, -jnp.inf)
    col_max = jnp.max(kept, axis=0, keepdims=True)
    exp_terms = jnp.exp(kept - col_max)
    exp_total = jnp.sum(exp_terms, axis=0, keepdims=True)
    onehot = class_id == labels
    picked = jnp.sum(jnp.where(onehot, kept, 0.0), axis=0, keepdims=True)
    loss = jnp.log(exp_total) + col_max - picked
    loss_high = loss.astype(BF).astype(F32)
    grad = exp_terms / exp_total - onehot.astype(F32)
    grad = jnp.where(class_id == classes, loss_high, jnp.where(class_id == classes + 1, loss - loss_high, grad))
    grad_ref[...] = grad.astype(BF)


def join_kernel(marks_ref, own_ref, y_ref, z_ref, both_ref, out_ref):
    chunks = [ref[...].astype(F32) for ref in (own_ref, z_ref, y_ref, both_ref)]
    for g in range(4):
        out_ref[g] = pick(marks_ref, g // 2, g % 2, chunks).astype(BF)


def grad_kernel(marks_ref, own_ref, sib_ref, mix_ref, slope_ref, grad_ref, scaled_ref):
    chunks = own_ref.shape[0]
    core = jnp.broadcast_to(marks_ref[0:1, :], own_ref.shape[1:]) == 1
    for g in range(chunks):
        own, sib = own_ref[g].astype(F32), sib_ref[g].astype(F32)
        grad_ref[:, g * LANE : (g + 1) * LANE] = jnp.where(core, sib, own).astype(BF)
        grad_ref[:, (chunks + g) * LANE : (chunks + g + 1) * LANE] = jnp.where(core, own, sib).astype(BF)
    scaled_ref[...] = (dot(mix_ref[...], grad_ref[...], ((1,), (0,))) * slope_ref[...]).astype(BF)


def branch_kernel(hidden_ref, grad_ref, w_out_ref, scaled_ref, pre_ref, gain_sum_ref, mixed_ref, give_ref, means_ref):
    mixed = dot(hidden_ref[...], grad_ref[...], ((1,), (1,))).astype(BF)
    mixed_ref[...] = mixed
    width = give_ref.shape[1]
    wide = scaled_ref[...].astype(F32)
    mean_part = jnp.sum(wide * gain_sum_ref[...], axis=0, keepdims=True)
    proj_part = jnp.sum(wide * pre_ref[...], axis=0, keepdims=True)
    means = jnp.concatenate([mean_part, proj_part, jnp.zeros((SUB_ROWS - 2, wide.shape[1]), F32)], axis=0)
    means_ref[...] = means
    give_ref[...] = jnp.concatenate([dot(mixed, w_out_ref[:, width:], ((0,), (0,))), means], axis=0).astype(BF)


def own_branch_kernel(mixed_ref, w_out_ref, means_ref, keep_ref):
    width = keep_ref.shape[1]
    keep_ref[...] = jnp.concatenate([dot(mixed_ref[...], w_out_ref[:, :width], ((0,), (0,))), means_ref[...]], axis=0)


def message_of(d, turned_ref, own_ref, got_ref, keep_ref, sib_ref):
    units = own_ref.shape[0]
    at = slice(d * LANE, (d + 1) * LANE)
    rows = dot(turned_ref[at, :units], own_ref[...], ((1,), (0,))) + dot(turned_ref[at, units:], got_ref[...], ((1,), (0,)))
    means = keep_ref[CLASS_ROWS:, :] + sib_ref[CLASS_ROWS:, :].astype(F32)
    means = [means[n : n + 1, g * LANE : (g + 1) * LANE] for n in range(2) for g in range(8)]
    means = jnp.concatenate(means + [jnp.zeros((EXTRA - 16, LANE), F32)], axis=0)
    branch = keep_ref[:CLASS_ROWS, at] + sib_ref[:CLASS_ROWS, at].astype(F32)
    branch = jnp.concatenate([branch, jnp.zeros((7 * EXTRA - CLASS_ROWS, LANE), F32)], axis=0)
    extra = jnp.concatenate([means] + [branch[g * EXTRA : (g + 1) * EXTRA] for g in range(7)], axis=1)
    return jnp.concatenate([rows, extra], axis=0)


def message_kernel(ids, *refs):
    for d, out in zip(ids, refs[-len(ids) :]):
        out[...] = message_of(d, *refs[: -len(ids)])


def far_kernel(*refs):
    upper, lower = refs[-2:]
    cut = upper.shape[0]
    total = message_of(CHIPS // 2, *refs[:-2])
    upper[...] = total[:cut].astype(BF)
    lower[...] = total[cut:].astype(BF)


def sum_kernel(begin, own_ref, got_ref, *outs):
    own, got = own_ref[...], got_ref[...].astype(F32)
    end = begin + got.shape[0]
    pieces = [own[:begin]] * (begin > 0) + [own[begin:end] + got] + [own[end:]] * (end < own.shape[0])
    total = jnp.concatenate(pieces, axis=0) if len(pieces) > 1 else pieces[0]
    for n, out in enumerate(outs):
        width = out.shape[1]
        out[...] = total[:, n * width : (n + 1) * width].astype(BF)


def d_w_out_kernel(mixed_ref, head_ref, scale_ref, out_ref, done_ref, held, sems):
    done_ref[...] = jnp.zeros_like(done_ref)
    mixed = mixed_ref[...]
    copies = []
    for n in range(sems.shape[0]):
        at = slice(n * held.shape[1] // sems.shape[0], (n + 1) * held.shape[1] // sems.shape[0])
        held[:, at] = dot(mixed, head_ref[:, at], ((1,), (0,))) * scale_ref[:, at]
        copies.append(pltpu.make_async_copy(held.at[:, at], out_ref.at[:, at], sems.at[n]))
        copies[-1].start()
    for copy in copies:
        copy.wait()


def d_w_in_kernel(places_ref, gain_ref, scaled_ref, stats_ref, own_ref, sib_ref, out_ref, done_ref, held, sems):
    done_ref[...] = jnp.zeros_like(done_ref)
    scaled = scaled_ref[...]
    shift = jnp.sum(scaled.astype(F32) * stats_ref[0:1, :], axis=1, keepdims=True)
    copies = []
    for side, blocks in enumerate((own_ref, sib_ref)):
        for n in range(0, CHIPS, 2):
            both = dot(scaled, blocks[n * LANE : (n + 2) * LANE, :], ((1,), (1,))) - shift
            for k in range(2):
                at = columns(places_ref, 2 * (n + k) + side)
                slot = len(copies)
                held[slot] = both[:, k * LANE : (k + 1) * LANE] * gain_ref[:, at]
                copies.append(pltpu.make_async_copy(held.at[slot], out_ref.at[:, at], sems.at[slot]))
                copies[-1].start()
    for copy in copies:
        copy.wait()


def head_kernel(classes, x_ref, head_ref, grad_ref, out_grad_ref, d_head_ref, loss_ref):
    grad = grad_ref[...]
    out_grad_ref[...] = dot(head_ref[...], grad, ((0,), (0,)))
    d_head_ref[...] = dot(grad, x_ref[...], ((1,), (1,)))
    loss_ref[...] = (jnp.sum(grad[classes : classes + 2].astype(F32)) / grad.shape[1]).reshape(1, 1)


def put_conv_grad(groups, got, means_rows, conv_ref, stats_ref, grid_pad):
    rows = conv_ref.shape[0]
    channels = rows * 2 * CHIPS
    for n, g in enumerate(groups):
        at = slice(g * LANE, (g + 1) * LANE)
        normed = (conv_ref[:, at].astype(F32) - stats_ref[0:1, at]) * stats_ref[1:2, at]
        conv_grad = got[:rows, n * LANE : (n + 1) * LANE] - (means_rows[g : g + 1, :] + normed * means_rows[8 + g : 9 + g, :]) * (1.0 / channels)
        put_rows(grid_pad, 4 * g, conv_grad)


def add_taps(groups, copies, copies_x, sums):
    for g in groups:
        conv_grad = copies[HALF, pl.ds(4 * g + HALF, 4)]
        for j in range(KS):
            for i in range(KS):
                prod = (conv_grad * copies_x[j, pl.ds(4 * g + i, 4)]).reshape(16, 8, LANE)
                index = i * KS + j
                total = jnp.sum(prod, axis=0)
                if g == 0:
                    sums[index] = total
                else:
                    sums[index] += total


def copy_rows(begin, end, grid_pad, copies):
    rows = pl.ds(begin, end - begin)
    for j in range(KS):
        copies[j, rows] = grid_pad[rows, pl.ds(8 + j - HALF, WIN_W), :]


def upper_kernel(mine_ref, forth_ref, back_ref, conv_ref, stats_ref, taps, copies_x, out_grad_ref,
                 d_x_ref, sums, grid_pad, extra_ref, copies):
    rows = conv_ref.shape[0]
    width = forth_ref.shape[1]
    got = mine_ref[:, :width] + forth_ref[...].astype(F32) + back_ref[...].astype(F32)
    extra_ref[...] = got[rows:]
    clear_border(grid_pad)
    put_conv_grad(range(4), got, got[rows:, :LANE], conv_ref, stats_ref, grid_pad)
    copy_rows(0, 16 + HALF, grid_pad, copies)
    for g in range(3):
        at = slice(g * LANE, (g + 1) * LANE)
        d_x_ref[:, at] = out_grad_ref[:, at] + conv_rows(copies, taps, 4 * g, True).reshape(LANE, LANE).T
    add_taps(range(4), copies, copies_x, sums)


def lower_kernel(classes, mine_ref, forth_ref, back_ref, conv_ref, stats_ref, taps, copies_x, out_grad_ref, head_grad_ref, head_ref, scale_ref,
                 d_upper_ref, sums_ref, grid_ref, extra_ref, d_x_ref, d_dw_ref, d_scale_ref, d_head_ref, grid_pad, copies, sums):
    rows = conv_ref.shape[0]
    width = forth_ref.shape[1]
    got = mine_ref[:, width:] + forth_ref[...].astype(F32) + back_ref[...].astype(F32)
    extra = jnp.concatenate([extra_ref[...], got[rows:]], axis=1)
    branch = jnp.concatenate([extra[:, g * LANE : (g + 1) * LANE] for g in range(1, 8)], axis=0)[:CLASS_ROWS]
    sums[...] = sums_ref[...]
    grid_pad[...] = grid_ref[...]
    put_conv_grad(range(4, 8), got, extra[:, :LANE], conv_ref, stats_ref, grid_pad)
    copy_rows(12, WIN_H + 2 * HALF, grid_pad, copies)
    d_x_ref[:, : 3 * LANE] = d_upper_ref[...]
    for g in range(3, 8):
        at = slice(g * LANE, (g + 1) * LANE)
        d_x_ref[:, at] = out_grad_ref[:, at] + conv_rows(copies, taps, 4 * g, True).reshape(LANE, LANE).T
    add_taps(range(4, 8), copies, copies_x, sums)
    d_dw_ref[...] = jnp.sum(sums[...], axis=1)
    d_scale_ref[...] = jnp.sum(head_ref[...].astype(F32) * branch, axis=0, keepdims=True)
    d_head_ref[...] = (head_grad_ref[...] + scale_ref[...] * branch)[:classes]


def walk_step(walk, step):
    forth, back = walk[(1 - step) % CHIPS][0], walk[step - 1][0]
    half = forth.shape[0] // 2
    if step < CHIPS // 2:
        walk[(-step) % CHIPS], walk[step] = (send(forth, FORTH),), (send(back, BACK),)
    else:
        walk[step] = (send(forth[:half], FORTH), send(back[half:], BACK))


def hold(walk, step, *others):
    spots = [(-step) % CHIPS, step]
    held = lax.optimization_barrier((walk[spots[0]][0], walk[spots[1]][0], *others))
    walk[spots[0]], walk[spots[1]] = (held[0],), (held[1],)
    return held[2:]


def per_device(features, dw_weight, norm_gain, layer_scale, w_in, w_out, w_head, labels):
    rows, tokens = features.shape
    units, channels = w_in.shape
    classes = w_head.shape[1]
    me = lax.axis_index("ch")
    places = lax.dynamic_index_in_dim(jnp.asarray(PLACES), me, 0, keepdims=False)
    marks = lax.dynamic_index_in_dim(jnp.asarray(MARKS), me, 0, keepdims=False)
    taps = dw_weight.T
    scale_row, gain_row, labels_row = layer_scale[None, :], norm_gain[None, :], labels[None, :]
    grid_shape = pltpu.VMEM((WIN_H + 2 * HALF, WIN_W + 16, LANE), F32)
    copies_size = (KS, WIN_H + 2 * HALF, WIN_W, LANE)
    half_channels = CHIPS * rows
    vm = lambda *arrays: [(a, VMEM) for a in arrays]
    spot, mark = [(places, SMEM)], vm(marks)
    f32s, bf16s, sums_size = ((units, tokens), F32), ((units, tokens), BF), ((8, tokens), F32)

    (conv_out,) = call(
        conv_kernel, [((rows, tokens), BF)], vm(features, taps), [grid_shape, pltpu.VMEM(copies_size, F32)],
        limit=12, name="conv_forward",
    )
    walk = {0: (conv_out,)}
    walk_step(walk, 1)
    w_own, w_give, gain_sum = call(
        weights_kernel,
        [((units, half_channels), BF), ((units, half_channels), BF), ((units, 1), F32)],
        spot + vm(w_in, gain_row), flops=4e8, moved=4e6, limit=12, name="weights_ready", after=[conv_out, marks],
    )
    w_own, w_give, gain_sum = hold(walk, 1, w_own, w_give, gain_sum)
    w_sib = send(w_give, SIBLING)
    walk_step(walk, 2)
    so_far = call(
        functools.partial(first_kernel, (0, 1, 7)), [f32s, f32s, sums_size],
        vm(w_own, w_sib, *walk[0], *walk[1], *walk[7]), flops=1e9, moved=4e6, limit=16, name="forward_first",
    )
    so_far = hold(walk, 2, *so_far)
    walk_step(walk, 3)
    made = call(
        mix_kernel,
        [((CLASS_ROWS, channels), BF), ((units, CLASS_ROWS), BF), ((units, channels), BF), ((CLASS_ROWS, rows), BF), ((1, rows), F32)],
        spot + vm(w_out, scale_row, w_head.T), flops=1e9, moved=4e6, limit=12, name="mix_ready", after=[so_far[2]],
    )
    so_far = call(
        functools.partial(next_kernel, (2, 6)), [f32s, bf16s, sums_size],
        vm(w_own, w_sib, *so_far, *walk[2], *walk[6]), flops=6e8, moved=4e6, limit=16, name="forward_next",
    )
    *so_far, head_pad, mix, w_out_walk, my_head, my_scale = hold(walk, 3, *so_far, *made)
    acc, give, sums = so_far
    got, sib_sums = send(give, SIBLING), send(sums, SIBLING)
    walk_step(walk, 4)
    acc, pair_sums = call(
        functools.partial(pairs_kernel, (3, 5)), [f32s, sums_size],
        vm(w_own, w_give, acc, sums, *walk[3], *walk[5], send(walk[3][0], SIBLING), send(walk[5][0], SIBLING)),
        flops=1e9, moved=4e6, limit=16, name="forward_pairs",
    )
    upper, acc, pair_sums = lax.optimization_barrier((walk[4][0], acc, pair_sums))
    walk[4] = (upper, walk[4][1])
    far = [*walk[4], *[send(b, SIBLING) for b in walk[4]]]
    chunks = tokens // LANE // 2
    chunk = lambda count, kind=F32: ((count, CLASS_ROWS, LANE), kind)
    pre_act, hidden, stats, keep, give = call(
        forward_kernel, [f32s, bf16s, sums_size, chunk(chunks), chunk(chunks)],
        mark + vm(acc, got, sums, sib_sums, pair_sums, gain_sum, mix, my_head, features, w_own, w_give, *far),
        flops=1e9, moved=4e6, limit=16, name="forward_hidden",
    )

    own_chunk = ((CLASS_ROWS, LANE), F32)
    others = (2, 4, 6)
    kept, *gives = call(fold_kernel, [own_chunk] * 4, mark + vm(keep, send(give, SIBLING)), limit=4, name="fold_core")
    (packed,) = call(
        pack_kernel, [((half_channels, tokens), BF)], vm(*[b for d in range(CHIPS) for b in walk[d]]), flops=4e8, moved=4e6, limit=10, name="pack_blocks", after=[kept],
    )
    sib_packed = send(packed, SIBLING)
    (slope,) = call(slope_kernel, [f32s], vm(pre_act, stats), flops=5e8, moved=4e6, limit=8, name="gelu_slope", after=[packed])
    (kept,) = call(
        add_kernel, [own_chunk], vm(kept, *[send(part, flip_perm(bits)) for part, bits in zip(gives, others)]), limit=4, name="fold_chips", after=[slope],
    )
    (turned,) = call(turn_kernel, [((half_channels, 2 * units), BF)], vm(w_own, w_sib), flops=4e8, moved=4e6, limit=10, name="weights_turned", after=[kept])
    (grad,) = call(
        functools.partial(softmax_kernel, classes), [((CLASS_ROWS, LANE), BF)], mark + vm(kept, send(kept, flip_perm(8)), labels_row), limit=4, name="class_grad", after=[turned, sib_packed],
    )
    (copies_x,) = call(copies_kernel, [(copies_size, F32)], vm(features), [grid_shape], flops=4e8, moved=4e6, limit=12, name="window_copies", after=[grad])
    (grad,) = call(
        join_kernel, [((chunks, CLASS_ROWS, LANE), BF)], mark + vm(grad, *[send(grad, flip_perm(bits)) for bits in others]), limit=4, name="join_chips", after=[copies_x],
    )

    grad, scaled = call(
        grad_kernel, [((CLASS_ROWS, tokens), BF), bf16s], mark + vm(grad, send(grad, SIBLING), mix, slope), flops=6e8, moved=4e6, limit=12, name="hidden_grad",
    )
    got = send(scaled, SIBLING)
    extra_rows = CLASS_ROWS + SUB_ROWS
    mixed, give, means = call(
        branch_kernel, [((units, CLASS_ROWS), BF), ((extra_rows, half_channels), BF), ((SUB_ROWS, tokens), F32)],
        vm(hidden, grad, w_out_walk, scaled, pre_act, gain_sum), flops=8e8, moved=4e6, limit=12, name="class_products",
    )
    (keep,) = call(
        own_branch_kernel, [((extra_rows, half_channels), F32)], vm(mixed, w_out_walk, means), flops=4e8, moved=4e6, limit=8, name="class_products_own",
    )
    sources = vm(turned, scaled, got, keep, send(give, SIBLING))
    height = rows + EXTRA
    cut = 80
    forth, back = call(far_kernel, [((cut, tokens), BF), ((height - cut, tokens), BF)], sources, flops=3e8, moved=2e6, limit=8, name="message_far")
    forth, back = send(forth, FORTH), send(back, BACK)
    d_w_out, d_w_out_done = call(
        d_w_out_kernel, [((units, channels), F32), ((8, LANE), F32)], vm(mixed, head_pad, scale_row),
        [pltpu.VMEM((units, channels), F32), pltpu.SemaphoreType.DMA((4,))], flops=1e9, moved=8e6, limit=12, name="d_w_out", out_spaces=(pl.ANY, pltpu.VMEM),
        after=[forth],
    )
    out_grad, head_grad, mean_loss = call(
        functools.partial(head_kernel, classes), [((rows, tokens), F32), ((CLASS_ROWS, rows), F32), ((1, 1), F32)],
        vm(features, my_head, grad), flops=4e8, moved=2e6, limit=8, name="class_head", after=[forth],
    )
    beside = {3: [], 2: [d_w_out_done, out_grad], 1: []}
    for step in range(CHIPS // 2 - 1, 0, -1):
        ahead, behind = call(
            functools.partial(message_kernel, (step, CHIPS - step)), [((height, tokens), F32)] * 2, sources,
            flops=6e8, moved=2e6, limit=8, name="messages",
        )
        first = step == CHIPS // 2 - 1
        parts = 2 if step == 1 else 1
        add = lambda begin, own, got, waits: call(
            functools.partial(sum_kernel, begin), [((height, tokens // parts), BF)] * parts, vm(own, got), limit=6, name="walk_sum", after=waits,
        )
        forth, back = add(0, ahead, forth, []), add(cut if first else 0, behind, back, beside[step])
        if step == 1:
            continue
        (forth,), (back,) = forth, back
        if step == 2:
            d_w_in, d_w_in_done = call(
                d_w_in_kernel, [((units, channels), F32), ((8, LANE), F32)], spot + vm(gain_row, scaled, stats, packed, sib_packed),
                [pltpu.VMEM((2 * CHIPS, units, LANE), F32), pltpu.SemaphoreType.DMA((2 * CHIPS,))],
                flops=2e9, moved=8e6, limit=12, name="d_w_in", out_spaces=(pl.ANY, pltpu.VMEM), after=[forth, back],
            )
            beside[1] = [d_w_in_done]
        forth, back = send(forth, FORTH), send(back, BACK)
    (mine,) = call(functools.partial(message_kernel, (0,)), [((height, tokens), F32)], sources, flops=3e8, moved=2e6, limit=8, name="messages", after=[ahead])
    ends = [(send(forth[n], FORTH), send(back[n], BACK)) for n in range(2)]
    upper = call(
        upper_kernel,
        [((rows, 3 * LANE), F32), ((KS * KS, 8, LANE), F32), (grid_shape.shape, F32), ((EXTRA, tokens // 2), F32)],
        vm(mine, *ends[0], conv_out, stats, taps, copies_x, out_grad), [pltpu.VMEM(copies_size, F32)],
        flops=4e8, moved=2e6, limit=16, name="conv_backward_upper",
    )
    d_features, d_dw, d_scale, d_head = call(
        functools.partial(lower_kernel, classes),
        [((rows, tokens), F32), ((KS * KS, rows), F32), ((1, rows), F32), ((classes, rows), F32)],
        vm(mine, *ends[1], conv_out, stats, taps, copies_x, out_grad, head_grad, my_head, my_scale, *upper),
        [grid_shape, pltpu.VMEM(copies_size, F32), pltpu.VMEM((KS * KS, 8, LANE), F32)], limit=16, name="conv_backward_lower",
    )
    return (d_features, d_dw.T, d_scale[0], d_w_in, d_w_out, d_head.T, mean_loss[0])


def conv_apply(in_grid, kernel):
    half = KS // 2
    padded = jnp.pad(in_grid, ((0, 0), (half, half), (half, half)))
    running = jnp.zeros(in_grid.shape, in_grid.dtype)
    for row_shift in range(KS):
        for col_shift in range(KS):
            tap = kernel[:, row_shift * KS + col_shift]
            running = (
                running
                + tap[:, None, None]
                * padded[:, row_shift : row_shift + WIN_H, col_shift : col_shift + WIN_W]
            )
    return running


def gelu_parts(values):
    cum_prob = 0.5 * (1.0 + lax.erf(values * 0.7071067811865476))
    density = jnp.exp(-0.5 * values * values) * 0.3989422804014327
    return (values * cum_prob, cum_prob + values * density)


def plain_device(features, dw_weight, norm_gain, layer_scale, w_in, w_out, w_head, labels):
    highest = lax.Precision.HIGHEST
    my_rows = features.shape[0]
    tok_count = features.shape[1]
    class_count = w_head.shape[1]
    row_offset = lax.axis_index("ch") * my_rows
    inputs_wide = features.astype(jnp.float32)
    in_grid = inputs_wide.reshape(my_rows, WIN_H, WIN_W)
    conv_out = conv_apply(in_grid, dw_weight).reshape(my_rows, tok_count).astype(jnp.bfloat16)
    conv_all = lax.all_gather(conv_out, "ch", axis=0, tiled=True)
    conv_wide = conv_all.astype(jnp.float32)
    tok_mean = jnp.mean(conv_wide, axis=0)
    centered = conv_wide - tok_mean[None, :]
    tok_var = jnp.mean(centered * centered, axis=0)
    inv_std = 1.0 / jnp.sqrt(tok_var + norm_eps)
    normed = centered * inv_std[None, :]
    norm_out = (norm_gain[:, None] * normed).astype(jnp.bfloat16)
    pre_act = jnp.dot(w_in, norm_out, preferred_element_type=jnp.float32)
    gelu_out, gelu_slope = gelu_parts(pre_act)
    hidden = gelu_out.astype(jnp.bfloat16)
    my_scale = lax.dynamic_slice_in_dim(layer_scale, row_offset, my_rows, 0)
    head_wide = w_head.astype(jnp.float32)
    my_head = lax.dynamic_slice_in_dim(head_wide, row_offset, my_rows, 0)
    w_cols = w_out
    branch_sum = lax.psum_scatter(
        lax.dot_general(
            w_cols, hidden, (((0,), (0,)), ((), ())), preferred_element_type=jnp.float32
        ),
        "ch",
        scatter_dimension=0,
        tiled=True,
    )
    block_out = inputs_wide + my_scale[:, None] * branch_sum
    part_logits = lax.dot_general(block_out, my_head, (((0,), (0,)), ((), ())), precision=highest)
    logits = lax.psum(part_logits, "ch")
    row_max = jnp.max(logits, axis=1, keepdims=True)
    exp_terms = jnp.exp(logits - row_max)
    exp_total = jnp.sum(exp_terms, axis=1, keepdims=True)
    log_total = jnp.log(exp_total) + row_max
    onehot = (labels[:, None] == jnp.arange(class_count, dtype=jnp.int32)[None, :]).astype(
        jnp.float32
    )
    picked = jnp.sum(logits * onehot, axis=1)
    mean_loss = jnp.mean(log_total[:, 0] - picked).reshape(1)
    logit_grad = exp_terms / exp_total - onehot
    out_grad = lax.dot_general(my_head, logit_grad, (((1,), (1,)), ((), ())), precision=highest)
    d_head = jnp.dot(block_out, logit_grad, precision=highest)
    d_scale = jnp.sum(out_grad * branch_sum, axis=1)
    branch_grad = (my_scale[:, None] * out_grad).astype(jnp.bfloat16)
    incoming = lax.all_gather(branch_grad, "ch", axis=0, tiled=True)
    hidden_acc = jnp.dot(w_cols, incoming, preferred_element_type=jnp.float32)
    tile_grad = lax.dot_general(
        hidden, incoming, (((1,), (1,)), ((), ())), preferred_element_type=jnp.float32
    )
    pre_grad = (hidden_acc * gelu_slope).astype(jnp.bfloat16)
    d_w_in = lax.dot_general(
        pre_grad, norm_out, (((1,), (1,)), ((), ())), preferred_element_type=jnp.float32
    )
    norm_grad = lax.dot_general(
        w_in, pre_grad, (((0,), (0,)), ((), ())), preferred_element_type=jnp.float32
    )
    gained = norm_gain[:, None] * norm_grad
    conv_term = (
        gained
        - jnp.mean(gained, axis=0)[None, :]
        - normed * jnp.mean(gained * normed, axis=0)[None, :]
    ) * inv_std[None, :]
    conv_grad = lax.psum_scatter(conv_term, "ch", scatter_dimension=0, tiled=True)
    unused, pullback = jax.vjp(conv_apply, in_grid, dw_weight)
    grid_grad, d_dw = pullback(conv_grad.reshape(my_rows, WIN_H, WIN_W))
    d_features = out_grad + grid_grad.reshape(my_rows, tok_count)
    return (d_features, d_dw, d_scale, d_w_in, tile_grad, d_head, mean_loss)


def solution(mesh):
    placed = (P("ch", "grp"), P("ch", None), P(), P(), P("ch", None), P("ch", None), P(), P("grp"))
    return jax.shard_map(
        per_device if mesh.shape["ch"] == 2 * CHIPS else plain_device,
        mesh=mesh,
        in_specs=placed,
        out_specs=(
            P("ch", "grp"),
            P("ch", "grp"),
            P(("grp", "ch")),
            P(("grp", "ch"), None),
            P(("grp", "ch"), None),
            P("ch", "grp"),
            P("grp"),
        ),
        check_vma=False,
    )
```
